32 devices in a mesh: seq: 8 (over y, x, core), ctx: 4 (over z).
Axes of the slice: x: 2, y: 2, z: 4, core: 2. Of those that a mesh axis runs over, the one named last changes fastest.
Arguments:
- tokens: bfloat16 [32, 1024, 768], P('seq', 'ctx'), may hold values from -6 to 6
- lengths: int32 [32], P('seq'), may hold values from 256 to 1024, as said below
- query_key_value_weight: bfloat16 [768, 2304], replicated, may hold values from -0.21875 to 0.21875
- attention_out_weight: bfloat16 [768, 768], replicated, may hold values from -0.875 to 0.875
- up_weight: bfloat16 [768, 3072], replicated, may hold values from -0.21875 to 0.21875
- down_weight: bfloat16 [3072, 768], replicated, may hold values from -0.109375 to 0.109375
- ln1_gain: float32 [768], replicated, may hold values from 0.1 to 1.9
- ln1_shift: float32 [768], replicated, may hold values from -1.5 to 1.5
- ln2_gain: float32 [768], replicated, may hold values from 0.1 to 1.9
- ln2_shift: float32 [768], replicated, may hold values from -1.5 to 1.5
- cotangent: bfloat16 [32, 1024, 768], P('seq', 'ctx'), may hold values from -6 to 6
Outputs:
- output: bfloat16 [32, 1024, 768], P('seq', 'ctx')
- grad_tokens: bfloat16 [32, 1024, 768], P('seq', 'ctx')
- grad_w_qkv: float32 [768, 2304], P('seq')
- grad_w_out: float32 [768, 768], P('seq')
- grad_w_up: float32 [768, 3072], P('seq')
- grad_w_down: float32 [3072, 768], P('seq')
- grad_ln1_gain: float32 [768], P('seq')
- grad_ln1_shift: float32 [768], P('seq')
- grad_ln2_gain: float32 [768], P('seq')
- grad_ln2_shift: float32 [768], P('seq')
The draws below stay inside these ranges and needn't reach their ends.
Inputs may be any that keep to these rules, and one draw needn't show every extreme that they name: `lengths`: in each aligned group of 4 sequences, one has exactly 1024 live positions.
All inputs are finite; a program needn't handle non-finite values.
Results may differ from the reference program's by a relative error of at most 0.014.
Values may be sent and summed in bfloat16 or wider, within the bound.
A program may use at most 384 MiB of HBM per device.

```python
import jax
import jax.numpy as jnp
from jax import lax

D = 768
H = 24
HD = 32
FF = 3072
SEQS_DEV = 4
LEN = 1024
SEQUENCES = 32


def draw_lengths(key, part):
    key = jax.random.fold_in(key, 7)
    first_key, second_key = jax.random.split(key)
    ragged = jax.random.randint(first_key, (SEQUENCES,), LEN // 4, LEN + 1, dtype=jnp.int32)
    chosen = jax.random.randint(second_key, (SEQUENCES // SEQS_DEV,), 0, SEQS_DEV, dtype=jnp.int32)
    within = jnp.arange(SEQUENCES, dtype=jnp.int32) % SEQS_DEV
    longest = within == jnp.repeat(chosen, SEQS_DEV)
    return jnp.where(longest, LEN, ragged).astype(jnp.int32)


def steps_of(own_key, shape, cuts, least, largest):
    level = 1.0
    for position, parts in cuts:
        steps = jax.random.uniform(jax.random.fold_in(jax.random.fold_in(own_key, 6), position), (parts,), jnp.float32, least / len(cuts), largest / len(cuts))
        level = level * jnp.repeat(jnp.exp(steps), shape[position] // parts).reshape((-1,) + (1,) * (len(shape) - 1 - position))
    return level


def normal_values(key, dims, scale, reach, shards=(), kind=jnp.bfloat16):
    loudness = steps_of(key, dims, shards, -0.22, 0.18) if shards else 1.0
    entries = jax.random.normal(key, dims, jnp.float32) * scale * loudness
    return jnp.minimum(jnp.maximum(entries, -reach), reach).astype(kind)


def setup_inputs(seed: int = 0) -> dict:
    key_list = jax.random.split(jax.random.key(seed), 12)
    return {
        "tokens": normal_values(key_list[0], (SEQUENCES, LEN, D), 1.0, 6.0, ((0, 8), (1, 4))),
        "lengths": draw_lengths(jax.random.fold_in(key_list[11], 71), 0),
        "query_key_value_weight": normal_values(key_list[2], (D, 3 * D), D ** -0.5, 0.21875),
        "attention_out_weight": normal_values(key_list[3], (D, D), (D // 16) ** -0.5, 0.875),
        "up_weight": normal_values(key_list[4], (D, FF), D ** -0.5, 0.21875),
        "down_weight": normal_values(key_list[5], (FF, D), FF ** -0.5, 0.109375),
        "ln1_gain": jnp.clip(1.0 + 0.18 * jax.random.normal(key_list[6], (D,), jnp.float32), 0.1, 1.9),
        "ln1_shift": normal_values(key_list[7], (D,), 0.3, 1.5, (), jnp.float32),
        "ln2_gain": jnp.clip(1.0 + 0.18 * jax.random.normal(key_list[8], (D,), jnp.float32), 0.1, 1.9),
        "ln2_shift": normal_values(key_list[9], (D,), 0.3, 1.5, (), jnp.float32),
        "cotangent": normal_values(key_list[10], (SEQUENCES, LEN, D), 1.0, 6.0, ((0, 8), (1, 4))),
    }


@jax.custom_vjp
def lowered_forward(v):
    return lax.optimization_barrier(v.astype(jnp.bfloat16)).astype(jnp.float32)

@jax.custom_vjp
def lowered_backward(v):
    return v

def low_keep(v):
    return (lowered_forward(v), None)

def low_pass(kept, grad):
    return (grad,)

def back_keep(v):
    return (v, None)

def back_low(kept, grad):
    return (lowered_forward(grad),)
lowered_forward.defvjp(low_keep, low_pass)
lowered_backward.defvjp(back_keep, back_low)
epsilon = 1e-05
highest_precision = lax.Precision.HIGHEST

def layer_norm(rows, gain, shift):
    average = lax.optimization_barrier(jnp.mean(rows, axis=-1, keepdims=True))
    centred = rows - average
    spread = lax.optimization_barrier(jnp.mean(centred * centred, axis=-1, keepdims=True))
    return centred * lax.rsqrt(spread + epsilon) * gain + shift

def attend_one(pieces):
    queries, keys, values, length = pieces
    scale = HD ** (-0.5)
    heads_q = queries.reshape(LEN, H, HD)
    heads_k = keys.reshape(LEN, H, HD)
    heads_v = values.reshape(LEN, H, HD)
    scores = jnp.einsum('qhd,khd->hqk', heads_q, heads_k, precision=highest_precision) * scale
    scores = lowered_backward(scores)
    places = jnp.arange(LEN, dtype=jnp.int32)
    allowed = (places[None, :] <= places[:, None]) & (places[None, :] < length)
    scores = jnp.where(allowed[None], scores, -1e+30)
    summit = lax.optimization_barrier(jnp.max(scores, axis=-1, keepdims=True))
    expo = jnp.exp(scores - summit)
    probs = expo / lax.optimization_barrier(jnp.sum(expo, axis=-1, keepdims=True))
    mixed_heads = jnp.einsum('hqk,khd->qhd', lowered_forward(probs), heads_v, precision=highest_precision)
    return mixed_heads.reshape(LEN, D)

def forward(block_tokens, block_lengths, query_key_value_weight, attention_out_weight, up_weight, down_weight, gain_one, shift_one, gain_two, shift_two):
    normed_input = lowered_forward(layer_norm(block_tokens, gain_one, shift_one))
    packed_rows = lowered_forward(lowered_backward(jnp.einsum('znc,cv->znv', normed_input, query_key_value_weight, precision=highest_precision)))
    queries = packed_rows[..., :D]
    keys = packed_rows[..., D:2 * D]
    values = packed_rows[..., 2 * D:]
    mixed_heads = lax.map(jax.checkpoint(attend_one), (queries, keys, values, block_lengths))
    mixed_heads = lowered_forward(lowered_backward(mixed_heads))
    branch_output = lowered_backward(jnp.einsum('znc,cv->znv', mixed_heads, attention_out_weight, precision=highest_precision))
    middle = block_tokens + branch_output
    normed_middle = lowered_forward(layer_norm(middle, gain_two, shift_two))
    hidden_state = lowered_backward(jnp.einsum('xnv,vm->xnm', normed_middle, up_weight, precision=highest_precision))
    active_tokens = lowered_forward(jax.nn.gelu(hidden_state, approximate=False))
    second_residual = lowered_backward(jnp.einsum('yug,gx->yux', active_tokens, down_weight, precision=highest_precision))
    total = middle + second_residual
    valid = jnp.arange(LEN, dtype=jnp.int32)[None, :] < block_lengths[:, None]
    return jnp.where(valid[..., None], total, 0.0)

def reference(tokens, lengths, query_key_value_weight, attention_out_weight, up_weight, down_weight, ln1_gain, ln1_shift, ln2_gain, ln2_shift, cotangent):
    params = (query_key_value_weight.astype(jnp.float32), attention_out_weight.astype(jnp.float32), up_weight.astype(jnp.float32), down_weight.astype(jnp.float32), ln1_gain, ln1_shift, ln2_gain, ln2_shift)
    groups = SEQUENCES // SEQS_DEV
    inputs = tokens.astype(jnp.float32).reshape(groups, SEQS_DEV, LEN, D)
    upstream = cotangent.astype(jnp.float32).reshape(groups, SEQS_DEV, LEN, D)
    grouped_lengths = lengths.reshape(groups, SEQS_DEV)

    def one_group(totals, pieces):
        block_in, block_lengths, block_cot = pieces

        def apply(block_tokens, *weights):
            return forward(block_tokens, block_lengths, *weights)
        result, pull = jax.vjp(apply, block_in, *params)
        grads = pull(block_cot)
        totals = tuple((total + grad for total, grad in zip(totals, grads[1:])))
        return (totals, (result.astype(jnp.bfloat16), grads[0].astype(jnp.bfloat16)))
    start = tuple((jnp.zeros_like(param) for param in params))
    totals, (results, grad_inputs) = lax.scan(one_group, start, (inputs, grouped_lengths, upstream))
    output = results.reshape(SEQUENCES, LEN, D)
    grad_tokens = grad_inputs.reshape(SEQUENCES, LEN, D)
    return (output, grad_tokens, totals[0], totals[1], totals[2], totals[3], totals[4], totals[5], totals[6], totals[7])
```

```python
import math

import jax
import jax.numpy as jnp
from jax import lax
from jax.experimental import pallas as pl
from jax.experimental.pallas import tpu as pltpu
from jax.sharding import PartitionSpec as P

HD = 32
LANES = 128
HEADS = LANES // HD
BLOCK = 256
SCALE = HD ** (-0.5)
SCALE_LOG2 = SCALE * math.log2(math.e)
BF16 = jnp.bfloat16
F32 = jnp.float32
epsilon = 1e-05
MIB = 2**20


def layer_norm(rows, gain, shift):
    average = jnp.mean(rows, axis=-1, keepdims=True)
    centred = rows - average
    spread = jnp.mean(centred * centred, axis=-1, keepdims=True)
    return centred * lax.rsqrt(spread + epsilon) * gain + shift


def exact_gelu(value):
    return jax.nn.gelu(value, approximate=False)


def dot(a, b, dim_a, dim_b):
    return lax.dot_general(
        a, b, (((dim_a,), (dim_b,)), ((), ())), preferred_element_type=F32
    )


def only_head(rows, head):
    lanes = lax.broadcasted_iota(jnp.int32, rows.shape, 1)
    return jnp.where(lanes // HD == head, rows, 0)


def mask_diagonal(scores, block, first, length):
    keys = first + lax.broadcasted_iota(jnp.int32, (block, block), 0)
    queries = first + lax.broadcasted_iota(jnp.int32, (block, block), 1)
    allowed = (keys <= queries) & (keys < length)
    below = scores.shape[0] - block
    diagonal = jnp.where(allowed, scores[below:], -1e30)
    return jnp.concatenate([scores[:below], diagonal], 0) if below else diagonal


def attention_forward_kernel(length_ref, q_ref, k_ref, v_ref, mixed_ref, log_ref, v_t, mixed_t):
    length = length_ref[0]
    count = q_ref.shape[0] // BLOCK
    v_t[...] = v_ref[...].T

    def scores_of(i, head):
        span = (i + 1) * BLOCK
        query = only_head(q_ref[i * BLOCK : span, :], head)
        return mask_diagonal(dot(k_ref[0:span, :], query, 1, 1), BLOCK, i * BLOCK, length)

    steps = [(i, head) for i in range(count) for head in range(HEADS)]
    scores = scores_of(*steps[0])
    for number, (i, head) in enumerate(steps):
        span = (i + 1) * BLOCK
        following = scores_of(*steps[number + 1]) if number + 1 < len(steps) else None
        summit = jnp.max(scores, axis=0, keepdims=True)
        expo = jnp.exp2(scores * SCALE_LOG2 - summit * SCALE_LOG2)
        denom = jnp.sum(expo, axis=0, keepdims=True)
        part = dot(v_t[head * HD : (head + 1) * HD, 0:span], expo.astype(BF16), 1, 0)
        mixed_t[head * HD : (head + 1) * HD, :] = part / denom
        log_ref[0, head : head + 1, i * BLOCK : span] = summit * SCALE_LOG2 + jnp.log2(denom)
        if head == HEADS - 1:
            mixed_ref[i * BLOCK : span, :] = mixed_t[...].T.astype(BF16)
        scores = following


def attention_backward_kernel(
    length_ref, q_ref, k_ref, v_ref, mixed_ref, grad_ref, log_ref,
    grad_q_ref, grad_k_ref, grad_v_ref, k_t, grad_q_t, probs_low, grads_low, sum_k, sum_v,
):
    length = length_ref[0]
    count = q_ref.shape[0] // BLOCK
    k_t[...] = k_ref[...].T

    def rows_of(i):
        rows = slice(i * BLOCK, (i + 1) * BLOCK)
        product = (grad_ref[rows, :].astype(F32) * mixed_ref[rows, :].astype(F32)).T
        queries = [only_head(q_ref[rows, :], head) for head in range(HEADS)]
        grads = [only_head(grad_ref[rows, :], head) for head in range(HEADS)]
        inner = [
            jnp.sum(product[head * HD : (head + 1) * HD], axis=0, keepdims=True)
            for head in range(HEADS)
        ]
        return (queries, grads, inner)

    prepared = [rows_of(i) for i in range(count)]

    def products_of(i, head):
        span = (i + 1) * BLOCK
        scores = dot(k_ref[0:span, :], prepared[i][0][head], 1, 1)
        return (scores, dot(v_ref[0:span, :], prepared[i][1][head], 1, 1))

    steps = [(i, head) for i in range(count) for head in range(HEADS)]
    current = products_of(*steps[0])
    for number, (i, head) in enumerate(steps):
        below = i * BLOCK
        span = below + BLOCK
        following = products_of(*steps[number + 1]) if number + 1 < len(steps) else None
        scores, grad_probs = current
        scores = mask_diagonal(scores, BLOCK, below, length)
        probs = jnp.exp2(scores * SCALE_LOG2 - log_ref[0, head : head + 1, below:span])
        grad_scores = (probs * (grad_probs - prepared[i][2][head])).astype(BF16)
        columns = slice(head * BLOCK, (head + 1) * BLOCK)
        probs_low[0:span, columns] = probs.astype(BF16)
        grads_low[0:span, columns] = grad_scores
        grad_q_t[head * HD : (head + 1) * HD, :] = dot(
            k_t[head * HD : (head + 1) * HD, 0:span], grad_scores, 1, 0
        )
        if head == HEADS - 1:
            grad_q_ref[below:span, :] = (grad_q_t[...].T * SCALE).astype(BF16)
            grad_v = dot(probs_low[0:span, :], jnp.concatenate(prepared[i][1], 0), 1, 0)
            grad_k = dot(grads_low[0:span, :], jnp.concatenate(prepared[i][0], 0), 1, 0)
            if below:
                sum_v[0:below, :] += grad_v[:below]
                sum_k[0:below, :] += grad_k[:below]
            sum_v[below:span, :] = grad_v[below:]
            sum_k[below:span, :] = grad_k[below:]
        current = following
    grad_k_ref[...] = (sum_k[...] * SCALE).astype(BF16)
    grad_v_ref[...] = sum_v[...].astype(BF16)


def column_blocks(rows, first):
    return pl.BlockSpec((rows, LANES), lambda group, length: (0, first + group))


def attention_forward(length, packed):
    rows, width = packed.shape[0], packed.shape[1] // 3
    groups = width // LANES
    blocks = lambda part: column_blocks(rows, part * groups)
    return pl.pallas_call(
        attention_forward_kernel,
        grid_spec=pltpu.PrefetchScalarGridSpec(
            num_scalar_prefetch=1,
            grid=(groups,),
            in_specs=[blocks(0), blocks(1), blocks(2)],
            out_specs=[
                blocks(0),
                pl.BlockSpec((1, HEADS, rows), lambda group, length: (group, 0, 0)),
            ],
            scratch_shapes=[pltpu.VMEM((LANES, rows), BF16), pltpu.VMEM((LANES, BLOCK), F32)],
        ),
        out_shape=[
            jax.ShapeDtypeStruct((rows, width), BF16),
            jax.ShapeDtypeStruct((groups, HEADS, rows), F32),
        ],
        compiler_params=pltpu.CompilerParams(vmem_limit_bytes=56 * MIB),
        cost_estimate=pl.CostEstimate(flops=16 * 10**9, bytes_accessed=7 * 10**6, transcendentals=0),
        name="attention_forward",
    )(length, packed, packed, packed)


def attention_backward(length, packed, mixed, grad_mixed, logs):
    rows, width = mixed.shape
    groups = width // LANES
    blocks = lambda part: column_blocks(rows, part * groups)
    return pl.pallas_call(
        attention_backward_kernel,
        grid_spec=pltpu.PrefetchScalarGridSpec(
            num_scalar_prefetch=1,
            grid=(groups,),
            in_specs=[
                blocks(0),
                blocks(1),
                blocks(2),
                blocks(0),
                blocks(0),
                pl.BlockSpec((1, HEADS, rows), lambda group, length: (group, 0, 0)),
            ],
            out_specs=[blocks(0)] * 3,
            scratch_shapes=[
                pltpu.VMEM((LANES, rows), BF16),
                pltpu.VMEM((LANES, BLOCK), F32),
                pltpu.VMEM((rows, HEADS * BLOCK), BF16),
                pltpu.VMEM((rows, HEADS * BLOCK), BF16),
                pltpu.VMEM((rows, LANES), F32),
                pltpu.VMEM((rows, LANES), F32),
            ],
        ),
        out_shape=[jax.ShapeDtypeStruct((rows, width), BF16)] * 3,
        compiler_params=pltpu.CompilerParams(vmem_limit_bytes=56 * MIB),
        cost_estimate=pl.CostEstimate(flops=40 * 10**9, bytes_accessed=12 * 10**6, transcendentals=0),
        name="attention_backward",
    )(length, packed, packed, packed, mixed, grad_mixed, logs)


def exchange(value, axis, size, bit):
    return lax.ppermute(value, axis, [(i, i ^ (1 << bit)) for i in range(size)])


def halve(value, axis, size, bit, dim):
    mine = (lax.axis_index(axis) >> bit) & 1
    kept = lax.dynamic_index_in_dim(value, mine, dim, keepdims=False)
    sent = lax.dynamic_index_in_dim(value, 1 - mine, dim, keepdims=False)
    got = exchange(sent, axis, size, bit)
    return (kept.astype(F32) + got.astype(F32)).astype(BF16)


def scatter_over_seq(value, size, order):
    bits = list(range(size.bit_length() - 1))
    value = value.reshape((2,) * len(bits) + value.shape[1:])
    left = bits[::-1]
    for bit in order:
        value = halve(value, "seq", size, bit, left.index(bit))
        left.remove(bit)
    return value


def sum_over_ctx(value, size):
    bits = list(range(size.bit_length() - 1))
    rows, columns = value.shape
    value = value.reshape((2,) * len(bits) + (rows // size, columns))
    left = bits[::-1]
    for bit in bits:
        value = halve(value, "ctx", size, bit, left.index(bit))
        left.remove(bit)
    for bit in bits[::-1]:
        got = exchange(value, "ctx", size, bit)
        low = ((lax.axis_index("ctx") >> bit) & 1) == 0
        value = jnp.stack([jnp.where(low, value, got), jnp.where(low, got, value)])
    value = value.transpose(tuple(bits[::-1]) + (len(bits), len(bits) + 1))
    return value.reshape(rows, columns)


def sum_weight(grad, seq_size, ctx_size):
    rows, columns = grad.shape
    blocks = grad.astype(BF16).reshape(seq_size, rows // seq_size, columns)
    order = list(range(seq_size.bit_length() - 1))
    other = order[:1] + order[1:][::-1]
    half = columns // 2
    first = scatter_over_seq(blocks[:, :, :half], seq_size, order)
    second = scatter_over_seq(blocks[:, :, half:], seq_size, other)
    summed = jnp.concatenate([first, second], axis=-1)
    return sum_over_ctx(summed, ctx_size).astype(F32)


def make_per_device(seq_size, ctx_size):
    def to_sequence(value):
        moved = lax.all_to_all(value, "ctx", 0, 0, tiled=True)
        return moved.reshape(-1, value.shape[-1])

    def to_blocks(value, shape):
        return lax.all_to_all(value.reshape(shape), "ctx", 0, 0, tiled=True)

    def per_device(
        tokens,
        lengths,
        query_key_value_weight,
        attention_out_weight,
        up_weight,
        down_weight,
        ln1_gain,
        ln1_shift,
        ln2_gain,
        ln2_shift,
        cotangent,
    ):
        shape = tokens.shape
        length = lax.dynamic_slice_in_dim(lengths, lax.axis_index("ctx"), 1)
        inputs = to_sequence(tokens).astype(F32)
        rows, width = inputs.shape
        valid = (jnp.arange(rows, dtype=jnp.int32) < length[0])[:, None]
        normed_input, ln1_pull = jax.vjp(layer_norm, inputs, ln1_gain, ln1_shift)
        normed_low = normed_input.astype(BF16)
        packed = jnp.dot(
            normed_low, query_key_value_weight, preferred_element_type=F32
        ).astype(BF16)
        mixed_low, logs = attention_forward(length, packed)
        middle = inputs + jnp.dot(mixed_low, attention_out_weight, preferred_element_type=F32)
        normed_middle, ln2_pull = jax.vjp(layer_norm, middle, ln2_gain, ln2_shift)
        normed_two_low = normed_middle.astype(BF16)
        hidden_state = jnp.dot(normed_two_low, up_weight, preferred_element_type=F32)
        active_tokens, gelu_pull = jax.vjp(exact_gelu, hidden_state)
        active_low = active_tokens.astype(BF16)
        total = middle + jnp.dot(active_low, down_weight, preferred_element_type=F32)
        output = to_blocks(jnp.where(valid, total, 0.0).astype(BF16), shape)
        upstream = jnp.where(valid, to_sequence(cotangent).astype(F32), 0.0)
        upstream_low = upstream.astype(BF16)
        grad_down = dot(active_low, upstream_low, 0, 0)
        grad_active = dot(upstream_low, down_weight, 1, 1)
        grad_hidden = gelu_pull(grad_active)[0].astype(BF16)
        grad_up = dot(normed_two_low, grad_hidden, 0, 0)
        grad_normed_two = dot(grad_hidden, up_weight, 1, 1)
        grad_middle_norm, grad_gain_two, grad_shift_two = ln2_pull(grad_normed_two)
        grad_middle = upstream + grad_middle_norm
        grad_branch = grad_middle.astype(BF16)
        grad_out = dot(mixed_low, grad_branch, 0, 0)
        grad_mixed = dot(grad_branch, attention_out_weight, 1, 1).astype(BF16)
        grad_packed = jnp.concatenate(
            attention_backward(length, packed, mixed_low, grad_mixed, logs), axis=-1
        )
        grad_qkv = dot(normed_low, grad_packed, 0, 0)
        grad_normed = dot(grad_packed, query_key_value_weight, 1, 1)
        grad_input_norm, grad_gain_one, grad_shift_one = ln1_pull(grad_normed)
        grad_tokens = to_blocks((grad_middle + grad_input_norm).astype(BF16), shape)
        vectors = jnp.stack([grad_gain_one, grad_shift_one, grad_gain_two, grad_shift_two])
        vectors = lax.psum(vectors, ("seq", "ctx"))
        share = width // seq_size
        vectors = lax.dynamic_slice_in_dim(vectors, lax.axis_index("seq") * share, share, 1)
        return (
            output,
            grad_tokens,
            sum_weight(grad_qkv, seq_size, ctx_size),
            sum_weight(grad_out, seq_size, ctx_size),
            sum_weight(grad_up, seq_size, ctx_size),
            sum_weight(grad_down, seq_size, ctx_size),
            vectors[0],
            vectors[1],
            vectors[2],
            vectors[3],
        )

    return per_device


def solution(mesh):
    placed = (P("seq", "ctx", None), P("seq")) + (P(),) * 8 + (P("seq", "ctx", None),)
    weights = (P("seq", None),) * 4 + (P("seq"),) * 4
    return jax.shard_map(
        make_per_device(mesh.shape["seq"], mesh.shape["ctx"]),
        mesh=mesh,
        in_specs=placed,
        out_specs=(P("seq", "ctx", None),) * 2 + weights,
        check_vma=False,
    )
```

```python
import functools
import math

import jax
import jax.numpy as jnp
from jax import lax
from jax.experimental import pallas as pl
from jax.experimental.pallas import tpu as pltpu
from jax.sharding import PartitionSpec as P

HD = 32
LANES = 128
HEADS = LANES // HD
BLOCK = 256
SCALE = HD ** (-0.5)
SCALE_LOG2 = SCALE * math.log2(math.e)
BF16 = jnp.bfloat16
F32 = jnp.float32
MESH = pl.DeviceIdType.MESH
epsilon = 1e-05
MIB = 2**20
ANY = pl.BlockSpec(memory_space=pl.ANY)
SMEM = pl.BlockSpec(memory_space=pltpu.SMEM)
ONE = pl.Buffered(1)


def dot(a, b, dim_a, dim_b):
    return lax.dot_general(
        a, b, (((dim_a,), (dim_b,)), ((), ())), preferred_element_type=F32
    )


def whole(shape):
    return pl.BlockSpec(shape, lambda step: (0,) * len(shape), pipeline_mode=ONE)


def struct(shape, kind=BF16):
    return jax.ShapeDtypeStruct(shape, kind)


def greet(partners):
    barrier = pltpu.get_barrier_semaphore()
    for partner in partners:
        pl.semaphore_signal(barrier, inc=1, device_id=partner, device_id_type=MESH)
    pl.semaphore_wait(barrier, len(partners))


def to_partner(source, target, send_sem, recv_sem, partner):
    return pltpu.make_async_remote_copy(
        src_ref=source,
        dst_ref=target,
        send_sem=send_sem,
        recv_sem=recv_sem,
        device_id=partner,
        device_id_type=MESH,
    )


def normalise(rows):
    centred = rows - jnp.mean(rows, axis=-1, keepdims=True)
    inverse = lax.rsqrt(jnp.mean(centred * centred, axis=-1, keepdims=True) + epsilon)
    return (centred * inverse, inverse)


def normalise_backward(grad, hat, inverse, gain):
    grad_hat = grad * gain
    along = jnp.mean(grad_hat * hat, axis=-1, keepdims=True)
    return inverse * (grad_hat - jnp.mean(grad_hat, axis=-1, keepdims=True) - hat * along)


def gelu_and_slope(value):
    bell = jnp.exp2(value * value * (-0.5 * math.log2(math.e)))
    t = 1.0 / (1.0 + jnp.abs(value) * (0.3275911 * math.sqrt(0.5)))
    series = (1.061405429 * t - 1.453152027) * t + 1.421413741
    series = ((series * t - 0.284496736) * t + 0.254829592) * t
    tail = (0.5 * series) * bell
    cdf = jnp.where(value >= 0, 1.0 - tail, tail)
    return (value * cdf, cdf + value * (bell * (1.0 / math.sqrt(2.0 * math.pi))))


def only_head(rows, head):
    lanes = lax.broadcasted_iota(jnp.int32, rows.shape, 1)
    return jnp.where(lanes // HD == head, rows, 0)


def mask_diagonal(scores, block, first, length):
    keys = first + lax.broadcasted_iota(jnp.int32, (block, block), 0)
    queries = first + lax.broadcasted_iota(jnp.int32, (block, block), 1)
    allowed = (keys <= queries) & (keys < length)
    below = scores.shape[0] - block
    diagonal = jnp.where(allowed, scores[below:], -1e30)
    return jnp.concatenate([scores[:below], diagonal], 0) if below else diagonal


def attend(group, length, packed, mixed_ref, log_ref, v_t, mixed_t):
    rows, width = packed.shape[0], packed.shape[1] // 3
    count = rows // BLOCK
    columns = [
        pl.ds(pl.multiple_of(part * width + group * LANES, LANES), LANES) for part in range(3)
    ]
    v_t[...] = packed[:, columns[2]].T

    def scores_of(i, head):
        span = (i + 1) * BLOCK
        query = only_head(packed[i * BLOCK : span, columns[0]], head)
        scores = dot(packed[0:span, columns[1]], query, 1, 1)
        return mask_diagonal(scores, BLOCK, i * BLOCK, length)

    steps = [(i, head) for i in range(count) for head in range(HEADS)]
    scores = scores_of(*steps[0])
    for number, (i, head) in enumerate(steps):
        span = (i + 1) * BLOCK
        following = scores_of(*steps[number + 1]) if number + 1 < len(steps) else None
        summit = jnp.max(scores, axis=0, keepdims=True)
        expo = jnp.exp2(scores * SCALE_LOG2 - summit * SCALE_LOG2)
        denom = jnp.sum(expo, axis=0, keepdims=True)
        part = dot(v_t[head * HD : (head + 1) * HD, 0:span], expo.astype(BF16), 1, 0)
        mixed_t[head * HD : (head + 1) * HD, :] = part / denom
        log_ref[0, head : head + 1, i * BLOCK : span] = summit * SCALE_LOG2 + jnp.log2(denom)
        if head == HEADS - 1:
            mixed_ref[i * BLOCK : span, :] = mixed_t[...].T.astype(BF16)
        scores = following


def front_kernel(
    ctx, length_ref, tokens, cotangent, weight, gain, shift,
    inputs_out, normed_out, packed_out, cotangent_out, mixed_ref, log_ref,
    inputs, normed, packed, v_t, mixed_t, send, recv, cot_send, cot_recv, local,
):
    step = pl.program_id(0)
    me = lax.axis_index("ctx")
    block = tokens.shape[1]
    offsets = [1] + list(range(2, ctx))

    def token_copy(offset):
        return to_partner(
            tokens.at[me ^ offset], inputs.at[me], send.at[offset], recv.at[offset],
            {"ctx": me ^ offset},
        )

    def cotangent_copy(offset):
        return to_partner(
            cotangent.at[me ^ offset], cotangent_out.at[me], cot_send.at[offset],
            cot_recv.at[offset], {"ctx": me ^ offset},
        )

    own_cotangent = pltpu.make_async_copy(cotangent.at[me], cotangent_out.at[me], local.at[1])
    keeps = [
        pltpu.make_async_copy(inputs, inputs_out, local.at[2]),
        pltpu.make_async_copy(normed, normed_out, local.at[3]),
        pltpu.make_async_copy(packed, packed_out, local.at[4]),
    ]

    @pl.when(step == 0)
    def _():
        own = pltpu.make_async_copy(tokens.at[me], inputs.at[me], local.at[0])
        own.start()
        greet([{"ctx": me ^ offset} for offset in offsets])
        for offset in offsets[::-1]:
            token_copy(offset).start()

        def project(source):
            hat, _ = normalise(inputs[source].astype(F32))
            low = (hat * gain[...] + shift[...]).astype(BF16)
            rows = pl.ds(pl.multiple_of(source * block, block), block)
            normed[rows, :] = low
            packed[rows, :] = dot(low, weight[...], 1, 0).astype(BF16)

        own.wait()
        project(me)
        for offset in offsets:
            token_copy(offset).wait_recv()
            if offset == offsets[-1]:
                for earlier in offsets:
                    token_copy(earlier).wait_send()
                own_cotangent.start()
                for later in offsets[::-1]:
                    cotangent_copy(later).start()
            project(me ^ offset)
        for keep in keeps:
            keep.start()

    @pl.when(step > 0)
    def _():
        attend(step - 1, length_ref[0], packed, mixed_ref, log_ref, v_t, mixed_t)

    @pl.when(step == pl.num_programs(0) - 1)
    def _():
        for keep in keeps:
            keep.wait()
        own_cotangent.wait()
        for offset in offsets:
            cotangent_copy(offset).wait()


def front(ctx, length, tokens, cotangent, weight, gain, shift):
    blocks, block, width = tokens.shape
    rows, groups = blocks * block, width // LANES
    group_of = lambda step: jnp.maximum(step - 1, 0)
    return pl.pallas_call(
        functools.partial(front_kernel, ctx),
        grid=(1 + groups,),
        in_specs=[SMEM, ANY, ANY, whole(weight.shape), whole(gain.shape), whole(shift.shape)],
        out_specs=[
            ANY, ANY, ANY, ANY,
            pl.BlockSpec((rows, LANES), lambda step: (0, group_of(step))),
            pl.BlockSpec((1, HEADS, rows), lambda step: (group_of(step), 0, 0)),
        ],
        out_shape=[
            struct(tokens.shape),
            struct((rows, width)),
            struct((rows, 3 * width)),
            struct(tokens.shape),
            struct((rows, width)),
            struct((groups, HEADS, rows), F32),
        ],
        scratch_shapes=[
            pltpu.VMEM(tokens.shape, BF16),
            pltpu.VMEM((rows, width), BF16),
            pltpu.VMEM((rows, 3 * width), BF16),
            pltpu.VMEM((LANES, rows), BF16),
            pltpu.VMEM((LANES, BLOCK), F32),
            pltpu.SemaphoreType.DMA((ctx,)),
            pltpu.SemaphoreType.DMA((ctx,)),
            pltpu.SemaphoreType.DMA((ctx,)),
            pltpu.SemaphoreType.DMA((ctx,)),
            pltpu.SemaphoreType.DMA((5,)),
        ],
        compiler_params=pltpu.CompilerParams(
            vmem_limit_bytes=56 * MIB, collective_id=0, has_side_effects=True
        ),
        name="front",
    )(length, tokens, cotangent, weight, gain, shift)


def feed_forward_kernel(
    blocks, length_ref, inputs, mixed, cotangent, out_weight, up_weight, down_weight, gain, shift,
    output, grad_middle_ref, grad_mixed_ref, grad_down_ref, grad_up_ref, grad_out_ref, grad_norm_ref,
    normed, upstream, branch, active, hidden, staged, send, recv, local,
):
    step = pl.program_id(0)
    me = lax.axis_index("ctx")
    block = staged.shape[1]
    width = normed.shape[1]
    wide = active.shape[1]
    cuts = wide // width

    def output_copy(row):
        return to_partner(
            staged.at[row], output.at[me], send.at[row], recv.at[me], {"ctx": row}
        )

    own_output = pltpu.make_async_copy(staged.at[me], output.at[me], local)

    @pl.when(step == 0)
    def _():
        greet([{"ctx": me ^ offset} for offset in range(1, blocks)])
        grad_norm_ref[...] = jnp.zeros_like(grad_norm_ref)

    @pl.when(step < blocks)
    def _():
        rows = pl.ds(pl.multiple_of(step * block, block), block)
        middle = inputs[step].astype(F32) + dot(mixed[rows, :], out_weight[...], 1, 0)
        hat, inverse = normalise(middle)
        low = (hat * gain[...] + shift[...]).astype(BF16)
        normed[rows, :] = low
        places = step * block + lax.broadcasted_iota(jnp.int32, (block, 1), 0)
        valid = places < length_ref[0]
        upstream_full = jnp.where(valid, cotangent[step].astype(F32), 0.0)
        upstream_low = upstream_full.astype(BF16)
        upstream[rows, :] = upstream_low

        def products_of(cut):
            part = slice(cut * width, (cut + 1) * width)
            return (
                dot(low, up_weight[:, part], 1, 0),
                dot(upstream_low, down_weight[part, :], 1, 1),
            )

        current = products_of(0)
        total, grad_normed = middle, 0.0
        for cut in range(cuts):
            part = slice(cut * width, (cut + 1) * width)
            following = products_of(cut + 1) if cut + 1 < cuts else None
            value, slope = gelu_and_slope(current[0])
            value = value.astype(BF16)
            grad_hidden = (slope * current[1]).astype(BF16)
            active[rows, part] = value
            hidden[rows, part] = grad_hidden
            total = total + dot(value, down_weight[part, :], 1, 0)
            grad_normed = grad_normed + dot(grad_hidden, up_weight[:, part], 1, 1)
            current = following
        staged[step] = jnp.where(valid, total, 0.0).astype(BF16)

        @pl.when(step != me)
        def _():
            output_copy(step).start()

        @pl.when(step == me)
        def _():
            own_output.start()

        grad_norm_ref[0:1, :] += jnp.sum(grad_normed * hat, axis=0, keepdims=True)
        grad_norm_ref[1:2, :] += jnp.sum(grad_normed, axis=0, keepdims=True)
        grad_middle = upstream_full + normalise_backward(grad_normed, hat, inverse, gain[...])
        grad_middle_ref[...] = grad_middle
        grad_branch = grad_middle.astype(BF16)
        branch[rows, :] = grad_branch
        grad_mixed_ref[...] = dot(grad_branch, out_weight[...], 1, 1).astype(BF16)

    @pl.when(step == blocks)
    def _():
        grad_out_ref[...] = dot(mixed[...], branch[...], 0, 0).astype(BF16)

    @pl.when(step >= blocks)
    def _():
        size = grad_down_ref.shape[0]
        part = pl.ds(pl.multiple_of((step - blocks) * size, size), size)
        grad_down_ref[...] = dot(active[:, part], upstream[...], 0, 0).astype(BF16)
        grad_up_ref[...] = dot(normed[...], hidden[:, part], 0, 0).astype(BF16)

    @pl.when(step == pl.num_programs(0) - 1)
    def _():
        own_output.wait()
        for row in range(blocks):

            @pl.when(row != me)
            def _():
                copy = output_copy(row)
                copy.wait_send()
                to_partner(
                    staged.at[row], output.at[row], send.at[row], recv.at[row], {"ctx": row}
                ).wait_recv()


def feed_forward(length, inputs, mixed, cotangent, out_weight, up_weight, down_weight, gain, shift):
    blocks, block, width = inputs.shape
    rows, wide = blocks * block, up_weight.shape[1]
    size = 512
    steps = blocks + wide // size
    early = lambda step: jnp.minimum(step, blocks - 1)
    late = lambda step: jnp.maximum(step - blocks, 0)
    operands = (inputs, mixed, cotangent, out_weight, up_weight, down_weight, gain, shift)
    return pl.pallas_call(
        functools.partial(feed_forward_kernel, blocks),
        grid=(steps,),
        in_specs=[SMEM] + [whole(operand.shape) for operand in operands],
        out_specs=[
            ANY,
            pl.BlockSpec((block, width), lambda step: (early(step), 0)),
            pl.BlockSpec((block, width), lambda step: (early(step), 0)),
            pl.BlockSpec((size, width), lambda step: (late(step), 0)),
            pl.BlockSpec((width, size), lambda step: (0, late(step))),
            whole((width, width)),
            whole((8, width)),
        ],
        out_shape=[
            struct(inputs.shape),
            struct((rows, width), F32),
            struct((rows, width)),
            struct((wide, width)),
            struct((width, wide)),
            struct((width, width)),
            struct((8, width), F32),
        ],
        scratch_shapes=[
            pltpu.VMEM((rows, width), BF16),
            pltpu.VMEM((rows, width), BF16),
            pltpu.VMEM((rows, width), BF16),
            pltpu.VMEM((rows, wide), BF16),
            pltpu.VMEM((rows, wide), BF16),
            pltpu.VMEM(inputs.shape, BF16),
            pltpu.SemaphoreType.DMA((blocks,)),
            pltpu.SemaphoreType.DMA((blocks,)),
            pltpu.SemaphoreType.DMA,
        ],
        compiler_params=pltpu.CompilerParams(
            vmem_limit_bytes=60 * MIB, collective_id=1, has_side_effects=True
        ),
        name="feed_forward",
    )(length, *operands)


def attention_backward_kernel(
    length_ref, q_ref, k_ref, v_ref, mixed_ref, grad_ref, log_ref,
    grad_q_ref, grad_k_ref, grad_v_ref, k_t, grad_q_t, probs_low, grads_low, sum_k, sum_v,
):
    length = length_ref[0]
    count = q_ref.shape[0] // BLOCK
    k_t[...] = k_ref[...].T

    def rows_of(i):
        rows = slice(i * BLOCK, (i + 1) * BLOCK)
        product = (grad_ref[rows, :].astype(F32) * mixed_ref[rows, :].astype(F32)).T
        queries = [only_head(q_ref[rows, :], head) for head in range(HEADS)]
        grads = [only_head(grad_ref[rows, :], head) for head in range(HEADS)]
        inner = [
            jnp.sum(product[head * HD : (head + 1) * HD], axis=0, keepdims=True)
            for head in range(HEADS)
        ]
        return (queries, grads, inner)

    prepared = [rows_of(i) for i in range(count)]

    def products_of(i, head):
        span = (i + 1) * BLOCK
        scores = dot(k_ref[0:span, :], prepared[i][0][head], 1, 1)
        return (scores, dot(v_ref[0:span, :], prepared[i][1][head], 1, 1))

    steps = [(i, head) for i in range(count) for head in range(HEADS)]
    current = products_of(*steps[0])
    for number, (i, head) in enumerate(steps):
        below = i * BLOCK
        span = below + BLOCK
        following = products_of(*steps[number + 1]) if number + 1 < len(steps) else None
        scores, grad_probs = current
        scores = mask_diagonal(scores, BLOCK, below, length)
        probs = jnp.exp2(scores * SCALE_LOG2 - log_ref[0, head : head + 1, below:span])
        grad_scores = (probs * (grad_probs - prepared[i][2][head])).astype(BF16)
        columns = slice(head * BLOCK, (head + 1) * BLOCK)
        probs_low[0:span, columns] = probs.astype(BF16)
        grads_low[0:span, columns] = grad_scores
        grad_q_t[head * HD : (head + 1) * HD, :] = dot(
            k_t[head * HD : (head + 1) * HD, 0:span], grad_scores, 1, 0
        )
        if head == HEADS - 1:
            grad_q_ref[below:span, :] = (grad_q_t[...].T * SCALE).astype(BF16)
            grad_v = dot(probs_low[0:span, :], jnp.concatenate(prepared[i][1], 0), 1, 0)
            grad_k = dot(grads_low[0:span, :], jnp.concatenate(prepared[i][0], 0), 1, 0)
            if below:
                sum_v[0:below, :] += grad_v[:below]
                sum_k[0:below, :] += grad_k[:below]
            sum_v[below:span, :] = grad_v[below:]
            sum_k[below:span, :] = grad_k[below:]
        current = following
    grad_k_ref[...] = (sum_k[...] * SCALE).astype(BF16)
    grad_v_ref[...] = sum_v[...].astype(BF16)


def column_blocks(rows, first):
    return pl.BlockSpec((rows, LANES), lambda group, length: (0, first + group))


def attention_backward(length, packed, mixed, grad_mixed, logs):
    rows, width = mixed.shape
    groups = width // LANES
    blocks = lambda part: column_blocks(rows, part * groups)
    return pl.pallas_call(
        attention_backward_kernel,
        grid_spec=pltpu.PrefetchScalarGridSpec(
            num_scalar_prefetch=1,
            grid=(groups,),
            in_specs=[
                blocks(0),
                blocks(1),
                blocks(2),
                blocks(0),
                blocks(0),
                pl.BlockSpec((1, HEADS, rows), lambda group, length: (group, 0, 0)),
            ],
            out_specs=[blocks(0)] * 3,
            scratch_shapes=[
                pltpu.VMEM((LANES, rows), BF16),
                pltpu.VMEM((LANES, BLOCK), F32),
                pltpu.VMEM((rows, HEADS * BLOCK), BF16),
                pltpu.VMEM((rows, HEADS * BLOCK), BF16),
                pltpu.VMEM((rows, LANES), F32),
                pltpu.VMEM((rows, LANES), F32),
            ],
        ),
        out_shape=[jax.ShapeDtypeStruct((rows, width), BF16)] * 3,
        compiler_params=pltpu.CompilerParams(vmem_limit_bytes=56 * MIB),
        cost_estimate=pl.CostEstimate(flops=40 * 10**9, bytes_accessed=12 * 10**6, transcendentals=0),
        name="attention_backward",
    )(length, packed, packed, packed, mixed, grad_mixed, logs)


def exchange(value, axis, size, bit):
    return lax.ppermute(value, axis, [(i, i ^ (1 << bit)) for i in range(size)])


def halve(value, axis, size, bit, dim):
    mine = (lax.axis_index(axis) >> bit) & 1
    kept = lax.dynamic_index_in_dim(value, mine, dim, keepdims=False)
    sent = lax.dynamic_index_in_dim(value, 1 - mine, dim, keepdims=False)
    got = exchange(sent, axis, size, bit)
    return (kept.astype(F32) + got.astype(F32)).astype(BF16)


def scatter_over_seq(value, size, order):
    bits = list(range(size.bit_length() - 1))
    value = value.reshape((2,) * len(bits) + value.shape[1:])
    left = bits[::-1]
    for bit in order:
        value = halve(value, "seq", size, bit, left.index(bit))
        left.remove(bit)
    return value


def sum_over_ctx(value, size):
    bits = list(range(size.bit_length() - 1))
    rows, columns = value.shape
    value = value.reshape((2,) * len(bits) + (rows // size, columns))
    left = bits[::-1]
    for bit in bits:
        value = halve(value, "ctx", size, bit, left.index(bit))
        left.remove(bit)
    for bit in bits[::-1]:
        got = exchange(value, "ctx", size, bit)
        low = ((lax.axis_index("ctx") >> bit) & 1) == 0
        value = jnp.stack([jnp.where(low, value, got), jnp.where(low, got, value)])
    value = value.transpose(tuple(bits[::-1]) + (len(bits), len(bits) + 1))
    return value.reshape(rows, columns)


def sum_weight(grad, seq_size, ctx_size):
    rows, columns = grad.shape
    blocks = grad.astype(BF16).reshape(seq_size, rows // seq_size, columns)
    order = list(range(seq_size.bit_length() - 1))
    other = order[:1] + order[1:][::-1]
    half = columns // 2
    first = scatter_over_seq(blocks[:, :, :half], seq_size, order)
    second = scatter_over_seq(blocks[:, :, half:], seq_size, other)
    summed = jnp.concatenate([first, second], axis=-1)
    return sum_over_ctx(summed, ctx_size).astype(F32)


def make_per_device(seq_size, ctx_size):
    def per_device(
        tokens,
        lengths,
        query_key_value_weight,
        attention_out_weight,
        up_weight,
        down_weight,
        ln1_gain,
        ln1_shift,
        ln2_gain,
        ln2_shift,
        cotangent,
    ):
        shape = tokens.shape
        width = shape[-1]
        length = lax.dynamic_slice_in_dim(lengths, lax.axis_index("ctx"), 1)
        row = lambda vector: vector.reshape(1, width)
        inputs, normed_low, packed, cotangent, mixed_low, logs = front(
            ctx_size, length, tokens, cotangent, query_key_value_weight, row(ln1_gain), row(ln1_shift)
        )
        output, grad_middle, grad_mixed, grad_down, grad_up, grad_out, grad_norm_two = feed_forward(
            length, inputs, mixed_low, cotangent, attention_out_weight, up_weight, down_weight,
            row(ln2_gain), row(ln2_shift),
        )
        grad_packed = jnp.concatenate(
            attention_backward(length, packed, mixed_low, grad_mixed, logs), axis=-1
        )
        grad_qkv = dot(normed_low, grad_packed, 0, 0)
        grad_normed = dot(grad_packed, query_key_value_weight, 1, 1)
        hat, inverse = normalise(inputs.reshape(-1, width).astype(F32))
        grad_gain_one = jnp.sum(grad_normed * hat, axis=0)
        grad_shift_one = jnp.sum(grad_normed, axis=0)
        grad_inputs = grad_middle + normalise_backward(grad_normed, hat, inverse, ln1_gain)
        grad_tokens = lax.all_to_all(grad_inputs.astype(BF16).reshape(shape), "ctx", 0, 0, tiled=True)
        vectors = jnp.stack([grad_gain_one, grad_shift_one, grad_norm_two[0], grad_norm_two[1]])
        vectors = lax.psum(vectors, ("seq", "ctx"))
        share = width // seq_size
        vectors = lax.dynamic_slice_in_dim(vectors, lax.axis_index("seq") * share, share, 1)
        return (
            output,
            grad_tokens,
            sum_weight(grad_qkv, seq_size, ctx_size),
            sum_weight(grad_out, seq_size, ctx_size),
            sum_weight(grad_up, seq_size, ctx_size),
            sum_weight(grad_down, seq_size, ctx_size),
            vectors[0],
            vectors[1],
            vectors[2],
            vectors[3],
        )

    return per_device


def solution(mesh):
    placed = (P("seq", "ctx", None), P("seq")) + (P(),) * 8 + (P("seq", "ctx", None),)
    weights = (P("seq", None),) * 4 + (P("seq"),) * 4
    return jax.shard_map(
        make_per_device(mesh.shape["seq"], mesh.shape["ctx"]),
        mesh=mesh,
        in_specs=placed,
        out_specs=(P("seq", "ctx", None),) * 2 + weights,
        check_vma=False,
    )
```

```python
import functools
import math

import jax
import jax.numpy as jnp
from jax import lax
from jax.experimental import pallas as pl
from jax.experimental.pallas import tpu as pltpu
from jax.sharding import PartitionSpec as P

HD = 32
LANES = 128
HEADS = LANES // HD
BLOCK = 256
SCALE = HD ** (-0.5)
SCALE_LOG2 = SCALE * math.log2(math.e)
BF16 = jnp.bfloat16
F32 = jnp.float32
MESH = pl.DeviceIdType.MESH
epsilon = 1e-05
MIB = 2**20
VMEM_LIMIT = 62 * MIB
ANY = pl.BlockSpec(memory_space=pl.ANY)
SMEM = pl.BlockSpec(memory_space=pltpu.SMEM)
ONE = pl.Buffered(1)


def dot(a, b, dim_a, dim_b):
    return lax.dot_general(
        a, b, (((dim_a,), (dim_b,)), ((), ())), preferred_element_type=F32
    )


def whole(shape):
    return pl.BlockSpec(shape, lambda step: (0,) * len(shape), pipeline_mode=ONE)


def struct(shape, kind=BF16):
    return jax.ShapeDtypeStruct(shape, kind)


def greet(partners):
    barrier = pltpu.get_barrier_semaphore()
    for partner in partners:
        pl.semaphore_signal(barrier, inc=1, device_id=partner, device_id_type=MESH)
    pl.semaphore_wait(barrier, len(partners))


def to_partner(source, target, send_sem, recv_sem, partner):
    return pltpu.make_async_remote_copy(
        src_ref=source,
        dst_ref=target,
        send_sem=send_sem,
        recv_sem=recv_sem,
        device_id=partner,
        device_id_type=MESH,
    )


def normalise(rows):
    centred = rows - jnp.mean(rows, axis=-1, keepdims=True)
    inverse = lax.rsqrt(jnp.mean(centred * centred, axis=-1, keepdims=True) + epsilon)
    return (centred * inverse, inverse)


def normalise_backward(grad, hat, inverse, gain):
    grad_hat = grad * gain
    along = jnp.mean(grad_hat * hat, axis=-1, keepdims=True)
    return inverse * (grad_hat - jnp.mean(grad_hat, axis=-1, keepdims=True) - hat * along)


def gelu_and_slope(value):
    bell = jnp.exp2(value * value * (-0.5 * math.log2(math.e)))
    t = 1.0 / (1.0 + jnp.abs(value) * (0.3275911 * math.sqrt(0.5)))
    series = (1.061405429 * t - 1.453152027) * t + 1.421413741
    series = ((series * t - 0.284496736) * t + 0.254829592) * t
    tail = (0.5 * series) * bell
    cdf = jnp.where(value >= 0, 1.0 - tail, tail)
    return (value * cdf, cdf + value * (bell * (1.0 / math.sqrt(2.0 * math.pi))))


def only_head(rows, head):
    lanes = lax.broadcasted_iota(jnp.int32, rows.shape, 1)
    return jnp.where(lanes // HD == head, rows, 0)


def mask_diagonal(scores, block, first, length):
    keys = first + lax.broadcasted_iota(jnp.int32, (block, block), 0)
    queries = first + lax.broadcasted_iota(jnp.int32, (block, block), 1)
    allowed = (keys <= queries) & (keys < length)
    below = scores.shape[0] - block
    diagonal = jnp.where(allowed, scores[below:], -1e30)
    return jnp.concatenate([scores[:below], diagonal], 0) if below else diagonal


def attend(group, length, packed, mixed_ref, log_ref, v_t, mixed_t):
    rows, width = packed.shape[0], packed.shape[1] // 3
    count = rows // BLOCK
    columns = [
        pl.ds(pl.multiple_of(part * width + group * LANES, LANES), LANES) for part in range(3)
    ]
    v_t[...] = packed[:, columns[2]].T

    def scores_of(i, head):
        span = (i + 1) * BLOCK
        query = only_head(packed[i * BLOCK : span, columns[0]], head)
        scores = dot(packed[0:span, columns[1]], query, 1, 1)
        return mask_diagonal(scores, BLOCK, i * BLOCK, length)

    steps = [(i, head) for i in range(count) for head in range(HEADS)]
    scores = scores_of(*steps[0])
    for number, (i, head) in enumerate(steps):
        span = (i + 1) * BLOCK
        following = scores_of(*steps[number + 1]) if number + 1 < len(steps) else None
        summit = jnp.max(scores, axis=0, keepdims=True)
        expo = jnp.exp2(scores * SCALE_LOG2 - summit * SCALE_LOG2)
        denom = jnp.sum(expo, axis=0, keepdims=True)
        part = dot(v_t[head * HD : (head + 1) * HD, 0:span], expo.astype(BF16), 1, 0)
        mixed_t[head * HD : (head + 1) * HD, :] = part / denom
        log_ref[0, head : head + 1, i * BLOCK : span] = summit * SCALE_LOG2 + jnp.log2(denom)
        if head == HEADS - 1:
            mixed_ref[i * BLOCK : span, :] = mixed_t[...].T.astype(BF16)
        scores = following


def front_kernel(
    ctx, length_ref, tokens, cotangent, weight, gain, shift,
    inputs_out, normed_out, packed_out, cotangent_out, mixed_ref, log_ref,
    inputs, normed, packed, v_t, mixed_t, send, recv, cot_send, cot_recv, local,
):
    step = pl.program_id(0)
    me = lax.axis_index("ctx")
    block = tokens.shape[1]
    offsets = [1] + list(range(2, ctx))

    def token_copy(offset):
        return to_partner(
            tokens.at[me ^ offset], inputs.at[me], send.at[offset], recv.at[offset],
            {"ctx": me ^ offset},
        )

    def cotangent_copy(offset):
        return to_partner(
            cotangent.at[me ^ offset], cotangent_out.at[me], cot_send.at[offset],
            cot_recv.at[offset], {"ctx": me ^ offset},
        )

    own_cotangent = pltpu.make_async_copy(cotangent.at[me], cotangent_out.at[me], local.at[1])
    keeps = [
        pltpu.make_async_copy(inputs, inputs_out, local.at[2]),
        pltpu.make_async_copy(normed, normed_out, local.at[3]),
        pltpu.make_async_copy(packed, packed_out, local.at[4]),
    ]

    @pl.when(step == 0)
    def _():
        own = pltpu.make_async_copy(tokens.at[me], inputs.at[me], local.at[0])
        own.start()
        greet([{"ctx": me ^ offset} for offset in offsets])
        for offset in offsets[::-1]:
            token_copy(offset).start()

        def project(source):
            hat, _ = normalise(inputs[source].astype(F32))
            low = (hat * gain[...] + shift[...]).astype(BF16)
            rows = pl.ds(pl.multiple_of(source * block, block), block)
            normed[rows, :] = low
            packed[rows, :] = dot(low, weight[...], 1, 0).astype(BF16)

        own.wait()
        project(me)
        for offset in offsets:
            token_copy(offset).wait_recv()
            if offset == offsets[-1]:
                for earlier in offsets:
                    token_copy(earlier).wait_send()
                own_cotangent.start()
                for later in offsets[::-1]:
                    cotangent_copy(later).start()
            project(me ^ offset)
        for keep in keeps:
            keep.start()

    @pl.when(step > 0)
    def _():
        attend(step - 1, length_ref[0], packed, mixed_ref, log_ref, v_t, mixed_t)

    @pl.when(step == pl.num_programs(0) - 1)
    def _():
        for keep in keeps:
            keep.wait()
        own_cotangent.wait()
        for offset in offsets:
            cotangent_copy(offset).wait()


def front(ctx, length, tokens, cotangent, weight, gain, shift):
    blocks, block, width = tokens.shape
    rows, groups = blocks * block, width // LANES
    group_of = lambda step: jnp.maximum(step - 1, 0)
    return pl.pallas_call(
        functools.partial(front_kernel, ctx),
        grid=(1 + groups,),
        in_specs=[SMEM, ANY, ANY, whole(weight.shape), whole(gain.shape), whole(shift.shape)],
        out_specs=[
            ANY, ANY, ANY, ANY,
            pl.BlockSpec((rows, LANES), lambda step: (0, group_of(step))),
            pl.BlockSpec((1, HEADS, rows), lambda step: (group_of(step), 0, 0)),
        ],
        out_shape=[
            struct(tokens.shape),
            struct((rows, width)),
            struct((rows, 3 * width)),
            struct(tokens.shape),
            struct((rows, width)),
            struct((groups, HEADS, rows), F32),
        ],
        scratch_shapes=[
            pltpu.VMEM(tokens.shape, BF16),
            pltpu.VMEM((rows, width), BF16),
            pltpu.VMEM((rows, 3 * width), BF16),
            pltpu.VMEM((LANES, rows), BF16),
            pltpu.VMEM((LANES, BLOCK), F32),
            pltpu.SemaphoreType.DMA((ctx,)),
            pltpu.SemaphoreType.DMA((ctx,)),
            pltpu.SemaphoreType.DMA((ctx,)),
            pltpu.SemaphoreType.DMA((ctx,)),
            pltpu.SemaphoreType.DMA((5,)),
        ],
        compiler_params=pltpu.CompilerParams(
            vmem_limit_bytes=56 * MIB, collective_id=0, has_side_effects=True
        ),
        name="front",
    )(length, tokens, cotangent, weight, gain, shift)


def feed_forward_kernel(
    blocks, length_ref, inputs, mixed, cotangent, out_weight, up_weight, down_weight, gain, shift,
    output, grad_middle_ref, grad_mixed_ref, grad_down_ref, grad_up_ref, grad_out_ref, grad_norm_ref,
    normed, upstream, branch, active, hidden, staged, send, recv, local,
):
    step = pl.program_id(0)
    me = lax.axis_index("ctx")
    block = staged.shape[1]
    width = normed.shape[1]
    wide = active.shape[1]
    cuts = wide // width

    def output_copy(row):
        return to_partner(
            staged.at[row], output.at[me], send.at[row], recv.at[me], {"ctx": row}
        )

    own_output = pltpu.make_async_copy(staged.at[me], output.at[me], local)

    @pl.when(step == 0)
    def _():
        greet([{"ctx": me ^ offset} for offset in range(1, blocks)])
        grad_norm_ref[...] = jnp.zeros_like(grad_norm_ref)

    @pl.when(step < blocks)
    def _():
        rows = pl.ds(pl.multiple_of(step * block, block), block)
        middle = inputs[step].astype(F32) + dot(mixed[rows, :], out_weight[...], 1, 0)
        hat, inverse = normalise(middle)
        low = (hat * gain[...] + shift[...]).astype(BF16)
        normed[rows, :] = low
        places = step * block + lax.broadcasted_iota(jnp.int32, (block, 1), 0)
        valid = places < length_ref[0]
        upstream_full = jnp.where(valid, cotangent[step].astype(F32), 0.0)
        upstream_low = upstream_full.astype(BF16)
        upstream[rows, :] = upstream_low

        def products_of(cut):
            part = slice(cut * width, (cut + 1) * width)
            return (
                dot(low, up_weight[:, part], 1, 0),
                dot(upstream_low, down_weight[part, :], 1, 1),
            )

        current = products_of(0)
        total, grad_normed = middle, 0.0
        for cut in range(cuts):
            part = slice(cut * width, (cut + 1) * width)
            following = products_of(cut + 1) if cut + 1 < cuts else None
            value, slope = gelu_and_slope(current[0])
            value = value.astype(BF16)
            grad_hidden = (slope * current[1]).astype(BF16)
            active[rows, part] = value
            hidden[rows, part] = grad_hidden
            total = total + dot(value, down_weight[part, :], 1, 0)
            grad_normed = grad_normed + dot(grad_hidden, up_weight[:, part], 1, 1)
            current = following
        staged[step] = jnp.where(valid, total, 0.0).astype(BF16)

        @pl.when(step != me)
        def _():
            output_copy(step).start()

        @pl.when(step == me)
        def _():
            own_output.start()

        grad_norm_ref[0:1, :] += jnp.sum(grad_normed * hat, axis=0, keepdims=True)
        grad_norm_ref[1:2, :] += jnp.sum(grad_normed, axis=0, keepdims=True)
        grad_middle = upstream_full + normalise_backward(grad_normed, hat, inverse, gain[...])
        grad_middle_ref[...] = grad_middle
        grad_branch = grad_middle.astype(BF16)
        branch[rows, :] = grad_branch
        grad_mixed_ref[...] = dot(grad_branch, out_weight[...], 1, 1).astype(BF16)

    @pl.when(step == blocks)
    def _():
        grad_out_ref[...] = dot(mixed[...], branch[...], 0, 0).astype(BF16)

    @pl.when(step >= blocks)
    def _():
        size = grad_down_ref.shape[0]
        part = pl.ds(pl.multiple_of((step - blocks) * size, size), size)
        grad_down_ref[...] = dot(active[:, part], upstream[...], 0, 0).astype(BF16)
        grad_up_ref[...] = dot(normed[...], hidden[:, part], 0, 0).astype(BF16)

    @pl.when(step == pl.num_programs(0) - 1)
    def _():
        own_output.wait()
        for row in range(blocks):

            @pl.when(row != me)
            def _():
                copy = output_copy(row)
                copy.wait_send()
                to_partner(
                    staged.at[row], output.at[row], send.at[row], recv.at[row], {"ctx": row}
                ).wait_recv()


def feed_forward(length, inputs, mixed, cotangent, out_weight, up_weight, down_weight, gain, shift):
    blocks, block, width = inputs.shape
    rows, wide = blocks * block, up_weight.shape[1]
    size = 512
    steps = blocks + wide // size
    early = lambda step: jnp.minimum(step, blocks - 1)
    late = lambda step: jnp.maximum(step - blocks, 0)
    operands = (inputs, mixed, cotangent, out_weight, up_weight, down_weight, gain, shift)
    return pl.pallas_call(
        functools.partial(feed_forward_kernel, blocks),
        grid=(steps,),
        in_specs=[SMEM] + [whole(operand.shape) for operand in operands],
        out_specs=[
            ANY,
            pl.BlockSpec((block, width), lambda step: (early(step), 0)),
            pl.BlockSpec((block, width), lambda step: (early(step), 0)),
            pl.BlockSpec((size, width), lambda step: (late(step), 0)),
            pl.BlockSpec((width, size), lambda step: (0, late(step))),
            whole((width, width)),
            whole((8, width)),
        ],
        out_shape=[
            struct(inputs.shape),
            struct((rows, width), F32),
            struct((rows, width)),
            struct((wide, width)),
            struct((width, wide)),
            struct((width, width)),
            struct((8, width), F32),
        ],
        scratch_shapes=[
            pltpu.VMEM((rows, width), BF16),
            pltpu.VMEM((rows, width), BF16),
            pltpu.VMEM((rows, width), BF16),
            pltpu.VMEM((rows, wide), BF16),
            pltpu.VMEM((rows, wide), BF16),
            pltpu.VMEM(inputs.shape, BF16),
            pltpu.SemaphoreType.DMA((blocks,)),
            pltpu.SemaphoreType.DMA((blocks,)),
            pltpu.SemaphoreType.DMA,
        ],
        compiler_params=pltpu.CompilerParams(
            vmem_limit_bytes=60 * MIB, collective_id=1, has_side_effects=True
        ),
        name="feed_forward",
    )(length, *operands)


PARTS = 3
KINDS = 8


class Chunk:
    def __init__(self, source, own, stages, send, recv, local, places):
        self.source, self.own = source, own
        self.r1, self.r2a, self.r2b, self.r3, self.z1, self.z2, self.out = stages
        self.send, self.recv, self.local, self.places = send, recv, local, places
        self.cut = self.r3.shape[-1] // 2

    def copy(self, kind):
        seq, ctx, core, x, y, low = self.places
        cut = self.cut
        ways = (
            lambda: (self.source.at[:, :, 1 - core], self.r1, {"seq": seq ^ 1}),
            lambda: (self.r1.at[:, 1 - x, :, :, 0:cut], self.r2a, {"seq": seq ^ 2}),
            lambda: (self.r1.at[1 - y, :, :, :, cut:], self.r2b, {"seq": seq ^ 4}),
            lambda: (self.r2a.at[1 - y], self.r3.at[:, :, 0:cut], {"seq": seq ^ 4}),
            lambda: (self.r2b.at[1 - x], self.r3.at[:, :, cut:], {"seq": seq ^ 2}),
            lambda: (self.r3.at[1 - low], self.z1, {"ctx": ctx ^ 1}),
            lambda: (self.z1, self.z2, {"ctx": ctx ^ 2}),
            lambda: (self.out.at[low], self.out.at[low], {"ctx": ctx ^ 1}),
        )
        source, target, partner = ways[kind]()
        return to_partner(source, target, self.send.at[kind], self.recv.at[kind], partner)

    def own_copy(self):
        core = self.places[2]
        return pltpu.make_async_copy(self.source.at[:, :, core], self.own, self.local)

    def event(self, number):
        seq, ctx, core, x, y, low = self.places
        cut = self.cut
        if number == 0:
            self.copy(0).start()
            if self.own is not None:
                self.own_copy().start()
        if number == 1:
            self.copy(0).wait_recv()
            if self.own is not None:
                self.own_copy().wait()
            for along_y in range(2):
                for along_x in range(2):
                    if self.own is not None:
                        kept = self.own[along_y, along_x]
                    else:
                        kept = self.source[along_y, along_x, core]
                    self.r1[along_y, along_x] += kept
            self.copy(1).start()
            self.copy(2).start()
        if number == 2:
            self.copy(1).wait_recv()
            self.copy(2).wait_recv()
            for other in range(2):
                self.r2a[other] += self.r1[other, x, :, :, 0:cut]
                self.r2b[other] += self.r1[y, other, :, :, cut:]
            self.copy(3).start()
            self.copy(4).start()
        if number == 3:
            self.copy(3).wait_recv()
            self.copy(4).wait_recv()
            self.r3[:, :, 0:cut] += self.r2a[y]
            self.r3[:, :, cut:] += self.r2b[x]
            self.copy(5).start()
        if number == 4:
            self.copy(5).wait_recv()
            self.z1[...] += self.r3[low]
            self.copy(6).start()
        if number == 5:
            self.copy(6).wait_recv()
            self.out[low] = self.z1[...] + self.z2[...]
            self.copy(7).start()
        if number == 6:
            to_partner(
                self.out.at[1 - low], self.out.at[1 - low], self.send.at[7], self.recv.at[7],
                {"ctx": ctx ^ 1},
            ).wait_recv()
            for kind in range(KINDS):
                self.copy(kind).wait_send()


def chunk_scratch(rows, columns, held):
    shapes = [
        (2, 2, 2, rows, columns),
        (2, 2, rows, columns // 2),
        (2, 2, rows, columns // 2),
        (2, rows, columns),
        (rows, columns),
        (rows, columns),
        (2, rows, columns),
    ]
    if held:
        shapes.insert(0, (2, 2, 2, rows, columns))
    return [pltpu.VMEM(shape, BF16) for shape in shapes]


PLAN = {
    (0, 0): [(0, 0)],
    (0, 3): [(1, 0), (2, 0)],
    (1, 0): [(0, 1)],
    (2, 0): [(3, 0)],
    (2, 3): [(0, 2), (1, 1)],
    (3, 0): [(2, 1), (3, 1)],
    (4, 0): [(4, 0)],
    (4, 1): [(0, 3)],
    (4, 3): [(2, 2), (3, 2), (4, 1)],
    (5, 0): [(0, 4)],
    (5, 1): [(1, 2)],
    (5, 3): [(2, 3), (3, 3)],
}
PLAN_BEFORE_NORM = [(5, 0), (4, 2), (1, 3), (0, 5), (2, 4), (3, 4)]
PLAN_AFTER_NORM = [
    "v0", (5, 1), (4, 3), "v1", (2, 5), (3, 5), (1, 4), "v2", (5, 2), (4, 4), "v3", (0, 6), (1, 5),
    (5, 3), (4, 5), (5, 4), "v4", (2, 6), (3, 6), (1, 6), (5, 5), (4, 6), (5, 6), "v5",
]


def back_kernel(
    fast, ctx, length_ref, q_ref, k_ref, v_ref, mixed_ref, grad_ref, log_ref, inputs_in, normed_in,
    middle_in, weight_in, gain, norm_two, *rest,
):
    rest = list(rest)
    take = lambda count: [rest.pop(0) for _ in range(count)]
    sources = take(3) if fast else []
    (grad_tokens,) = take(1)
    results = take(4) if fast else take(1)
    (vector_out,) = take(1)
    (inputs, normed, middle, weight, grad_normed, pair, partial, staged) = take(8)
    (k_t, grad_q_t, probs_low, grads_low, sum_k, sum_v) = take(6)
    (vectors, vectors_got, local, token_send, token_recv, v_send, v_recv) = take(7)
    step = pl.program_id(0)
    seq, me = lax.axis_index("seq"), lax.axis_index("ctx")
    rows, width = normed.shape
    blocks, block = staged.shape[0], staged.shape[1]
    groups = width // LANES
    chunks = []
    if fast:
        send, recv = take(2)
        places = (seq, me, seq % 2, (seq // 2) % 2, seq // 4, me % 2)
        for number in range(3 + PARTS):
            held = number < 3
            own = take(1)[0] if held else None
            source = sources[number] if held else partial.at[number - 3]
            chunks.append(
                Chunk(
                    source, own, take(7), send.at[number], recv.at[number],
                    local.at[5 + number], places,
                )
            )

    def run(name):
        if not fast:
            return
        if isinstance(name, tuple):
            chunks[name[0]].event(name[1])
            return
        number = int(name[1:])
        partners = [{"seq": seq ^ 1}, {"seq": seq ^ 2}, {"seq": seq ^ 4}]
        partners += [{"ctx": me ^ 1}, {"ctx": me ^ 2}]
        exchange = lambda n: to_partner(
            vectors.at[n], vectors_got.at[n], v_send.at[n], v_recv.at[n], partners[n]
        )
        if number:
            exchange(number - 1).wait()
            vectors[number] = vectors[number - 1] + vectors_got[number - 1]
        if number < len(partners):
            exchange(number).start()

    loads = [
        pltpu.make_async_copy(inputs_in, inputs, local.at[0]),
        pltpu.make_async_copy(normed_in, normed, local.at[1]),
        pltpu.make_async_copy(middle_in, middle, local.at[2]),
        pltpu.make_async_copy(weight_in, weight, local.at[3]),
    ]

    @pl.when(step == 0)
    def _():
        partners = [{"ctx": me ^ offset} for offset in range(1, ctx)]
        if fast:
            partners += [{"seq": seq ^ 1}, {"seq": seq ^ 2}, {"seq": seq ^ 4}]
        greet(partners)
        for load in loads:
            load.start()

    def hook(i):
        for group in range(groups):
            if (group, i) in PLAN:

                @pl.when(step == group)
                def _():
                    for name in PLAN[group, i]:
                        run(name)

    @pl.when(step < groups)
    def _():
        side = pl.ds(pl.multiple_of((step % 2) * LANES, LANES), LANES)
        attend_backward(
            hook, side, length_ref[0], q_ref, k_ref, v_ref, mixed_ref, grad_ref, log_ref, pair,
            k_t, grad_q_t, probs_low, grads_low, sum_k, sum_v,
        )

    @pl.when(step == 1)
    def _():
        for load in loads:
            load.wait()
        grad_normed[...] = jnp.zeros_like(grad_normed)

    @pl.when((step < groups) & (step % 2 == 1))
    def _():
        part = step // 2
        for name in range(PARTS):
            columns = slice(name * 2 * LANES, (name + 1) * 2 * LANES)
            product = dot(normed[...], pair[name], 0, 0).astype(BF16)
            if fast:
                partial[part, :, :, :, :, :, columns] = product.reshape(
                    2, 2, 2, 2, width // 16, 2 * LANES
                )
            else:
                partial[part, :, columns] = product
            there = pl.ds(
                pl.multiple_of(name * width + part * 2 * LANES, 2 * LANES), 2 * LANES
            )
            grad_normed[...] += dot(pair[name], weight[:, there], 1, 1)

    def token_copy(row):
        return to_partner(
            staged.at[row], grad_tokens.at[me], token_send.at[row], token_recv.at[me], {"ctx": row}
        )

    own_tokens = pltpu.make_async_copy(staged.at[me], grad_tokens.at[me], local.at[4])

    @pl.when(step == groups)
    def _():
        for name in PLAN_BEFORE_NORM:
            run(name)
        gain_sum, shift_sum = 0.0, 0.0
        for row in range(blocks):
            there = slice(row * block, (row + 1) * block)
            hat, inverse = normalise(inputs[row].astype(F32))
            grad = grad_normed[there, :]
            gain_sum = gain_sum + jnp.sum(grad * hat, axis=0, keepdims=True)
            shift_sum = shift_sum + jnp.sum(grad, axis=0, keepdims=True)
            total = middle[there, :] + normalise_backward(grad, hat, inverse, gain[...])
            staged[row] = total.astype(BF16)

            @pl.when(row != me)
            def _():
                token_copy(row).start()

            @pl.when(row == me)
            def _():
                own_tokens.start()

        vectors[0] = jnp.concatenate([gain_sum, shift_sum, norm_two[0:6, :]], axis=0)
        for name in PLAN_AFTER_NORM:
            run(name)
        if fast:
            for number in range(3):
                results[number][...] = chunks[number].out[...]
            for number in range(PARTS):
                results[3][number] = chunks[3 + number].out[...]
            vector_out[...] = vectors[5]
        else:
            results[0][...] = partial[...]
            vector_out[...] = vectors[0]
        own_tokens.wait()
        for row in range(blocks):

            @pl.when(row != me)
            def _():
                token_copy(row).wait_send()
                to_partner(
                    staged.at[row], grad_tokens.at[row], token_send.at[row], token_recv.at[row],
                    {"ctx": row},
                ).wait_recv()


def attend_backward(
    hook, side, length, q_ref, k_ref, v_ref, mixed_ref, grad_ref, log_ref, pair,
    k_t, grad_q_t, probs_low, grads_low, sum_k, sum_v,
):
    count = q_ref.shape[0] // BLOCK
    k_t[...] = k_ref[...].T

    def rows_of(i):
        rows = slice(i * BLOCK, (i + 1) * BLOCK)
        product = (grad_ref[rows, :].astype(F32) * mixed_ref[rows, :].astype(F32)).T
        queries = [only_head(q_ref[rows, :], head) for head in range(HEADS)]
        grads = [only_head(grad_ref[rows, :], head) for head in range(HEADS)]
        inner = [
            jnp.sum(product[head * HD : (head + 1) * HD], axis=0, keepdims=True)
            for head in range(HEADS)
        ]
        return (queries, grads, inner)

    prepared = [rows_of(i) for i in range(count)]

    def products_of(i, head):
        span = (i + 1) * BLOCK
        scores = dot(k_ref[0:span, :], prepared[i][0][head], 1, 1)
        return (scores, dot(v_ref[0:span, :], prepared[i][1][head], 1, 1))

    steps = [(i, head) for i in range(count) for head in range(HEADS)]
    current = products_of(*steps[0])
    for number, (i, head) in enumerate(steps):
        below = i * BLOCK
        span = below + BLOCK
        if head == 0:
            hook(i)
        following = products_of(*steps[number + 1]) if number + 1 < len(steps) else None
        scores, grad_probs = current
        scores = mask_diagonal(scores, BLOCK, below, length)
        probs = jnp.exp2(scores * SCALE_LOG2 - log_ref[0, head : head + 1, below:span])
        grad_scores = (probs * (grad_probs - prepared[i][2][head])).astype(BF16)
        columns = slice(head * BLOCK, (head + 1) * BLOCK)
        probs_low[0:span, columns] = probs.astype(BF16)
        grads_low[0:span, columns] = grad_scores
        grad_q_t[head * HD : (head + 1) * HD, :] = dot(
            k_t[head * HD : (head + 1) * HD, 0:span], grad_scores, 1, 0
        )
        if head == HEADS - 1:
            pair[0, below:span, side] = (grad_q_t[...].T * SCALE).astype(BF16)
            grad_v = dot(probs_low[0:span, :], jnp.concatenate(prepared[i][1], 0), 1, 0)
            grad_k = dot(grads_low[0:span, :], jnp.concatenate(prepared[i][0], 0), 1, 0)
            if below:
                sum_v[0:below, :] += grad_v[:below]
                sum_k[0:below, :] += grad_k[:below]
            sum_v[below:span, :] = grad_v[below:]
            sum_k[below:span, :] = grad_k[below:]
        current = following
    pair[1, :, side] = (sum_k[...] * SCALE).astype(BF16)
    pair[2, :, side] = sum_v[...].astype(BF16)


def back(
    fast, ctx, length, packed, mixed, grad_mixed, logs, inputs, normed, middle, weight, gain,
    norm_two, partials,
):
    rows, width = mixed.shape
    blocks, block, _ = inputs.shape
    groups = width // LANES
    group_of = lambda step: jnp.minimum(step, groups - 1)
    columns = lambda part: pl.BlockSpec(
        (rows, LANES), lambda step: (0, part * groups + group_of(step))
    )
    if fast:
        lead = (2, 2, 2, 2)
        partials = [
            grad.reshape(lead + (grad.shape[0] // 16, grad.shape[1])) for grad in partials
        ]
        sizes = [grad.shape[-2:] for grad in partials] + [(width // 16, width)] * PARTS
        reduced = [(2,) + size for size in sizes[:3]] + [(PARTS, 2, width // 16, width)]
        held = [PARTS] + list(lead) + [width // 16, width]
        extra = [
            pltpu.SemaphoreType.DMA((len(sizes), KINDS)),
            pltpu.SemaphoreType.DMA((len(sizes), KINDS)),
        ]
        for number, size in enumerate(sizes):
            extra += chunk_scratch(*size, held=number < 3)
    else:
        partials = []
        reduced = [(PARTS, width, width)]
        held = [PARTS, width, width]
        extra = []
    scratch = [
        pltpu.VMEM(inputs.shape, BF16),
        pltpu.VMEM((rows, width), BF16),
        pltpu.VMEM((rows, width), F32),
        pltpu.VMEM(weight.shape, BF16),
        pltpu.VMEM((rows, width), F32),
        pltpu.VMEM((PARTS, rows, 2 * LANES), BF16),
        pltpu.VMEM(tuple(held), BF16),
        pltpu.VMEM(inputs.shape, BF16),
        pltpu.VMEM((LANES, rows), BF16),
        pltpu.VMEM((LANES, BLOCK), F32),
        pltpu.VMEM((rows, HEADS * BLOCK), BF16),
        pltpu.VMEM((rows, HEADS * BLOCK), BF16),
        pltpu.VMEM((rows, LANES), F32),
        pltpu.VMEM((rows, LANES), F32),
        pltpu.VMEM((6, 8, width), F32),
        pltpu.VMEM((5, 8, width), F32),
        pltpu.SemaphoreType.DMA((5 + 3 + PARTS,)),
        pltpu.SemaphoreType.DMA((blocks,)),
        pltpu.SemaphoreType.DMA((blocks,)),
        pltpu.SemaphoreType.DMA((5,)),
        pltpu.SemaphoreType.DMA((5,)),
    ]
    return pl.pallas_call(
        functools.partial(back_kernel, fast, ctx),
        grid=(groups + 1,),
        in_specs=[
            SMEM, columns(0), columns(1), columns(2), columns(0), columns(0),
            pl.BlockSpec((1, HEADS, rows), lambda step: (group_of(step), 0, 0)),
            ANY, ANY, ANY, ANY, whole(gain.shape), whole(norm_two.shape),
        ] + [ANY] * len(partials),
        out_specs=[ANY] + [whole(shape) for shape in reduced] + [whole((8, width))],
        out_shape=[struct(inputs.shape)]
        + [struct(shape) for shape in reduced]
        + [struct((8, width), F32)],
        scratch_shapes=scratch + extra,
        compiler_params=pltpu.CompilerParams(
            vmem_limit_bytes=VMEM_LIMIT, collective_id=2, has_side_effects=True
        ),
        name="back",
    )(
        length, packed, packed, packed, mixed, grad_mixed, logs, inputs, normed, middle, weight,
        gain, norm_two, *partials,
    )


def exchange(value, axis, size, bit):
    return lax.ppermute(value, axis, [(i, i ^ (1 << bit)) for i in range(size)])


def halve(value, axis, size, bit, dim):
    mine = (lax.axis_index(axis) >> bit) & 1
    kept = lax.dynamic_index_in_dim(value, mine, dim, keepdims=False)
    sent = lax.dynamic_index_in_dim(value, 1 - mine, dim, keepdims=False)
    got = exchange(sent, axis, size, bit)
    return (kept.astype(F32) + got.astype(F32)).astype(BF16)


def scatter_over_seq(value, size, order):
    bits = list(range(size.bit_length() - 1))
    value = value.reshape((2,) * len(bits) + value.shape[1:])
    left = bits[::-1]
    for bit in order:
        value = halve(value, "seq", size, bit, left.index(bit))
        left.remove(bit)
    return value


def sum_over_ctx(value, size):
    bits = list(range(size.bit_length() - 1))
    rows, columns = value.shape
    value = value.reshape((2,) * len(bits) + (rows // size, columns))
    left = bits[::-1]
    for bit in bits:
        value = halve(value, "ctx", size, bit, left.index(bit))
        left.remove(bit)
    for bit in bits[::-1]:
        got = exchange(value, "ctx", size, bit)
        low = ((lax.axis_index("ctx") >> bit) & 1) == 0
        value = jnp.stack([jnp.where(low, value, got), jnp.where(low, got, value)])
    value = value.transpose(tuple(bits[::-1]) + (len(bits), len(bits) + 1))
    return value.reshape(rows, columns)


def sum_weight(grad, seq_size, ctx_size):
    rows, columns = grad.shape
    blocks = grad.reshape(seq_size, rows // seq_size, columns)
    order = list(range(seq_size.bit_length() - 1))
    other = order[:1] + order[1:][::-1]
    half = columns // 2
    first = scatter_over_seq(blocks[:, :, :half], seq_size, order)
    second = scatter_over_seq(blocks[:, :, half:], seq_size, other)
    return sum_over_ctx(jnp.concatenate([first, second], axis=-1), ctx_size)


def unpair(parts, rows, width):
    parts = parts.reshape(PARTS, rows, 3, width // PARTS)
    return parts.transpose(1, 2, 0, 3).reshape(rows, 3 * width)


def make_per_device(seq_size, ctx_size):
    fast = seq_size == 8 and ctx_size == 4

    def per_device(
        tokens,
        lengths,
        query_key_value_weight,
        attention_out_weight,
        up_weight,
        down_weight,
        ln1_gain,
        ln1_shift,
        ln2_gain,
        ln2_shift,
        cotangent,
    ):
        width = tokens.shape[-1]
        length = lax.dynamic_slice_in_dim(lengths, lax.axis_index("ctx"), 1)
        row = lambda vector: vector.reshape(1, width)
        inputs, normed_low, packed, cotangent, mixed_low, logs = front(
            ctx_size, length, tokens, cotangent, query_key_value_weight, row(ln1_gain), row(ln1_shift)
        )
        output, grad_middle, grad_mixed, grad_down, grad_up, grad_out, grad_norm_two = feed_forward(
            length, inputs, mixed_low, cotangent, attention_out_weight, up_weight, down_weight,
            row(ln2_gain), row(ln2_shift),
        )
        partials = [grad_down, grad_up, grad_out]
        grad_tokens, *sums, vectors = back(
            fast, ctx_size, length, packed, mixed_low, grad_mixed, logs, inputs, normed_low,
            grad_middle, query_key_value_weight, row(ln1_gain), grad_norm_two, partials,
        )
        share = width // seq_size
        if fast:
            down, up, out = [part.reshape(-1, part.shape[-1]) for part in sums[:3]]
            qkv = unpair(sums[3], share, width)
        else:
            grad_qkv = unpair(sums[0], width, width)
            down, up, out, qkv = [
                sum_weight(part, seq_size, ctx_size) for part in partials + [grad_qkv]
            ]
            vectors = lax.psum(vectors, ("seq", "ctx"))
        vectors = lax.dynamic_slice_in_dim(vectors, lax.axis_index("seq") * share, share, 1)
        return (
            output,
            grad_tokens,
            qkv.astype(F32),
            out.astype(F32),
            up.astype(F32),
            down.astype(F32),
            vectors[0],
            vectors[1],
            vectors[2],
            vectors[3],
        )

    return per_device


def solution(mesh):
    placed = (P("seq", "ctx", None), P("seq")) + (P(),) * 8 + (P("seq", "ctx", None),)
    weights = (P("seq", None),) * 4 + (P("seq"),) * 4
    return jax.shard_map(
        make_per_device(mesh.shape["seq"], mesh.shape["ctx"]),
        mesh=mesh,
        in_specs=placed,
        out_specs=(P("seq", "ctx", None),) * 2 + weights,
        check_vma=False,
    )
```

```python
import functools
import math

import jax
import jax.numpy as jnp
from jax import lax
from jax.experimental import pallas as pl
from jax.experimental.pallas import tpu as pltpu
from jax.sharding import PartitionSpec as P

HD = 32
LANES = 128
HEADS = LANES // HD
BLOCK = 256
SCALE = HD ** (-0.5)
SCALE_LOG2 = SCALE * math.log2(math.e)
BF16 = jnp.bfloat16
F32 = jnp.float32
MESH = pl.DeviceIdType.MESH
epsilon = 1e-05
MIB = 2**20
VMEM_LIMIT = 62 * MIB
ANY = pl.BlockSpec(memory_space=pl.ANY)
SMEM = pl.BlockSpec(memory_space=pltpu.SMEM)
ONE = pl.Buffered(1)
VECTOR = pl.BlockSpec(memory_space=pltpu.VMEM)


def dot(a, b, dim_a, dim_b):
    return lax.dot_general(
        a, b, (((dim_a,), (dim_b,)), ((), ())), preferred_element_type=F32
    )


def whole(shape):
    return pl.BlockSpec(shape, lambda step: (0,) * len(shape), pipeline_mode=ONE)


def row_of(vector):
    return vector[...].reshape(1, -1)


def struct(shape, kind=BF16):
    return jax.ShapeDtypeStruct(shape, kind)


def greet(partners):
    barrier = pltpu.get_barrier_semaphore()
    for partner in partners:
        pl.semaphore_signal(barrier, inc=1, device_id=partner, device_id_type=MESH)
    pl.semaphore_wait(barrier, len(partners))


def to_partner(source, target, send_sem, recv_sem, partner):
    return pltpu.make_async_remote_copy(
        src_ref=source,
        dst_ref=target,
        send_sem=send_sem,
        recv_sem=recv_sem,
        device_id=partner,
        device_id_type=MESH,
    )


def normalise(rows):
    centred = rows - jnp.mean(rows, axis=-1, keepdims=True)
    inverse = lax.rsqrt(jnp.mean(centred * centred, axis=-1, keepdims=True) + epsilon)
    return (centred * inverse, inverse)


def normalise_backward(grad, hat, inverse, gain):
    grad_hat = grad * gain
    along = jnp.mean(grad_hat * hat, axis=-1, keepdims=True)
    return inverse * (grad_hat - jnp.mean(grad_hat, axis=-1, keepdims=True) - hat * along)


def gelu_and_slope(value):
    cdf = 0.5 * lax.erf(value * math.sqrt(0.5)) + 0.5
    bell = jnp.exp2(value * value * (-0.5 * math.log2(math.e)))
    return (value * cdf, cdf + value * (bell * (1.0 / math.sqrt(2.0 * math.pi))))


def only_head(rows, head):
    lanes = lax.broadcasted_iota(jnp.int32, rows.shape, 1)
    return jnp.where(lanes // HD == head, rows, 0)


def mask_diagonal(scores, block, first, length):
    keys = first + lax.broadcasted_iota(jnp.int32, (block, block), 0)
    queries = first + lax.broadcasted_iota(jnp.int32, (block, block), 1)
    allowed = (keys <= queries) & (keys < length)
    below = scores.shape[0] - block
    diagonal = jnp.where(allowed, scores[below:], -1e30)
    return jnp.concatenate([scores[:below], diagonal], 0) if below else diagonal


def attend(group, length, packed, mixed_ref, log_ref, v_t, mixed_t):
    rows, width = packed.shape[0], packed.shape[1] // 3
    count = rows // BLOCK
    columns = [
        pl.ds(pl.multiple_of(part * width + group * LANES, LANES), LANES) for part in range(3)
    ]
    v_t[...] = packed[:, columns[2]].T

    def scores_of(i, head):
        span = (i + 1) * BLOCK
        query = only_head(packed[i * BLOCK : span, columns[0]], head)
        scores = dot(packed[0:span, columns[1]], query, 1, 1)
        return mask_diagonal(scores, BLOCK, i * BLOCK, length)

    steps = [(i, head) for i in range(count) for head in range(HEADS)]
    scores = scores_of(*steps[0])
    for number, (i, head) in enumerate(steps):
        span = (i + 1) * BLOCK
        following = scores_of(*steps[number + 1]) if number + 1 < len(steps) else None
        summit = jnp.max(scores, axis=0, keepdims=True)
        expo = jnp.exp2(scores * SCALE_LOG2 - summit * SCALE_LOG2)
        denom = jnp.sum(expo, axis=0, keepdims=True)
        part = dot(v_t[head * HD : (head + 1) * HD, 0:span], expo.astype(BF16), 1, 0)
        mixed_t[head * HD : (head + 1) * HD, :] = part / denom
        log_ref[0, head : head + 1, i * BLOCK : span] = summit * SCALE_LOG2 + jnp.log2(denom)
        if head == HEADS - 1:
            mixed_ref[i * BLOCK : span, :] = mixed_t[...].T.astype(BF16)
        scores = following


def front_kernel(
    ctx, length_ref, tokens, cotangent, weight, gain, shift,
    inputs_out, normed_out, packed_out, cotangent_out, mixed_ref, log_ref,
    inputs, normed, packed, v_t, mixed_t, send, recv, cot_send, cot_recv, local,
):
    step = pl.program_id(0)
    me = lax.axis_index("ctx")
    block = tokens.shape[1]
    offsets = [1] + list(range(2, ctx))

    def token_copy(offset):
        return to_partner(
            tokens.at[me ^ offset], inputs.at[me], send.at[offset], recv.at[offset],
            {"ctx": me ^ offset},
        )

    def cotangent_copy(offset):
        return to_partner(
            cotangent.at[me ^ offset], cotangent_out.at[me], cot_send.at[offset],
            cot_recv.at[offset], {"ctx": me ^ offset},
        )

    own_cotangent = pltpu.make_async_copy(cotangent.at[me], cotangent_out.at[me], local.at[1])
    keeps = [
        pltpu.make_async_copy(inputs, inputs_out, local.at[2]),
        pltpu.make_async_copy(normed, normed_out, local.at[3]),
        pltpu.make_async_copy(packed, packed_out, local.at[4]),
    ]

    @pl.when(step == 0)
    def _():
        own = pltpu.make_async_copy(tokens.at[me], inputs.at[me], local.at[0])
        own.start()
        greet([{"ctx": me ^ offset} for offset in offsets])
        for offset in offsets[::-1]:
            token_copy(offset).start()

        def project(source):
            hat, _ = normalise(inputs[source].astype(F32))
            low = (hat * row_of(gain) + row_of(shift)).astype(BF16)
            rows = pl.ds(pl.multiple_of(source * block, block), block)
            normed[rows, :] = low
            packed[rows, :] = dot(low, weight[...], 1, 0).astype(BF16)

        own.wait()
        project(me)
        for offset in offsets:
            token_copy(offset).wait_recv()
            if offset == offsets[-1]:
                for earlier in offsets:
                    token_copy(earlier).wait_send()
                own_cotangent.start()
                for later in offsets[::-1]:
                    cotangent_copy(later).start()
            project(me ^ offset)
        for keep in keeps:
            keep.start()

    @pl.when(step > 0)
    def _():
        attend(step - 1, length_ref[me], packed, mixed_ref, log_ref, v_t, mixed_t)

    @pl.when(step == pl.num_programs(0) - 1)
    def _():
        for keep in keeps:
            keep.wait()
        own_cotangent.wait()
        for offset in offsets:
            cotangent_copy(offset).wait()


def front(ctx, length, tokens, cotangent, weight, gain, shift):
    blocks, block, width = tokens.shape
    rows, groups = blocks * block, width // LANES
    group_of = lambda step: jnp.maximum(step - 1, 0)
    return pl.pallas_call(
        functools.partial(front_kernel, ctx),
        grid=(1 + groups,),
        in_specs=[SMEM, ANY, ANY, whole(weight.shape), VECTOR, VECTOR],
        out_specs=[
            ANY, ANY, ANY, ANY,
            pl.BlockSpec((rows, LANES), lambda step: (0, group_of(step))),
            pl.BlockSpec((1, HEADS, rows), lambda step: (group_of(step), 0, 0)),
        ],
        out_shape=[
            struct(tokens.shape),
            struct((rows, width)),
            struct((rows, 3 * width)),
            struct(tokens.shape),
            struct((rows, width)),
            struct((groups, HEADS, rows), F32),
        ],
        scratch_shapes=[
            pltpu.VMEM(tokens.shape, BF16),
            pltpu.VMEM((rows, width), BF16),
            pltpu.VMEM((rows, 3 * width), BF16),
            pltpu.VMEM((LANES, rows), BF16),
            pltpu.VMEM((LANES, BLOCK), F32),
            pltpu.SemaphoreType.DMA((ctx,)),
            pltpu.SemaphoreType.DMA((ctx,)),
            pltpu.SemaphoreType.DMA((ctx,)),
            pltpu.SemaphoreType.DMA((ctx,)),
            pltpu.SemaphoreType.DMA((5,)),
        ],
        compiler_params=pltpu.CompilerParams(
            vmem_limit_bytes=56 * MIB, collective_id=0, has_side_effects=True
        ),
        name="front",
    )(length, tokens, cotangent, weight, gain, shift)


PARTS = 3
KINDS = 8


class Chunk:
    def __init__(self, source, own, stages, send, recv, local, places, second=False):
        self.source, self.own, self.second = source, own, second
        self.r1, self.r2a, self.r2b, self.r3, self.z1, self.z2, self.out = stages
        self.send, self.recv, self.local, self.places = send, recv, local, places
        self.cut = self.r2a.shape[-1]

    def copy(self, kind):
        seq, ctx, core, x, y, low = self.places
        cut = self.cut
        ways = (
            lambda: (self.source.at[:, :, 1 - core], self.r1, {"seq": seq ^ 1}),
            lambda: (self.r1.at[:, 1 - x, :, :, 0:cut], self.r2a, {"seq": seq ^ 2}),
            lambda: (self.r1.at[1 - y, :, :, :, cut:], self.r2b, {"seq": seq ^ 4}),
            lambda: (self.r2a.at[1 - y], self.r3.at[:, :, 0:cut], {"seq": seq ^ 4}),
            lambda: (self.r2b.at[1 - x], self.r3.at[:, :, cut:], {"seq": seq ^ 2}),
            lambda: (self.r3.at[1 - low], self.z1, {"ctx": ctx ^ 1}),
            lambda: (self.z1, self.z2, {"ctx": ctx ^ 2}),
            lambda: (self.out.at[low], self.out.at[low], {"ctx": ctx ^ 1}),
        )
        source, target, partner = ways[kind]()
        return to_partner(source, target, self.send.at[kind], self.recv.at[kind], partner)

    def own_copy(self):
        core = self.places[2]
        return pltpu.make_async_copy(self.source.at[:, :, core], self.own, self.local)

    def add_second(self):
        _, _, _, x, y, _ = self.places
        cut = self.cut
        self.copy(1).wait_recv()
        self.copy(2).wait_recv()
        for other in range(2):
            self.r2a[other] += self.r1[other, x, :, :, 0:cut]
            self.r2b[other] += self.r1[y, other, :, :, cut:]

    def finish_second(self):
        self.add_second()
        for kind in range(3):
            self.copy(kind).wait_send()

    def event(self, number):
        seq, ctx, core, x, y, low = self.places
        cut = self.cut
        if number == 0:
            self.copy(0).start()
            if self.own is not None:
                self.own_copy().start()
        if number == 1:
            self.copy(0).wait_recv()
            if self.own is not None:
                self.own_copy().wait()
            for along_y in range(2):
                for along_x in range(2):
                    if self.own is not None:
                        kept = self.own[along_y, along_x]
                    else:
                        kept = self.source[along_y, along_x, core]
                    self.r1[along_y, along_x] += kept
            self.copy(1).start()
            self.copy(2).start()
        if number == 2:
            if not self.second:
                self.add_second()
            self.copy(3).start()
            self.copy(4).start()
        if number == 3:
            self.copy(3).wait_recv()
            self.copy(4).wait_recv()
            self.r3[:, :, 0:cut] += self.r2a[y]
            self.r3[:, :, cut:] += self.r2b[x]
            self.copy(5).start()
        if number == 4:
            self.copy(5).wait_recv()
            self.z1[...] += self.r3[low]
            self.copy(6).start()
        if number == 5:
            self.copy(6).wait_recv()
            self.out[low] = self.z1[...] + self.z2[...]
            self.copy(7).start()
        if number == 6:
            to_partner(
                self.out.at[1 - low], self.out.at[1 - low], self.send.at[7], self.recv.at[7],
                {"ctx": ctx ^ 1},
            ).wait_recv()
            for kind in range(3 if self.second else 0, KINDS):
                self.copy(kind).wait_send()


CUT = 512
PIECES = 8


def feed_forward_kernel(
    fast, blocks, length_ref, inputs, mixed, out_weight, gain, shift, up_in, down_in,
    cotangent_in,
    output, grad_down_out, grad_middle_ref, grad_mixed_ref, grad_up_ref, grad_out_ref,
    grad_norm_ref, *rest,
):
    rest = list(rest)
    take = lambda count: [rest.pop(0) for _ in range(count)]
    carried = take(2) if fast else []
    (up_weight, down_weight, normed, upstream, branch, active, hidden, scaled, inverse_of) = take(9)
    (staged, cotangent, grad_down, output_send, output_recv, local) = take(6)
    step = pl.program_id(0)
    seq, me = lax.axis_index("seq"), lax.axis_index("ctx")
    block, width = staged.shape[1:]
    wide = active.shape[1]
    cuts = wide // CUT
    backward = blocks + 1
    late = backward + blocks
    chunk = None
    if fast:
        send, recv, r1, r2a, r2b = take(5)
        places = (seq, me, seq % 2, (seq // 2) % 2, seq // 4, me % 2)
        chunk = Chunk(
            grad_down, None, (r1, r2a, r2b, None, None, None, None), send, recv, None, places
        )

    def output_copy(row):
        return to_partner(
            staged.at[row], output.at[me], output_send.at[row], output_recv.at[me], {"ctx": row}
        )

    own_output = pltpu.make_async_copy(staged.at[me], output.at[me], local.at[0])
    cotangent_load = pltpu.make_async_copy(cotangent_in, cotangent, local.at[4])
    up_load = pltpu.make_async_copy(up_in, up_weight, local.at[1])
    down_load = pltpu.make_async_copy(down_in, down_weight, local.at[2])

    @pl.when(step == 0)
    def _():
        up_load.start()
        down_load.start()
        partners = [{"ctx": me ^ offset} for offset in range(1, blocks)]
        if fast:
            partners += [{"seq": seq ^ 1}, {"seq": seq ^ 2}, {"seq": seq ^ 4}]
        greet(partners)
        cotangent_load.start()
        grad_norm_ref[...] = jnp.zeros_like(grad_norm_ref)

    def rows_of(number):
        return pl.ds(pl.multiple_of(number * block, block), block)

    def valid_rows(number):
        places = number * block + lax.broadcasted_iota(jnp.int32, (block, 1), 0)
        return places < length_ref[me]

    @pl.when(step < blocks)
    def _():
        row = me ^ ((step + blocks // 2) % blocks)
        rows = rows_of(row)
        middle = inputs[row].astype(F32) + dot(mixed[rows, :], out_weight[...], 1, 0)
        hat, inverse = normalise(middle)
        scaled[rows, :] = hat
        inverse_of[rows, :] = inverse
        low = (hat * row_of(gain) + row_of(shift)).astype(BF16)
        normed[rows, :] = low

        @pl.when(step == 0)
        def _():
            up_load.wait()
            down_load.wait()

        product_of = lambda cut: dot(low, up_weight[:, cut * CUT : (cut + 1) * CUT], 1, 0)
        current = product_of(0)
        total = middle
        for cut in range(cuts):
            part = slice(cut * CUT, (cut + 1) * CUT)
            following = product_of(cut + 1) if cut + 1 < cuts else None
            value, slope = gelu_and_slope(current)
            value = value.astype(BF16)
            active[rows, part] = value
            hidden[rows, part] = slope.astype(BF16)
            total = total + dot(value, down_weight[part, :], 1, 0)
            current = following
        staged[row] = jnp.where(valid_rows(row), total, 0.0).astype(BF16)

        @pl.when(row != me)
        def _():
            output_copy(row).start()

        @pl.when(row == me)
        def _():
            own_output.start()

    @pl.when(step == blocks)
    def _():
        cotangent_load.wait()
        for row in range(blocks):
            kept = jnp.where(valid_rows(row), cotangent[row], 0)
            upstream[row * block : (row + 1) * block, :] = kept
        size = wide // PIECES

        @pl.loop(0, PIECES)
        def _(piece):
            columns = pl.ds(pl.multiple_of(piece * size, LANES), size)
            product = dot(active[:, columns], upstream[...], 0, 0)
            product = product.astype(BF16).reshape(2, size // 2, width)
            grad_down[piece // 4, (piece // 2) % 2, piece % 2] = product

        if fast:
            chunk.event(0)
        else:
            pltpu.make_async_copy(grad_down, grad_down_out, local.at[3]).start()

    @pl.when((step >= backward) & (step < late))
    def _():
        number = step - backward
        rows = rows_of(number)
        upstream_low = upstream[rows, :]

        @pl.when(number == 2)
        def _():
            if fast:
                chunk.event(1)

        product_of = lambda cut: dot(
            upstream_low, down_weight[cut * CUT : (cut + 1) * CUT, :], 1, 1
        )
        current = product_of(0)
        grad_normed = 0.0
        for cut in range(cuts):
            part = slice(cut * CUT, (cut + 1) * CUT)
            following = product_of(cut + 1) if cut + 1 < cuts else None
            grad_hidden = (hidden[rows, part].astype(F32) * current).astype(BF16)
            hidden[rows, part] = grad_hidden
            grad_normed = grad_normed + dot(grad_hidden, up_weight[:, part], 1, 1)
            current = following
        hat = scaled[rows, :]
        grad_norm_ref[0:1, :] += jnp.sum(grad_normed * hat, axis=0, keepdims=True)
        grad_norm_ref[1:2, :] += jnp.sum(grad_normed, axis=0, keepdims=True)
        through = normalise_backward(grad_normed, hat, inverse_of[rows, :], row_of(gain))
        grad_middle = upstream_low.astype(F32) + through
        grad_middle_ref[...] = grad_middle
        grad_branch = grad_middle.astype(BF16)
        branch[rows, :] = grad_branch
        grad_mixed_ref[...] = dot(grad_branch, out_weight[...], 1, 1).astype(BF16)

    @pl.when(step == late)
    def _():
        grad_out_ref[...] = dot(mixed[...], branch[...], 0, 0).astype(BF16)

    @pl.when(step >= late)
    def _():
        size = grad_up_ref.shape[1]
        part = pl.ds(pl.multiple_of((step - late) * size, size), size)
        grad_up_ref[...] = dot(normed[...], hidden[:, part], 0, 0).astype(BF16)

    @pl.when(step == pl.num_programs(0) - 1)
    def _():
        own_output.wait()
        for row in range(blocks):

            @pl.when(row != me)
            def _():
                output_copy(row).wait_send()
                to_partner(
                    staged.at[row], output.at[row], output_send.at[row], output_recv.at[row],
                    {"ctx": row},
                ).wait_recv()

        if fast:
            chunk.finish_second()
            for there, here in zip(carried, (r2a, r2b)):
                there[...] = here[...]
        else:
            pltpu.make_async_copy(grad_down, grad_down_out, local.at[3]).wait()


def feed_forward(
    fast, length, inputs, mixed, cotangent, out_weight, up_weight, down_weight, gain, shift
):
    blocks, block, width = inputs.shape
    rows, wide = blocks * block, up_weight.shape[1]
    size = 512
    late = 2 * blocks + 1
    steps = late + wide // size
    back_row = lambda step: jnp.clip(step - blocks - 1, 0, blocks - 1)
    up_part = lambda step: jnp.maximum(step - late, 0)
    operands = (inputs, mixed, out_weight)
    piece = wide // PIECES // 2
    lead = (2, 2, 2, 2)
    half = (2, 2, piece, width // 2)
    grad_down_shape = lead + (piece, width) if not fast else (8, LANES)
    carried = [whole(half)] * 2 if fast else []
    extra = []
    if fast:
        extra = [
            pltpu.SemaphoreType.DMA((KINDS,)),
            pltpu.SemaphoreType.DMA((KINDS,)),
            pltpu.VMEM((2, 2, 2, piece, width), BF16),
            pltpu.VMEM(half, BF16),
            pltpu.VMEM(half, BF16),
        ]
    return pl.pallas_call(
        functools.partial(feed_forward_kernel, fast, blocks),
        grid=(steps,),
        in_specs=[SMEM]
        + [whole(operand.shape) for operand in operands]
        + [VECTOR, VECTOR, ANY, ANY, ANY],
        out_specs=[
            ANY,
            ANY,
            pl.BlockSpec((block, width), lambda step: (back_row(step), 0)),
            pl.BlockSpec((block, width), lambda step: (back_row(step), 0)),
            pl.BlockSpec((width, size), lambda step: (0, up_part(step))),
            whole((width, width)),
            whole((8, width)),
        ]
        + carried,
        out_shape=[
            struct(inputs.shape),
            struct(grad_down_shape),
            struct((rows, width), F32),
            struct((rows, width)),
            struct((width, wide)),
            struct((width, width)),
            struct((8, width), F32),
        ]
        + [struct(half)] * len(carried),
        scratch_shapes=[
            pltpu.VMEM(up_weight.shape, BF16),
            pltpu.VMEM(down_weight.shape, BF16),
            pltpu.VMEM((rows, width), BF16),
            pltpu.VMEM((rows, width), BF16),
            pltpu.VMEM((rows, width), BF16),
            pltpu.VMEM((rows, wide), BF16),
            pltpu.VMEM((rows, wide), BF16),
            pltpu.VMEM((rows, width), F32),
            pltpu.VMEM((rows, 1), F32),
            pltpu.VMEM(inputs.shape, BF16),
            pltpu.VMEM(inputs.shape, BF16),
            pltpu.VMEM(lead + (piece, width), BF16),
            pltpu.SemaphoreType.DMA((blocks,)),
            pltpu.SemaphoreType.DMA((blocks,)),
            pltpu.SemaphoreType.DMA((5,)),
        ]
        + extra,
        compiler_params=pltpu.CompilerParams(
            vmem_limit_bytes=VMEM_LIMIT, collective_id=1, has_side_effects=True
        ),
        name="feed_forward",
    )(length, *operands, gain, shift, up_weight, down_weight, cotangent)


def chunk_scratch(rows, columns, number):
    shapes = [
        (2, 2, 2, rows, columns),
        (2, 2, rows, columns // 2),
        (2, 2, rows, columns // 2),
        (2, rows, columns),
        (rows, columns),
        (rows, columns),
        (2, rows, columns),
    ]
    if number == 0:
        shapes = shapes[3:]
    elif number < 3:
        shapes.insert(0, (2, 2, 2, rows, columns))
    return [pltpu.VMEM(shape, BF16) for shape in shapes]


PLAN = {
    (0, 0): [(0, 2), (1, 0), (2, 0)],
    (1, 0): [(1, 1)],
    (1, 1): [(0, 3)],
    (2, 0): [(0, 4), (3, 0)],
    (2, 3): [(1, 2), (2, 1), (3, 1)],
    (3, 2): [(2, 2), (3, 2)],
    (3, 3): [(1, 3), (2, 3)],
    (4, 0): [(0, 5), (4, 0), (3, 3)],
    (4, 2): [(1, 4), (2, 4), (4, 1)],
    (5, 0): [(3, 4), (4, 2)],
    (5, 2): [(2, 5), (4, 3)],
    (5, 3): [(3, 5), (4, 4)],
}
PLAN_BEFORE_NORM = [(1, 5), (4, 5)]
PLAN_AFTER_NORM = [
    (5, 0), "v0", (5, 1), "v1", (5, 2), "v2", (5, 3), "v3", (0, 6), (2, 6), (3, 6), (1, 6), (4, 6),
    (5, 4), "v4", (5, 5), "v5", (5, 6),
]


def back_kernel(
    fast, ctx, length_ref, q_ref, k_ref, v_ref, mixed_ref, grad_ref, log_ref, inputs_in, normed_in,
    middle_in, weight_in, gain, norm_two, *rest,
):
    rest = list(rest)
    take = lambda count: [rest.pop(0) for _ in range(count)]
    sources = take(4) if fast else []
    (grad_tokens,) = take(1)
    results = take(4) if fast else take(1)
    (vector_out,) = take(1)
    (inputs, normed, middle, weight, grad_normed, pair, partial, staged) = take(8)
    (k_t, grad_q_t, probs_low, grads_low, sum_k, sum_v) = take(6)
    (vectors, vectors_got, local, token_send, token_recv, v_send, v_recv) = take(7)
    step = pl.program_id(0)
    seq, me = lax.axis_index("seq"), lax.axis_index("ctx")
    rows, width = normed.shape
    blocks, block = staged.shape[0], staged.shape[1]
    groups = width // LANES
    chunks = []
    if fast:
        send, recv = take(2)
        places = (seq, me, seq % 2, (seq // 2) % 2, seq // 4, me % 2)
        for number in range(3 + PARTS):
            own, stages = None, [None] * 7
            if number == 0:
                stages[1:] = sources[:2] + take(4)
            elif number < 3:
                own, *stages = take(8)
            else:
                stages = take(7)
            source = sources[number + 1] if number < 3 else partial.at[number - 3]
            chunks.append(
                Chunk(
                    source, own, stages, send.at[number], recv.at[number], local.at[5 + number],
                    places, second=number == 0,
                )
            )

    def run(name):
        if not fast:
            return
        if isinstance(name, tuple):
            chunks[name[0]].event(name[1])
            return
        number = int(name[1:])
        partners = [{"seq": seq ^ 1}, {"seq": seq ^ 2}, {"seq": seq ^ 4}]
        partners += [{"ctx": me ^ 1}, {"ctx": me ^ 2}]
        exchange = lambda n: to_partner(
            vectors.at[n], vectors_got.at[n], v_send.at[n], v_recv.at[n], partners[n]
        )
        if number:
            exchange(number - 1).wait()
            vectors[number] = vectors[number - 1] + vectors_got[number - 1]
        if number < len(partners):
            exchange(number).start()

    loads = [
        pltpu.make_async_copy(inputs_in, inputs, local.at[0]),
        pltpu.make_async_copy(normed_in, normed, local.at[1]),
        pltpu.make_async_copy(middle_in, middle, local.at[2]),
        pltpu.make_async_copy(weight_in, weight, local.at[3]),
    ]

    @pl.when(step == 0)
    def _():
        partners = [{"ctx": me ^ offset} for offset in range(1, ctx)]
        if fast:
            partners += [{"seq": seq ^ 1}, {"seq": seq ^ 2}, {"seq": seq ^ 4}]
        greet(partners)
        for load in loads:
            load.start()

    def hook(i):
        for group in range(groups):
            if (group, i) in PLAN:

                @pl.when(step == group)
                def _():
                    for name in PLAN[group, i]:
                        run(name)

    @pl.when(step < groups)
    def _():
        side = pl.ds(pl.multiple_of((step % 2) * LANES, LANES), LANES)
        attend_backward(
            hook, side, length_ref[me], q_ref, k_ref, v_ref, mixed_ref, grad_ref, log_ref, pair,
            k_t, grad_q_t, probs_low, grads_low, sum_k, sum_v,
        )

    @pl.when(step == 1)
    def _():
        for load in loads:
            load.wait()
        grad_normed[...] = jnp.zeros_like(grad_normed)

    def weight_gradient(part):
        @pl.loop(0, PARTS)
        def _(name):
            columns = pl.ds(pl.multiple_of(name * 2 * LANES, 2 * LANES), 2 * LANES)
            product = dot(normed[...], pair[name], 0, 0).astype(BF16)
            if fast:
                product = product.reshape(2, 2, 2, 2, width // 16, 2 * LANES)
                partial[part, :, :, :, :, :, columns] = product
            else:
                partial[part, :, columns] = product

    @pl.when((step < groups) & (step % 2 == 1))
    def _():
        part = step // 2

        @pl.loop(0, PARTS)
        def _(name):
            there = pl.multiple_of(name * width + part * 2 * LANES, 2 * LANES)
            grad_normed[...] += dot(pair[name], weight[:, pl.ds(there, 2 * LANES)], 1, 1)

        @pl.when(step < groups - 1)
        def _():
            weight_gradient(part)

    def token_copy(row):
        return to_partner(
            staged.at[row], grad_tokens.at[me], token_send.at[row], token_recv.at[me], {"ctx": row}
        )

    own_tokens = pltpu.make_async_copy(staged.at[me], grad_tokens.at[me], local.at[4])

    @pl.when(step == groups)
    def _():
        for name in PLAN_BEFORE_NORM:
            run(name)
        gain_sum, shift_sum = 0.0, 0.0
        for row in range(blocks):
            there = slice(row * block, (row + 1) * block)
            hat, inverse = normalise(inputs[row].astype(F32))
            grad = grad_normed[there, :]
            gain_sum = gain_sum + jnp.sum(grad * hat, axis=0, keepdims=True)
            shift_sum = shift_sum + jnp.sum(grad, axis=0, keepdims=True)
            total = middle[there, :] + normalise_backward(grad, hat, inverse, row_of(gain))
            staged[row] = total.astype(BF16)

            @pl.when(row != me)
            def _():
                token_copy(row).start()

            @pl.when(row == me)
            def _():
                own_tokens.start()

        vectors[0] = jnp.concatenate([gain_sum, shift_sum, norm_two[0:6, :]], axis=0)
        weight_gradient(PARTS - 1)
        for name in PLAN_AFTER_NORM:
            run(name)
        if fast:
            for number in range(3):
                results[number][...] = chunks[number].out[...]
            for number in range(PARTS):
                results[3][number] = chunks[3 + number].out[...]
            vector_out[...] = vectors[5]
        else:
            results[0][...] = partial[...]
            vector_out[...] = vectors[0]
        own_tokens.wait()
        for row in range(blocks):

            @pl.when(row != me)
            def _():
                token_copy(row).wait_send()
                to_partner(
                    staged.at[row], grad_tokens.at[row], token_send.at[row], token_recv.at[row],
                    {"ctx": row},
                ).wait_recv()


def attend_backward(
    hook, side, length, q_ref, k_ref, v_ref, mixed_ref, grad_ref, log_ref, pair,
    k_t, grad_q_t, probs_low, grads_low, sum_k, sum_v,
):
    count = q_ref.shape[0] // BLOCK
    k_t[...] = k_ref[...].T

    def rows_of(i):
        rows = slice(i * BLOCK, (i + 1) * BLOCK)
        product = (grad_ref[rows, :].astype(F32) * mixed_ref[rows, :].astype(F32)).T
        queries = [only_head(q_ref[rows, :], head) for head in range(HEADS)]
        grads = [only_head(grad_ref[rows, :], head) for head in range(HEADS)]
        inner = [
            jnp.sum(product[head * HD : (head + 1) * HD], axis=0, keepdims=True)
            for head in range(HEADS)
        ]
        return (queries, grads, inner)

    prepared = [rows_of(i) for i in range(count)]

    def products_of(i, head):
        span = (i + 1) * BLOCK
        scores = dot(k_ref[0:span, :], prepared[i][0][head], 1, 1)
        return (scores, dot(v_ref[0:span, :], prepared[i][1][head], 1, 1))

    steps = [(i, head) for i in range(count) for head in range(HEADS)]
    current = products_of(*steps[0])
    for number, (i, head) in enumerate(steps):
        below = i * BLOCK
        span = below + BLOCK
        if head == 0:
            hook(i)
        following = products_of(*steps[number + 1]) if number + 1 < len(steps) else None
        scores, grad_probs = current
        scores = mask_diagonal(scores, BLOCK, below, length)
        probs = jnp.exp2(scores * SCALE_LOG2 - log_ref[0, head : head + 1, below:span])
        grad_scores = (probs * (grad_probs - prepared[i][2][head])).astype(BF16)
        columns = slice(head * BLOCK, (head + 1) * BLOCK)
        probs_low[0:span, columns] = probs.astype(BF16)
        grads_low[0:span, columns] = grad_scores
        grad_q_t[head * HD : (head + 1) * HD, :] = dot(
            k_t[head * HD : (head + 1) * HD, 0:span], grad_scores, 1, 0
        )
        if head == HEADS - 1:
            pair[0, below:span, side] = (grad_q_t[...].T * SCALE).astype(BF16)
            grad_v = dot(probs_low[0:span, :], jnp.concatenate(prepared[i][1], 0), 1, 0)
            grad_k = dot(grads_low[0:span, :], jnp.concatenate(prepared[i][0], 0), 1, 0)
            if below:
                sum_v[0:below, :] += grad_v[:below]
                sum_k[0:below, :] += grad_k[:below]
            sum_v[below:span, :] = grad_v[below:]
            sum_k[below:span, :] = grad_k[below:]
        current = following
    pair[1, :, side] = (sum_k[...] * SCALE).astype(BF16)
    pair[2, :, side] = sum_v[...].astype(BF16)


def back(
    fast, ctx, length, packed, mixed, grad_mixed, logs, inputs, normed, middle, weight, gain,
    norm_two, partials,
):
    rows, width = mixed.shape
    blocks, block, _ = inputs.shape
    groups = width // LANES
    group_of = lambda step: jnp.minimum(step, groups - 1)
    columns = lambda part: pl.BlockSpec(
        (rows, LANES), lambda step: (0, part * groups + group_of(step))
    )
    if fast:
        lead = (2, 2, 2, 2)
        carried, partials = partials[:2], partials[2:]
        partials = [
            grad.reshape(lead + (grad.shape[0] // 16, grad.shape[1])) for grad in partials
        ]
        sizes = [(carried[0].shape[2], width)] + [grad.shape[-2:] for grad in partials]
        sizes += [(width // 16, width)] * PARTS
        partials = carried + partials
        reduced = [(2,) + size for size in sizes[:3]] + [(PARTS, 2, width // 16, width)]
        held = [PARTS] + list(lead) + [width // 16, width]
        extra = [
            pltpu.SemaphoreType.DMA((len(sizes), KINDS)),
            pltpu.SemaphoreType.DMA((len(sizes), KINDS)),
        ]
        for number, size in enumerate(sizes):
            extra += chunk_scratch(*size, number)
    else:
        partials = []
        reduced = [(PARTS, width, width)]
        held = [PARTS, width, width]
        extra = []
    scratch = [
        pltpu.VMEM(inputs.shape, BF16),
        pltpu.VMEM((rows, width), BF16),
        pltpu.VMEM((rows, width), F32),
        pltpu.VMEM(weight.shape, BF16),
        pltpu.VMEM((rows, width), F32),
        pltpu.VMEM((PARTS, rows, 2 * LANES), BF16),
        pltpu.VMEM(tuple(held), BF16),
        pltpu.VMEM(inputs.shape, BF16),
        pltpu.VMEM((LANES, rows), BF16),
        pltpu.VMEM((LANES, BLOCK), F32),
        pltpu.VMEM((rows, HEADS * BLOCK), BF16),
        pltpu.VMEM((rows, HEADS * BLOCK), BF16),
        pltpu.VMEM((rows, LANES), F32),
        pltpu.VMEM((rows, LANES), F32),
        pltpu.VMEM((6, 8, width), F32),
        pltpu.VMEM((5, 8, width), F32),
        pltpu.SemaphoreType.DMA((5 + 3 + PARTS,)),
        pltpu.SemaphoreType.DMA((blocks,)),
        pltpu.SemaphoreType.DMA((blocks,)),
        pltpu.SemaphoreType.DMA((5,)),
        pltpu.SemaphoreType.DMA((5,)),
    ]
    return pl.pallas_call(
        functools.partial(back_kernel, fast, ctx),
        grid=(groups + 1,),
        in_specs=[
            SMEM, columns(0), columns(1), columns(2), columns(0), columns(0),
            pl.BlockSpec((1, HEADS, rows), lambda step: (group_of(step), 0, 0)),
            ANY, ANY, ANY, ANY, VECTOR, whole(norm_two.shape),
        ] + [whole(partial.shape) if number < 2 else ANY for number, partial in enumerate(partials)],
        out_specs=[ANY] + [whole(shape) for shape in reduced] + [whole((8, width))],
        out_shape=[struct(inputs.shape)]
        + [struct(shape) for shape in reduced]
        + [struct((8, width), F32)],
        scratch_shapes=scratch + extra,
        compiler_params=pltpu.CompilerParams(
            vmem_limit_bytes=VMEM_LIMIT, collective_id=2, has_side_effects=True
        ),
        name="back",
    )(
        length, packed, packed, packed, mixed, grad_mixed, logs, inputs, normed, middle, weight,
        gain, norm_two, *partials,
    )


def exchange(value, axis, size, bit):
    return lax.ppermute(value, axis, [(i, i ^ (1 << bit)) for i in range(size)])


def halve(value, axis, size, bit, dim):
    mine = (lax.axis_index(axis) >> bit) & 1
    kept = lax.dynamic_index_in_dim(value, mine, dim, keepdims=False)
    sent = lax.dynamic_index_in_dim(value, 1 - mine, dim, keepdims=False)
    got = exchange(sent, axis, size, bit)
    return (kept.astype(F32) + got.astype(F32)).astype(BF16)


def scatter_over_seq(value, size, order):
    bits = list(range(size.bit_length() - 1))
    value = value.reshape((2,) * len(bits) + value.shape[1:])
    left = bits[::-1]
    for bit in order:
        value = halve(value, "seq", size, bit, left.index(bit))
        left.remove(bit)
    return value


def sum_over_ctx(value, size):
    bits = list(range(size.bit_length() - 1))
    rows, columns = value.shape
    value = value.reshape((2,) * len(bits) + (rows // size, columns))
    left = bits[::-1]
    for bit in bits:
        value = halve(value, "ctx", size, bit, left.index(bit))
        left.remove(bit)
    for bit in bits[::-1]:
        got = exchange(value, "ctx", size, bit)
        low = ((lax.axis_index("ctx") >> bit) & 1) == 0
        value = jnp.stack([jnp.where(low, value, got), jnp.where(low, got, value)])
    value = value.transpose(tuple(bits[::-1]) + (len(bits), len(bits) + 1))
    return value.reshape(rows, columns)


def sum_weight(grad, seq_size, ctx_size):
    rows, columns = grad.shape
    blocks = grad.reshape(seq_size, rows // seq_size, columns)
    order = list(range(seq_size.bit_length() - 1))
    other = order[:1] + order[1:][::-1]
    half = columns // 2
    first = scatter_over_seq(blocks[:, :, :half], seq_size, order)
    second = scatter_over_seq(blocks[:, :, half:], seq_size, other)
    return sum_over_ctx(jnp.concatenate([first, second], axis=-1), ctx_size)


def unpair(parts, rows, width):
    parts = parts.reshape(PARTS, rows, 3, width // PARTS)
    return parts.transpose(1, 2, 0, 3).reshape(rows, 3 * width)


def finish_kernel(output, tokens, qkv, out, up, down, *results):
    *results, copies = results
    output_out, tokens_out, qkv_out, out_out, up_out, down_out = results[:6]
    moves = [
        pltpu.make_async_copy(output, output_out, copies.at[0]),
        pltpu.make_async_copy(tokens, tokens_out, copies.at[1]),
    ]
    for move in moves:
        move.start()
    for source, target in ((out, out_out), (up, up_out), (down, down_out)):
        rows = source.shape[1]
        for half in range(2):
            target[half * rows : (half + 1) * rows, :] = source[half].astype(F32)
    rows, width = qkv.shape[2:]
    step = width // 3
    for part in range(PARTS):
        for half in range(2):
            for name in range(3):
                first = name * width + part * step
                value = qkv[part, half, :, name * step : (name + 1) * step]
                qkv_out[half * rows : (half + 1) * rows, first : first + step] = value.astype(F32)
    for move in moves:
        move.wait()


def finish(output, tokens, qkv, out, up, down):
    flat = lambda part: struct((2 * part.shape[1], part.shape[2]), F32)
    memory = pl.BlockSpec(memory_space=pltpu.VMEM)
    return pl.pallas_call(
        finish_kernel,
        in_specs=[ANY, ANY] + [memory] * 4,
        out_specs=[ANY, ANY] + [memory] * 4,
        out_shape=[
            struct(output.shape),
            struct(tokens.shape),
            struct((2 * qkv.shape[2], 3 * qkv.shape[3]), F32),
            flat(out),
            flat(up),
            flat(down),
        ],
        scratch_shapes=[pltpu.SemaphoreType.DMA((2,))],
        compiler_params=pltpu.CompilerParams(vmem_limit_bytes=24 * MIB),
        name="finish",
    )(output, tokens, qkv, out, up, down)


def make_per_device(seq_size, ctx_size):
    fast = seq_size == 8 and ctx_size == 4

    def per_device(
        tokens,
        lengths,
        query_key_value_weight,
        attention_out_weight,
        up_weight,
        down_weight,
        ln1_gain,
        ln1_shift,
        ln2_gain,
        ln2_shift,
        cotangent,
    ):
        width = tokens.shape[-1]
        inputs, normed_low, packed, cotangent, mixed_low, logs = front(
            ctx_size, lengths, tokens, cotangent, query_key_value_weight, ln1_gain, ln1_shift
        )
        (
            output, grad_down, grad_middle, grad_mixed, grad_up, grad_out, grad_norm_two, *carried
        ) = feed_forward(
            fast, lengths, inputs, mixed_low, cotangent, attention_out_weight, up_weight,
            down_weight, ln2_gain, ln2_shift,
        )
        partials = carried + [grad_up, grad_out]
        grad_tokens, *sums, vectors = back(
            fast, ctx_size, lengths, packed, mixed_low, grad_mixed, logs, inputs, normed_low,
            grad_middle, query_key_value_weight, ln1_gain, grad_norm_two, partials,
        )
        share = width // seq_size
        if fast:
            down, up, out, qkv = sums
            output, grad_tokens, qkv, out, up, down = finish(
                output, grad_tokens, qkv, out, up, down
            )
        else:
            grad_qkv = unpair(sums[0], width, width)
            grad_down = grad_down.reshape(-1, width)
            down, up, out, qkv = [
                sum_weight(part, seq_size, ctx_size)
                for part in (grad_down, grad_up, grad_out, grad_qkv)
            ]
            vectors = lax.psum(vectors, ("seq", "ctx"))
        vectors = lax.dynamic_slice_in_dim(vectors, lax.axis_index("seq") * share, share, 1)
        return (
            output,
            grad_tokens,
            qkv.astype(F32),
            out.astype(F32),
            up.astype(F32),
            down.astype(F32),
            vectors[0],
            vectors[1],
            vectors[2],
            vectors[3],
        )

    return per_device


def solution(mesh):
    placed = (P("seq", "ctx", None), P("seq")) + (P(),) * 8 + (P("seq", "ctx", None),)
    weights = (P("seq", None),) * 4 + (P("seq"),) * 4
    return jax.shard_map(
        make_per_device(mesh.shape["seq"], mesh.shape["ctx"]),
        mesh=mesh,
        in_specs=placed,
        out_specs=(P("seq", "ctx", None),) * 2 + weights,
        check_vma=False,
    )
```

```python
import functools
import math

import jax
import jax.numpy as jnp
from jax import lax
from jax.experimental import pallas as pl
from jax.experimental.pallas import tpu as pltpu
from jax.sharding import PartitionSpec as P

HD = 32
LANES = 128
HEADS = LANES // HD
BLOCK = 256
SCALE = HD ** (-0.5)
SCALE_LOG2 = SCALE * math.log2(math.e)
BF16 = jnp.bfloat16
F32 = jnp.float32
MESH = pl.DeviceIdType.MESH
epsilon = 1e-05
MIB = 2**20
VMEM_LIMIT = 62 * MIB
ANY = pl.BlockSpec(memory_space=pl.ANY)
SMEM = pl.BlockSpec(memory_space=pltpu.SMEM)
ONE = pl.Buffered(1)
VECTOR = pl.BlockSpec(memory_space=pltpu.VMEM)


def dot(a, b, dim_a, dim_b):
    return lax.dot_general(
        a, b, (((dim_a,), (dim_b,)), ((), ())), preferred_element_type=F32
    )


def whole(shape):
    return pl.BlockSpec(shape, lambda step: (0,) * len(shape), pipeline_mode=ONE)


def row_of(vector):
    return vector[...].reshape(1, -1)


def struct(shape, kind=BF16):
    return jax.ShapeDtypeStruct(shape, kind)


def greet(partners):
    barrier = pltpu.get_barrier_semaphore()
    for partner in partners:
        pl.semaphore_signal(barrier, inc=1, device_id=partner, device_id_type=MESH)
    pl.semaphore_wait(barrier, len(partners))


def to_partner(source, target, send_sem, recv_sem, partner):
    return pltpu.make_async_remote_copy(
        src_ref=source,
        dst_ref=target,
        send_sem=send_sem,
        recv_sem=recv_sem,
        device_id=partner,
        device_id_type=MESH,
    )


def normalise(rows):
    centred = rows - jnp.mean(rows, axis=-1, keepdims=True)
    inverse = lax.rsqrt(jnp.mean(centred * centred, axis=-1, keepdims=True) + epsilon)
    return (centred * inverse, inverse)


def normalise_backward(grad, hat, inverse, gain):
    grad_hat = grad * gain
    along = jnp.mean(grad_hat * hat, axis=-1, keepdims=True)
    return inverse * (grad_hat - jnp.mean(grad_hat, axis=-1, keepdims=True) - hat * along)


def gelu_and_slope(value):
    cdf = 0.5 * lax.erf(value * math.sqrt(0.5)) + 0.5
    bell = jnp.exp2(value * value * (-0.5 * math.log2(math.e)))
    return (value * cdf, cdf + value * (bell * (1.0 / math.sqrt(2.0 * math.pi))))


def only_head(rows, head):
    lanes = lax.broadcasted_iota(jnp.int32, rows.shape, 1)
    return jnp.where(lanes // HD == head, rows, 0)


def mask_diagonal(scores, block, first, length):
    keys = first + lax.broadcasted_iota(jnp.int32, (block, block), 0)
    queries = first + lax.broadcasted_iota(jnp.int32, (block, block), 1)
    allowed = (keys <= queries) & (keys < length)
    below = scores.shape[0] - block
    diagonal = jnp.where(allowed, scores[below:], -1e30)
    return jnp.concatenate([scores[:below], diagonal], 0) if below else diagonal


def attend(group, length, packed, mixed_ref, log_ref, v_t, mixed_t):
    rows, width = packed.shape[0], packed.shape[1] // 3
    count = rows // BLOCK
    columns = [
        pl.ds(pl.multiple_of(part * width + group * LANES, LANES), LANES) for part in range(3)
    ]
    v_t[...] = packed[:, columns[2]].T

    def scores_of(i, head):
        span = (i + 1) * BLOCK
        query = only_head(packed[i * BLOCK : span, columns[0]], head)
        scores = dot(packed[0:span, columns[1]], query, 1, 1)
        return mask_diagonal(scores, BLOCK, i * BLOCK, length)

    steps = [(i, head) for i in range(count) for head in range(HEADS)]
    scores = scores_of(*steps[0])
    for number, (i, head) in enumerate(steps):
        span = (i + 1) * BLOCK
        following = scores_of(*steps[number + 1]) if number + 1 < len(steps) else None
        summit = jnp.max(scores, axis=0, keepdims=True)
        expo = jnp.exp2(scores * SCALE_LOG2 - summit * SCALE_LOG2)
        denom = jnp.sum(expo, axis=0, keepdims=True)
        part = dot(v_t[head * HD : (head + 1) * HD, 0:span], expo.astype(BF16), 1, 0)
        mixed_t[head * HD : (head + 1) * HD, :] = part / denom
        log_ref[0, head : head + 1, i * BLOCK : span] = summit * SCALE_LOG2 + jnp.log2(denom)
        if head == HEADS - 1:
            mixed_ref[i * BLOCK : span, :] = mixed_t[...].T.astype(BF16)
        scores = following


def front_kernel(
    ctx, length_ref, tokens, cotangent, weight, gain, shift,
    inputs_out, normed_out, packed_out, cotangent_out, mixed_ref, log_ref,
    inputs, normed, packed, v_t, mixed_t, send, recv, cot_send, cot_recv, local,
):
    step = pl.program_id(0)
    me = lax.axis_index("ctx")
    block = tokens.shape[1]
    offsets = [1] + list(range(2, ctx))

    def token_copy(offset):
        return to_partner(
            tokens.at[me ^ offset], inputs.at[me], send.at[offset], recv.at[offset],
            {"ctx": me ^ offset},
        )

    def cotangent_copy(offset):
        return to_partner(
            cotangent.at[me ^ offset], cotangent_out.at[me], cot_send.at[offset],
            cot_recv.at[offset], {"ctx": me ^ offset},
        )

    own_cotangent = pltpu.make_async_copy(cotangent.at[me], cotangent_out.at[me], local.at[1])
    keeps = [
        pltpu.make_async_copy(inputs, inputs_out, local.at[2]),
        pltpu.make_async_copy(normed, normed_out, local.at[3]),
        pltpu.make_async_copy(packed, packed_out, local.at[4]),
    ]

    @pl.when(step == 0)
    def _():
        own = pltpu.make_async_copy(tokens.at[me], inputs.at[me], local.at[0])
        own.start()
        greet([{"ctx": me ^ offset} for offset in offsets])
        for offset in offsets[::-1]:
            token_copy(offset).start()

        def project(source):
            hat, _ = normalise(inputs[source].astype(F32))
            low = (hat * row_of(gain) + row_of(shift)).astype(BF16)
            rows = pl.ds(pl.multiple_of(source * block, block), block)
            normed[rows, :] = low
            packed[rows, :] = dot(low, weight[...], 1, 0).astype(BF16)

        own.wait()
        project(me)
        for offset in offsets:
            token_copy(offset).wait_recv()
            if offset == offsets[-1]:
                for earlier in offsets:
                    token_copy(earlier).wait_send()
                own_cotangent.start()
                for later in offsets[::-1]:
                    cotangent_copy(later).start()
            project(me ^ offset)
        for keep in keeps:
            keep.start()

    @pl.when(step > 0)
    def _():
        attend(step - 1, length_ref[me], packed, mixed_ref, log_ref, v_t, mixed_t)

    @pl.when(step == pl.num_programs(0) - 1)
    def _():
        for keep in keeps:
            keep.wait()
        own_cotangent.wait()
        for offset in offsets:
            cotangent_copy(offset).wait()


def front(ctx, length, tokens, cotangent, weight, gain, shift):
    blocks, block, width = tokens.shape
    rows, groups = blocks * block, width // LANES
    group_of = lambda step: jnp.maximum(step - 1, 0)
    return pl.pallas_call(
        functools.partial(front_kernel, ctx),
        grid=(1 + groups,),
        in_specs=[SMEM, ANY, ANY, whole(weight.shape), VECTOR, VECTOR],
        out_specs=[
            ANY, ANY, ANY, ANY,
            pl.BlockSpec((rows, LANES), lambda step: (0, group_of(step))),
            pl.BlockSpec((1, HEADS, rows), lambda step: (group_of(step), 0, 0)),
        ],
        out_shape=[
            struct(tokens.shape),
            struct((rows, width)),
            struct((rows, 3 * width)),
            struct(tokens.shape),
            struct((rows, width)),
            struct((groups, HEADS, rows), F32),
        ],
        scratch_shapes=[
            pltpu.VMEM(tokens.shape, BF16),
            pltpu.VMEM((rows, width), BF16),
            pltpu.VMEM((rows, 3 * width), BF16),
            pltpu.VMEM((LANES, rows), BF16),
            pltpu.VMEM((LANES, BLOCK), F32),
            pltpu.SemaphoreType.DMA((ctx,)),
            pltpu.SemaphoreType.DMA((ctx,)),
            pltpu.SemaphoreType.DMA((ctx,)),
            pltpu.SemaphoreType.DMA((ctx,)),
            pltpu.SemaphoreType.DMA((5,)),
        ],
        compiler_params=pltpu.CompilerParams(
            vmem_limit_bytes=56 * MIB, collective_id=0, has_side_effects=True
        ),
        name="front",
    )(length, tokens, cotangent, weight, gain, shift)


PARTS = 3
KINDS = 8


class Chunk:
    def __init__(self, source, own, stages, send, recv, local, places, second=False):
        self.source, self.own, self.second = source, own, second
        self.r1, self.r2a, self.r2b, self.r3, self.z1, self.z2, self.out = stages
        self.send, self.recv, self.local, self.places = send, recv, local, places
        self.cut = self.r2a.shape[-1]

    def copy(self, kind):
        seq, ctx, core, x, y, low = self.places
        cut = self.cut
        ways = (
            lambda: (self.source.at[:, :, 1 - core], self.r1, {"seq": seq ^ 1}),
            lambda: (self.r1.at[:, 1 - x, :, :, 0:cut], self.r2a, {"seq": seq ^ 2}),
            lambda: (self.r1.at[1 - y, :, :, :, cut:], self.r2b, {"seq": seq ^ 4}),
            lambda: (self.r2a.at[1 - y], self.r3.at[:, :, 0:cut], {"seq": seq ^ 4}),
            lambda: (self.r2b.at[1 - x], self.r3.at[:, :, cut:], {"seq": seq ^ 2}),
            lambda: (self.r3.at[1 - low], self.z1, {"ctx": ctx ^ 1}),
            lambda: (self.z1, self.z2, {"ctx": ctx ^ 2}),
            lambda: (self.out.at[low], self.out.at[low], {"ctx": ctx ^ 1}),
        )
        source, target, partner = ways[kind]()
        return to_partner(source, target, self.send.at[kind], self.recv.at[kind], partner)

    def own_copy(self):
        core = self.places[2]
        return pltpu.make_async_copy(self.source.at[:, :, core], self.own, self.local)

    def add_second(self):
        _, _, _, x, y, _ = self.places
        cut = self.cut
        self.copy(1).wait_recv()
        self.copy(2).wait_recv()
        for other in range(2):
            self.r2a[other] += self.r1[other, x, :, :, 0:cut]
            self.r2b[other] += self.r1[y, other, :, :, cut:]

    def finish_second(self):
        self.add_second()
        for kind in range(3):
            self.copy(kind).wait_send()

    def event(self, number):
        seq, ctx, core, x, y, low = self.places
        cut = self.cut
        if number == 0:
            self.copy(0).start()
            if self.own is not None:
                self.own_copy().start()
        if number == 1:
            self.copy(0).wait_recv()
            if self.own is not None:
                self.own_copy().wait()
            for along_y in range(2):
                for along_x in range(2):
                    if self.own is not None:
                        kept = self.own[along_y, along_x]
                    else:
                        kept = self.source[along_y, along_x, core]
                    self.r1[along_y, along_x] += kept
            self.copy(1).start()
            self.copy(2).start()
        if number == 2:
            if not self.second:
                self.add_second()
            self.copy(3).start()
            self.copy(4).start()
        if number == 3:
            self.copy(3).wait_recv()
            self.copy(4).wait_recv()
            self.r3[:, :, 0:cut] += self.r2a[y]
            self.r3[:, :, cut:] += self.r2b[x]
            self.copy(5).start()
        if number == 4:
            self.copy(5).wait_recv()
            self.z1[...] += self.r3[low]
            self.copy(6).start()
        if number == 5:
            self.copy(6).wait_recv()
            self.out[low] = self.z1[...] + self.z2[...]
            self.copy(7).start()
        if number == 6:
            to_partner(
                self.out.at[1 - low], self.out.at[1 - low], self.send.at[7], self.recv.at[7],
                {"ctx": ctx ^ 1},
            ).wait_recv()
            for kind in range(3 if self.second else 0, KINDS):
                self.copy(kind).wait_send()


CUT = 512
PIECES = 8


def feed_forward_kernel(
    fast, blocks, length_ref, inputs, mixed, out_weight, gain, shift, up_in, down_in,
    cotangent_in,
    output, grad_down_out, grad_middle_ref, grad_mixed_ref, grad_up_ref, grad_out_ref,
    grad_norm_ref, *rest,
):
    rest = list(rest)
    take = lambda count: [rest.pop(0) for _ in range(count)]
    carried = take(2) if fast else []
    (up_weight, down_weight, normed, upstream, branch, active, hidden, scaled, inverse_of) = take(9)
    (staged, cotangent, grad_down, output_send, output_recv, local) = take(6)
    step = pl.program_id(0)
    seq, me = lax.axis_index("seq"), lax.axis_index("ctx")
    block, width = staged.shape[1:]
    wide = active.shape[1]
    cuts = wide // CUT
    backward = blocks + 1
    late = backward + blocks
    chunk = None
    if fast:
        send, recv, r1, r2a, r2b = take(5)
        places = (seq, me, seq % 2, (seq // 2) % 2, seq // 4, me % 2)
        chunk = Chunk(
            grad_down, None, (r1, r2a, r2b, None, None, None, None), send, recv, None, places
        )

    def output_copy(row):
        return to_partner(
            staged.at[row], output.at[me], output_send.at[row], output_recv.at[me], {"ctx": row}
        )

    own_output = pltpu.make_async_copy(staged.at[me], output.at[me], local.at[0])
    cotangent_load = pltpu.make_async_copy(cotangent_in, cotangent, local.at[4])
    up_load = pltpu.make_async_copy(up_in, up_weight, local.at[1])
    down_load = pltpu.make_async_copy(down_in, down_weight, local.at[2])

    @pl.when(step == 0)
    def _():
        up_load.start()
        down_load.start()
        partners = [{"ctx": me ^ offset} for offset in range(1, blocks)]
        if fast:
            partners += [{"seq": seq ^ 1}, {"seq": seq ^ 2}, {"seq": seq ^ 4}]
        greet(partners)
        cotangent_load.start()
        grad_norm_ref[...] = jnp.zeros_like(grad_norm_ref)

    def rows_of(number):
        return pl.ds(pl.multiple_of(number * block, block), block)

    def valid_rows(number):
        places = number * block + lax.broadcasted_iota(jnp.int32, (block, 1), 0)
        return places < length_ref[me]

    @pl.when(step < blocks)
    def _():
        row = me ^ ((step + blocks // 2) % blocks)
        rows = rows_of(row)
        middle = inputs[row].astype(F32) + dot(mixed[rows, :], out_weight[...], 1, 0)
        hat, inverse = normalise(middle)
        scaled[rows, :] = hat
        inverse_of[rows, :] = inverse
        low = (hat * row_of(gain) + row_of(shift)).astype(BF16)
        normed[rows, :] = low

        @pl.when(step == 0)
        def _():
            up_load.wait()
            down_load.wait()

        product_of = lambda cut: dot(low, up_weight[:, cut * CUT : (cut + 1) * CUT], 1, 0)
        current = product_of(0)
        total = middle
        for cut in range(cuts):
            part = slice(cut * CUT, (cut + 1) * CUT)
            following = product_of(cut + 1) if cut + 1 < cuts else None
            value, slope = gelu_and_slope(current)
            value = value.astype(BF16)
            active[rows, part] = value
            hidden[rows, part] = slope.astype(BF16)
            total = total + dot(value, down_weight[part, :], 1, 0)
            current = following
        staged[row] = jnp.where(valid_rows(row), total, 0.0).astype(BF16)

        @pl.when(row != me)
        def _():
            output_copy(row).start()

        @pl.when(row == me)
        def _():
            own_output.start()

    @pl.when(step == blocks)
    def _():
        cotangent_load.wait()
        for row in range(blocks):
            kept = jnp.where(valid_rows(row), cotangent[row], 0)
            upstream[row * block : (row + 1) * block, :] = kept
        size = wide // PIECES

        @pl.loop(0, PIECES)
        def _(piece):
            columns = pl.ds(pl.multiple_of(piece * size, LANES), size)
            product = dot(active[:, columns], upstream[...], 0, 0)
            product = product.astype(BF16).reshape(2, size // 2, width)
            grad_down[piece // 4, (piece // 2) % 2, piece % 2] = product

        if fast:
            chunk.event(0)
        else:
            pltpu.make_async_copy(grad_down, grad_down_out, local.at[3]).start()

    @pl.when((step >= backward) & (step < late))
    def _():
        number = step - backward
        rows = rows_of(number)
        upstream_low = upstream[rows, :]

        @pl.when(number == 2)
        def _():
            if fast:
                chunk.event(1)

        product_of = lambda cut: dot(
            upstream_low, down_weight[cut * CUT : (cut + 1) * CUT, :], 1, 1
        )
        current = product_of(0)
        grad_normed = 0.0
        for cut in range(cuts):
            part = slice(cut * CUT, (cut + 1) * CUT)
            following = product_of(cut + 1) if cut + 1 < cuts else None
            grad_hidden = (hidden[rows, part].astype(F32) * current).astype(BF16)
            hidden[rows, part] = grad_hidden
            grad_normed = grad_normed + dot(grad_hidden, up_weight[:, part], 1, 1)
            current = following
        hat = scaled[rows, :]
        grad_norm_ref[0:1, :] += jnp.sum(grad_normed * hat, axis=0, keepdims=True)
        grad_norm_ref[1:2, :] += jnp.sum(grad_normed, axis=0, keepdims=True)
        through = normalise_backward(grad_normed, hat, inverse_of[rows, :], row_of(gain))
        grad_middle = upstream_low.astype(F32) + through
        grad_middle_ref[...] = grad_middle
        grad_branch = grad_middle.astype(BF16)
        branch[rows, :] = grad_branch
        grad_mixed_ref[...] = dot(grad_branch, out_weight[...], 1, 1).astype(BF16)

    @pl.when(step == late)
    def _():
        grad_out_ref[...] = dot(mixed[...], branch[...], 0, 0).astype(BF16)

    @pl.when(step >= late)
    def _():
        size = grad_up_ref.shape[1]
        part = pl.ds(pl.multiple_of((step - late) * size, size), size)
        grad_up_ref[...] = dot(normed[...], hidden[:, part], 0, 0).astype(BF16)

    @pl.when(step == pl.num_programs(0) - 1)
    def _():
        own_output.wait()
        for row in range(blocks):

            @pl.when(row != me)
            def _():
                output_copy(row).wait_send()
                to_partner(
                    staged.at[row], output.at[row], output_send.at[row], output_recv.at[row],
                    {"ctx": row},
                ).wait_recv()

        if fast:
            chunk.finish_second()
            for there, here in zip(carried, (r2a, r2b)):
                there[...] = here[...]
        else:
            pltpu.make_async_copy(grad_down, grad_down_out, local.at[3]).wait()


def feed_forward(
    fast, length, inputs, mixed, cotangent, out_weight, up_weight, down_weight, gain, shift
):
    blocks, block, width = inputs.shape
    rows, wide = blocks * block, up_weight.shape[1]
    size = 512
    late = 2 * blocks + 1
    steps = late + wide // size
    back_row = lambda step: jnp.clip(step - blocks - 1, 0, blocks - 1)
    up_part = lambda step: jnp.maximum(step - late, 0)
    operands = (inputs, mixed, out_weight)
    piece = wide // PIECES // 2
    lead = (2, 2, 2, 2)
    half = (2, 2, piece, width // 2)
    grad_down_shape = lead + (piece, width) if not fast else (8, LANES)
    carried = [whole(half)] * 2 if fast else []
    extra = []
    if fast:
        extra = [
            pltpu.SemaphoreType.DMA((KINDS,)),
            pltpu.SemaphoreType.DMA((KINDS,)),
            pltpu.VMEM((2, 2, 2, piece, width), BF16),
            pltpu.VMEM(half, BF16),
            pltpu.VMEM(half, BF16),
        ]
    return pl.pallas_call(
        functools.partial(feed_forward_kernel, fast, blocks),
        grid=(steps,),
        in_specs=[SMEM]
        + [whole(operand.shape) for operand in operands]
        + [VECTOR, VECTOR, ANY, ANY, ANY],
        out_specs=[
            ANY,
            ANY,
            pl.BlockSpec((block, width), lambda step: (back_row(step), 0)),
            pl.BlockSpec((block, width), lambda step: (back_row(step), 0)),
            pl.BlockSpec((width, size), lambda step: (0, up_part(step))),
            whole((width, width)),
            whole((8, width)),
        ]
        + carried,
        out_shape=[
            struct(inputs.shape),
            struct(grad_down_shape),
            struct((rows, width), F32),
            struct((rows, width)),
            struct((width, wide)),
            struct((width, width)),
            struct((8, width), F32),
        ]
        + [struct(half)] * len(carried),
        scratch_shapes=[
            pltpu.VMEM(up_weight.shape, BF16),
            pltpu.VMEM(down_weight.shape, BF16),
            pltpu.VMEM((rows, width), BF16),
            pltpu.VMEM((rows, width), BF16),
            pltpu.VMEM((rows, width), BF16),
            pltpu.VMEM((rows, wide), BF16),
            pltpu.VMEM((rows, wide), BF16),
            pltpu.VMEM((rows, width), F32),
            pltpu.VMEM((rows, 1), F32),
            pltpu.VMEM(inputs.shape, BF16),
            pltpu.VMEM(inputs.shape, BF16),
            pltpu.VMEM(lead + (piece, width), BF16),
            pltpu.SemaphoreType.DMA((blocks,)),
            pltpu.SemaphoreType.DMA((blocks,)),
            pltpu.SemaphoreType.DMA((5,)),
        ]
        + extra,
        compiler_params=pltpu.CompilerParams(
            vmem_limit_bytes=VMEM_LIMIT, collective_id=1, has_side_effects=True
        ),
        name="feed_forward",
    )(length, *operands, gain, shift, up_weight, down_weight, cotangent)


def chunk_scratch(rows, columns, number):
    shapes = [
        (2, 2, 2, rows, columns),
        (2, 2, rows, columns // 2),
        (2, 2, rows, columns // 2),
        (2, rows, columns),
        (rows, columns),
        (rows, columns),
        (2, rows, columns),
    ]
    if number == 0:
        shapes = shapes[3:]
    elif number < 3:
        shapes.insert(0, (2, 2, 2, rows, columns))
    return [pltpu.VMEM(shape, BF16) for shape in shapes]


PLAN = {
    (0, "start"): [(2, 0), (1, 0), (0, 2)],
    (1, "start"): [(2, 1), (1, 1), (0, 3)],
    (1, "end"): [(2, 2)],
    (2, "start"): [(0, 4), (3, 0)],
    (3, "start"): [(1, 2), (2, 3)],
    (3, "end"): [(2, 4), (3, 1), (1, 3)],
    (4, "start"): [(0, 5)],
    (5, "start"): [(3, 2), (4, 0), (1, 4)],
}
PLAN_BEFORE_NORM = [(3, 3)]
PLAN_AFTER_NORM = ["t0", "v0", "v1", "t1"]
PLAN_LAST = [
    (5, 0), (4, 1), (5, 1), "v2", (3, 4), (5, 2), (5, 3), (1, 5), (2, 5), "v3", (4, 2), "t2",
    (2, 6), (4, 3), (3, 5), (0, 6), (5, 4), "v4", (4, 4), "t3", (1, 6), (5, 5), "v5", (3, 6),
    (4, 5), (5, 6), (4, 6),
]
TOKEN_PIECES = 4


def back_kernel(
    fast, ctx, length_ref, q_ref, k_ref, v_ref, mixed_ref, grad_ref, log_ref, inputs_in, normed_in,
    middle_in, weight_in, gain, norm_two, *rest,
):
    rest = list(rest)
    take = lambda count: [rest.pop(0) for _ in range(count)]
    sources = take(4) if fast else []
    (grad_tokens,) = take(1)
    results = take(4) if fast else take(1)
    (vector_out,) = take(1)
    (inputs, normed, middle, weight, grad_normed, pair, partial, staged) = take(8)
    (k_t, grad_q_t, probs_low, grads_low, sum_k, sum_v) = take(6)
    (vectors, vectors_got, local, token_send, token_recv, v_send, v_recv) = take(7)
    step = pl.program_id(0)
    seq, me = lax.axis_index("seq"), lax.axis_index("ctx")
    rows, width = normed.shape
    blocks, block = staged.shape[0], staged.shape[1]
    groups = width // LANES
    chunks = []
    if fast:
        send, recv = take(2)
        places = (seq, me, seq % 2, (seq // 2) % 2, seq // 4, me % 2)
        for number in range(3 + PARTS):
            own, stages = None, [None] * 7
            if number == 0:
                stages[1:] = sources[:2] + take(4)
            elif number < 3:
                own, *stages = take(8)
            else:
                stages = take(7)
            source = sources[number + 1] if number < 3 else partial.at[number - 3]
            chunks.append(
                Chunk(
                    source, own, stages, send.at[number], recv.at[number], local.at[5 + number],
                    places, second=number == 0,
                )
            )

    def token_copy(row, piece, slot):
        size = block // TOKEN_PIECES
        rows_there = slice(piece * size, (piece + 1) * size)
        return to_partner(
            staged.at[row, rows_there], grad_tokens.at[slot, rows_there],
            token_send.at[row, piece], token_recv.at[slot, piece], {"ctx": row},
        )

    def run(name):
        if name[0] == "t":
            for row in range(blocks):

                @pl.when(row != me)
                def _():
                    token_copy(row, int(name[1:]), me).start()

            return
        if not fast:
            return
        if isinstance(name, tuple):
            chunks[name[0]].event(name[1])
            return
        number = int(name[1:])
        partners = [{"seq": seq ^ 1}, {"seq": seq ^ 2}, {"seq": seq ^ 4}]
        partners += [{"ctx": me ^ 1}, {"ctx": me ^ 2}]
        exchange = lambda n: to_partner(
            vectors.at[n], vectors_got.at[n], v_send.at[n], v_recv.at[n], partners[n]
        )
        if number:
            exchange(number - 1).wait()
            vectors[number] = vectors[number - 1] + vectors_got[number - 1]
        if number < len(partners):
            exchange(number).start()

    loads = [
        pltpu.make_async_copy(inputs_in, inputs, local.at[0]),
        pltpu.make_async_copy(normed_in, normed, local.at[1]),
        pltpu.make_async_copy(middle_in, middle, local.at[2]),
        pltpu.make_async_copy(weight_in, weight, local.at[3]),
    ]

    @pl.when(step == 0)
    def _():
        partners = [{"ctx": me ^ offset} for offset in range(1, ctx)]
        if fast:
            partners += [{"seq": seq ^ 1}, {"seq": seq ^ 2}, {"seq": seq ^ 4}]
        greet(partners)
        for load in loads:
            load.start()

    def hook(place):
        for group in range(groups):
            if (group, place) in PLAN:

                @pl.when(step == group)
                def _():
                    for name in PLAN[group, place]:
                        run(name)

    hook("start")

    @pl.when(step < groups)
    def _():
        side = pl.ds(pl.multiple_of((step % 2) * LANES, LANES), LANES)
        attend_backward(
            side, length_ref[me], q_ref, k_ref, v_ref, mixed_ref, grad_ref, log_ref, pair,
            k_t, grad_q_t, probs_low, grads_low, sum_k, sum_v,
        )

    hook("end")

    @pl.when(step == 1)
    def _():
        for load in loads:
            load.wait()
        grad_normed[...] = jnp.zeros_like(grad_normed)

    def weight_gradient(part):
        @pl.loop(0, PARTS)
        def _(name):
            columns = pl.ds(pl.multiple_of(name * 2 * LANES, 2 * LANES), 2 * LANES)
            product = dot(normed[...], pair[name], 0, 0).astype(BF16)
            if fast:
                product = product.reshape(2, 2, 2, 2, width // 16, 2 * LANES)
                partial[part, :, :, :, :, :, columns] = product
            else:
                partial[part, :, columns] = product

    @pl.when((step < groups) & (step % 2 == 1))
    def _():
        part = step // 2

        @pl.loop(0, PARTS)
        def _(name):
            there = pl.multiple_of(name * width + part * 2 * LANES, 2 * LANES)
            grad_normed[...] += dot(pair[name], weight[:, pl.ds(there, 2 * LANES)], 1, 1)

        @pl.when(step < groups - 1)
        def _():
            weight_gradient(part)

    own_tokens = pltpu.make_async_copy(staged.at[me], grad_tokens.at[me], local.at[4])

    @pl.when(step == groups)
    def _():
        for name in PLAN_BEFORE_NORM:
            run(name)
        gain_sum, shift_sum = 0.0, 0.0
        for row in range(blocks):
            there = slice(row * block, (row + 1) * block)
            hat, inverse = normalise(inputs[row].astype(F32))
            grad = grad_normed[there, :]
            gain_sum = gain_sum + jnp.sum(grad * hat, axis=0, keepdims=True)
            shift_sum = shift_sum + jnp.sum(grad, axis=0, keepdims=True)
            total = middle[there, :] + normalise_backward(grad, hat, inverse, row_of(gain))
            staged[row] = total.astype(BF16)

        own_tokens.start()
        vectors[0] = jnp.concatenate([gain_sum, shift_sum, norm_two[0:6, :]], axis=0)
        for name in PLAN_AFTER_NORM:
            run(name)
        weight_gradient(PARTS - 1)
        for name in PLAN_LAST:
            run(name)
        if fast:
            for number in range(3):
                results[number][...] = chunks[number].out[...]
            for number in range(PARTS):
                results[3][number] = chunks[3 + number].out[...]
            vector_out[...] = vectors[5]
        else:
            results[0][...] = partial[...]
            vector_out[...] = vectors[0]
        own_tokens.wait()
        for row in range(blocks):

            @pl.when(row != me)
            def _():
                for piece in range(TOKEN_PIECES):
                    token_copy(row, piece, me).wait_send()
                    token_copy(row, piece, row).wait_recv()


def attend_backward(
    side, length, q_ref, k_ref, v_ref, mixed_ref, grad_ref, log_ref, pair,
    k_t, grad_q_t, probs_low, grads_low, sum_k, sum_v,
):
    count = q_ref.shape[0] // BLOCK
    k_t[...] = k_ref[...].T

    def rows_of(i):
        rows = slice(i * BLOCK, (i + 1) * BLOCK)
        product = (grad_ref[rows, :].astype(F32) * mixed_ref[rows, :].astype(F32)).T
        queries = [only_head(q_ref[rows, :], head) for head in range(HEADS)]
        grads = [only_head(grad_ref[rows, :], head) for head in range(HEADS)]
        inner = [
            jnp.sum(product[head * HD : (head + 1) * HD], axis=0, keepdims=True)
            for head in range(HEADS)
        ]
        return (queries, grads, inner)

    prepared = [rows_of(i) for i in range(count)]

    def products_of(i, head):
        span = (i + 1) * BLOCK
        scores = dot(k_ref[0:span, :], prepared[i][0][head], 1, 1)
        return (scores, dot(v_ref[0:span, :], prepared[i][1][head], 1, 1))

    steps = [(i, head) for i in range(count) for head in range(HEADS)]
    current = products_of(*steps[0])
    for number, (i, head) in enumerate(steps):
        below = i * BLOCK
        span = below + BLOCK
        following = products_of(*steps[number + 1]) if number + 1 < len(steps) else None
        scores, grad_probs = current
        scores = mask_diagonal(scores, BLOCK, below, length)
        probs = jnp.exp2(scores * SCALE_LOG2 - log_ref[0, head : head + 1, below:span])
        grad_scores = (probs * (grad_probs - prepared[i][2][head])).astype(BF16)
        columns = slice(head * BLOCK, (head + 1) * BLOCK)
        probs_low[0:span, columns] = probs.astype(BF16)
        grads_low[0:span, columns] = grad_scores
        grad_q_t[head * HD : (head + 1) * HD, :] = dot(
            k_t[head * HD : (head + 1) * HD, 0:span], grad_scores, 1, 0
        )
        if head == HEADS - 1:
            pair[0, below:span, side] = (grad_q_t[...].T * SCALE).astype(BF16)
            grad_v = dot(probs_low[0:span, :], jnp.concatenate(prepared[i][1], 0), 1, 0)
            grad_k = dot(grads_low[0:span, :], jnp.concatenate(prepared[i][0], 0), 1, 0)
            if below:
                sum_v[0:below, :] += grad_v[:below]
                sum_k[0:below, :] += grad_k[:below]
            sum_v[below:span, :] = grad_v[below:]
            sum_k[below:span, :] = grad_k[below:]
        current = following
    pair[1, :, side] = (sum_k[...] * SCALE).astype(BF16)
    pair[2, :, side] = sum_v[...].astype(BF16)


def back(
    fast, ctx, length, packed, mixed, grad_mixed, logs, inputs, normed, middle, weight, gain,
    norm_two, partials,
):
    rows, width = mixed.shape
    blocks, block, _ = inputs.shape
    groups = width // LANES
    group_of = lambda step: jnp.minimum(step, groups - 1)
    columns = lambda part: pl.BlockSpec(
        (rows, LANES), lambda step: (0, part * groups + group_of(step))
    )
    if fast:
        lead = (2, 2, 2, 2)
        carried, partials = partials[:2], partials[2:]
        partials = [
            grad.reshape(lead + (grad.shape[0] // 16, grad.shape[1])) for grad in partials
        ]
        sizes = [(carried[0].shape[2], width)] + [grad.shape[-2:] for grad in partials]
        sizes += [(width // 16, width)] * PARTS
        partials = carried + partials
        reduced = [(2,) + size for size in sizes[:3]] + [(PARTS, 2, width // 16, width)]
        held = [PARTS] + list(lead) + [width // 16, width]
        extra = [
            pltpu.SemaphoreType.DMA((len(sizes), KINDS)),
            pltpu.SemaphoreType.DMA((len(sizes), KINDS)),
        ]
        for number, size in enumerate(sizes):
            extra += chunk_scratch(*size, number)
    else:
        partials = []
        reduced = [(PARTS, width, width)]
        held = [PARTS, width, width]
        extra = []
    scratch = [
        pltpu.VMEM(inputs.shape, BF16),
        pltpu.VMEM((rows, width), BF16),
        pltpu.VMEM((rows, width), F32),
        pltpu.VMEM(weight.shape, BF16),
        pltpu.VMEM((rows, width), F32),
        pltpu.VMEM((PARTS, rows, 2 * LANES), BF16),
        pltpu.VMEM(tuple(held), BF16),
        pltpu.VMEM(inputs.shape, BF16),
        pltpu.VMEM((LANES, rows), BF16),
        pltpu.VMEM((LANES, BLOCK), F32),
        pltpu.VMEM((rows, HEADS * BLOCK), BF16),
        pltpu.VMEM((rows, HEADS * BLOCK), BF16),
        pltpu.VMEM((rows, LANES), F32),
        pltpu.VMEM((rows, LANES), F32),
        pltpu.VMEM((6, 8, width), F32),
        pltpu.VMEM((5, 8, width), F32),
        pltpu.SemaphoreType.DMA((5 + 3 + PARTS,)),
        pltpu.SemaphoreType.DMA((blocks, TOKEN_PIECES)),
        pltpu.SemaphoreType.DMA((blocks, TOKEN_PIECES)),
        pltpu.SemaphoreType.DMA((5,)),
        pltpu.SemaphoreType.DMA((5,)),
    ]
    return pl.pallas_call(
        functools.partial(back_kernel, fast, ctx),
        grid=(groups + 1,),
        in_specs=[
            SMEM, columns(0), columns(1), columns(2), columns(0), columns(0),
            pl.BlockSpec((1, HEADS, rows), lambda step: (group_of(step), 0, 0)),
            ANY, ANY, ANY, ANY, VECTOR, whole(norm_two.shape),
        ] + [whole(partial.shape) if number < 2 else ANY for number, partial in enumerate(partials)],
        out_specs=[ANY] + [whole(shape) for shape in reduced] + [whole((8, width))],
        out_shape=[struct(inputs.shape)]
        + [struct(shape) for shape in reduced]
        + [struct((8, width), F32)],
        scratch_shapes=scratch + extra,
        compiler_params=pltpu.CompilerParams(
            vmem_limit_bytes=VMEM_LIMIT, collective_id=2, has_side_effects=True
        ),
        name="back",
    )(
        length, packed, packed, packed, mixed, grad_mixed, logs, inputs, normed, middle, weight,
        gain, norm_two, *partials,
    )


def exchange(value, axis, size, bit):
    return lax.ppermute(value, axis, [(i, i ^ (1 << bit)) for i in range(size)])


def halve(value, axis, size, bit, dim):
    mine = (lax.axis_index(axis) >> bit) & 1
    kept = lax.dynamic_index_in_dim(value, mine, dim, keepdims=False)
    sent = lax.dynamic_index_in_dim(value, 1 - mine, dim, keepdims=False)
    got = exchange(sent, axis, size, bit)
    return (kept.astype(F32) + got.astype(F32)).astype(BF16)


def scatter_over_seq(value, size, order):
    bits = list(range(size.bit_length() - 1))
    value = value.reshape((2,) * len(bits) + value.shape[1:])
    left = bits[::-1]
    for bit in order:
        value = halve(value, "seq", size, bit, left.index(bit))
        left.remove(bit)
    return value


def sum_over_ctx(value, size):
    bits = list(range(size.bit_length() - 1))
    rows, columns = value.shape
    value = value.reshape((2,) * len(bits) + (rows // size, columns))
    left = bits[::-1]
    for bit in bits:
        value = halve(value, "ctx", size, bit, left.index(bit))
        left.remove(bit)
    for bit in bits[::-1]:
        got = exchange(value, "ctx", size, bit)
        low = ((lax.axis_index("ctx") >> bit) & 1) == 0
        value = jnp.stack([jnp.where(low, value, got), jnp.where(low, got, value)])
    value = value.transpose(tuple(bits[::-1]) + (len(bits), len(bits) + 1))
    return value.reshape(rows, columns)


def sum_weight(grad, seq_size, ctx_size):
    rows, columns = grad.shape
    blocks = grad.reshape(seq_size, rows // seq_size, columns)
    order = list(range(seq_size.bit_length() - 1))
    other = order[:1] + order[1:][::-1]
    half = columns // 2
    first = scatter_over_seq(blocks[:, :, :half], seq_size, order)
    second = scatter_over_seq(blocks[:, :, half:], seq_size, other)
    return sum_over_ctx(jnp.concatenate([first, second], axis=-1), ctx_size)


def unpair(parts, rows, width):
    parts = parts.reshape(PARTS, rows, 3, width // PARTS)
    return parts.transpose(1, 2, 0, 3).reshape(rows, 3 * width)


def finish_kernel(output, tokens, qkv, out, up, down, *results):
    output_out, tokens_out, qkv_out, out_out, up_out, down_out, *held, copies = results
    sources = (output, tokens, qkv, out, up, down)
    loads = [
        pltpu.make_async_copy(source, target, copies.at[number])
        for number, (source, target) in enumerate(zip(sources, held))
    ]
    for load in loads:
        load.start()
    for load in loads:
        load.wait()
    moves = [
        pltpu.make_async_copy(held[0], output_out, copies.at[0]),
        pltpu.make_async_copy(held[1], tokens_out, copies.at[1]),
    ]
    for move in moves:
        move.start()
    qkv, out, up, down = held[2:]
    for source, target in ((out, out_out), (up, up_out), (down, down_out)):
        rows = source.shape[1]
        for half in range(2):
            target[half * rows : (half + 1) * rows, :] = source[half].astype(F32)
    rows, width = qkv.shape[2:]
    step = width // 3
    for part in range(PARTS):
        for half in range(2):
            for name in range(3):
                first = name * width + part * step
                value = qkv[part, half, :, name * step : (name + 1) * step]
                qkv_out[half * rows : (half + 1) * rows, first : first + step] = value.astype(F32)
    for move in moves:
        move.wait()


def finish(output, tokens, qkv, out, up, down):
    flat = lambda part: struct((2 * part.shape[1], part.shape[2]), F32)
    memory = pl.BlockSpec(memory_space=pltpu.VMEM)
    held = pl.BlockSpec(memory_space=pltpu.HBM)
    return pl.pallas_call(
        finish_kernel,
        in_specs=[held] * 6,
        out_specs=[held, held] + [memory] * 4,
        out_shape=[
            struct(output.shape),
            struct(tokens.shape),
            struct((2 * qkv.shape[2], 3 * qkv.shape[3]), F32),
            flat(out),
            flat(up),
            flat(down),
        ],
        scratch_shapes=[pltpu.VMEM(part.shape, BF16) for part in (output, tokens, qkv, out, up, down)]
        + [pltpu.SemaphoreType.DMA((6,))],
        compiler_params=pltpu.CompilerParams(vmem_limit_bytes=VMEM_LIMIT),
        name="finish",
    )(output, tokens, qkv, out, up, down)


def make_per_device(seq_size, ctx_size):
    fast = seq_size == 8 and ctx_size == 4

    def per_device(
        tokens,
        lengths,
        query_key_value_weight,
        attention_out_weight,
        up_weight,
        down_weight,
        ln1_gain,
        ln1_shift,
        ln2_gain,
        ln2_shift,
        cotangent,
    ):
        width = tokens.shape[-1]
        inputs, normed_low, packed, cotangent, mixed_low, logs = front(
            ctx_size, lengths, tokens, cotangent, query_key_value_weight, ln1_gain, ln1_shift
        )
        (
            output, grad_down, grad_middle, grad_mixed, grad_up, grad_out, grad_norm_two, *carried
        ) = feed_forward(
            fast, lengths, inputs, mixed_low, cotangent, attention_out_weight, up_weight,
            down_weight, ln2_gain, ln2_shift,
        )
        partials = carried + [grad_up, grad_out]
        grad_tokens, *sums, vectors = back(
            fast, ctx_size, lengths, packed, mixed_low, grad_mixed, logs, inputs, normed_low,
            grad_middle, query_key_value_weight, ln1_gain, grad_norm_two, partials,
        )
        share = width // seq_size
        if fast:
            down, up, out, qkv = sums
            output, grad_tokens, qkv, out, up, down = finish(
                output, grad_tokens, qkv, out, up, down
            )
        else:
            grad_qkv = unpair(sums[0], width, width)
            grad_down = grad_down.reshape(-1, width)
            down, up, out, qkv = [
                sum_weight(part, seq_size, ctx_size)
                for part in (grad_down, grad_up, grad_out, grad_qkv)
            ]
            vectors = lax.psum(vectors, ("seq", "ctx"))
        vectors = lax.dynamic_slice_in_dim(vectors, lax.axis_index("seq") * share, share, 1)
        return (
            output,
            grad_tokens,
            qkv.astype(F32),
            out.astype(F32),
            up.astype(F32),
            down.astype(F32),
            vectors[0],
            vectors[1],
            vectors[2],
            vectors[3],
        )

    return per_device


def solution(mesh):
    placed = (P("seq", "ctx", None), P("seq")) + (P(),) * 8 + (P("seq", "ctx", None),)
    weights = (P("seq", None),) * 4 + (P("seq"),) * 4
    return jax.shard_map(
        make_per_device(mesh.shape["seq"], mesh.shape["ctx"]),
        mesh=mesh,
        in_specs=placed,
        out_specs=(P("seq", "ctx", None),) * 2 + weights,
        check_vma=False,
    )
```

```python
import functools
import math

import jax
import jax.numpy as jnp
from jax import lax
from jax.experimental import pallas as pl
from jax.experimental.pallas import tpu as pltpu
from jax.sharding import PartitionSpec as P

HD = 32
LANES = 128
HEADS = LANES // HD
BLOCK = 256
SCALE = HD ** (-0.5)
SCALE_LOG2 = SCALE * math.log2(math.e)
BF16 = jnp.bfloat16
F32 = jnp.float32
MESH = pl.DeviceIdType.MESH
epsilon = 1e-05
MIB = 2**20
VMEM_LIMIT = 62 * MIB
COT_TAIL = 64
ANY = pl.BlockSpec(memory_space=pl.ANY)
SMEM = pl.BlockSpec(memory_space=pltpu.SMEM)
ONE = pl.Buffered(1)
VECTOR = pl.BlockSpec(memory_space=pltpu.VMEM)


def dot(a, b, dim_a, dim_b):
    return lax.dot_general(
        a, b, (((dim_a,), (dim_b,)), ((), ())), preferred_element_type=F32
    )


def whole(shape):
    return pl.BlockSpec(shape, lambda step: (0,) * len(shape), pipeline_mode=ONE)


def row_of(vector):
    return vector[...].reshape(1, -1)


def struct(shape, kind=BF16):
    return jax.ShapeDtypeStruct(shape, kind)


def greet(partners):
    barrier = pltpu.get_barrier_semaphore()
    for partner in partners:
        pl.semaphore_signal(barrier, inc=1, device_id=partner, device_id_type=MESH)
    pl.semaphore_wait(barrier, len(partners))


def to_partner(source, target, send_sem, recv_sem, partner):
    return pltpu.make_async_remote_copy(
        src_ref=source,
        dst_ref=target,
        send_sem=send_sem,
        recv_sem=recv_sem,
        device_id=partner,
        device_id_type=MESH,
    )


def normalise(rows):
    centred = rows - jnp.mean(rows, axis=-1, keepdims=True)
    inverse = lax.rsqrt(jnp.mean(centred * centred, axis=-1, keepdims=True) + epsilon)
    return (centred * inverse, inverse)


def normalise_backward(grad, hat, inverse, gain):
    grad_hat = grad * gain
    along = jnp.mean(grad_hat * hat, axis=-1, keepdims=True)
    return inverse * (grad_hat - jnp.mean(grad_hat, axis=-1, keepdims=True) - hat * along)


def gelu_and_slope(value):
    cdf = 0.5 * lax.erf(value * math.sqrt(0.5)) + 0.5
    bell = jnp.exp2(value * value * (-0.5 * math.log2(math.e)))
    return (value * cdf, cdf + value * (bell * (1.0 / math.sqrt(2.0 * math.pi))))


def only_head(rows, head):
    lanes = lax.broadcasted_iota(jnp.int32, rows.shape, 1)
    return jnp.where(lanes // HD == head, rows, 0)


def mask_diagonal(scores, block, first, length):
    keys = first + lax.broadcasted_iota(jnp.int32, (block, block), 0)
    queries = first + lax.broadcasted_iota(jnp.int32, (block, block), 1)
    allowed = (keys <= queries) & (keys < length)
    below = scores.shape[0] - block
    diagonal = jnp.where(allowed, scores[below:], -1e30)
    return jnp.concatenate([scores[:below], diagonal], 0) if below else diagonal


def attend(group, length, packed, mixed_ref, log_ref, v_t, mixed_t):
    rows, width = packed.shape[0], packed.shape[1] // 3
    count = rows // BLOCK
    columns = [
        pl.ds(pl.multiple_of(part * width + group * LANES, LANES), LANES) for part in range(3)
    ]
    v_t[...] = packed[:, columns[2]].T

    def scores_of(i, head):
        span = (i + 1) * BLOCK
        query = only_head(packed[i * BLOCK : span, columns[0]], head)
        scores = dot(packed[0:span, columns[1]], query, 1, 1)
        return mask_diagonal(scores, BLOCK, i * BLOCK, length)

    steps = [(i, head) for i in range(count) for head in range(HEADS)]
    scores = scores_of(*steps[0])
    for number, (i, head) in enumerate(steps):
        span = (i + 1) * BLOCK
        following = scores_of(*steps[number + 1]) if number + 1 < len(steps) else None
        summit = jnp.max(scores, axis=0, keepdims=True)
        expo = jnp.exp2(scores * SCALE_LOG2 - summit * SCALE_LOG2)
        denom = jnp.sum(expo, axis=0, keepdims=True)
        part = dot(v_t[head * HD : (head + 1) * HD, 0:span], expo.astype(BF16), 1, 0)
        mixed_t[head * HD : (head + 1) * HD, :] = part / denom
        log_ref[0, head : head + 1, i * BLOCK : span] = summit * SCALE_LOG2 + jnp.log2(denom)
        if head == HEADS - 1:
            mixed_ref[i * BLOCK : span, :] = mixed_t[...].T.astype(BF16)
        scores = following


def front_kernel(
    ctx, length_ref, tokens, cotangent, weight, gain, shift,
    inputs_out, normed_out, packed_out, cotangent_out, mixed_ref, log_ref,
    inputs, normed, packed, v_t, mixed_t, send, recv, cot_send, cot_recv, local,
):
    step = pl.program_id(0)
    me = lax.axis_index("ctx")
    block = tokens.shape[1]
    offsets = [1] + list(range(2, ctx))

    def token_copy(offset):
        return to_partner(
            tokens.at[me ^ offset], inputs.at[me], send.at[offset], recv.at[offset],
            {"ctx": me ^ offset},
        )

    def cotangent_copy(offset):
        return to_partner(
            cotangent.at[me ^ offset, 0:head], cotangent_out.at[me], cot_send.at[offset],
            cot_recv.at[offset], {"ctx": me ^ offset},
        )

    head = cotangent_out.shape[1]
    keeps = [
        pltpu.make_async_copy(inputs, inputs_out, local.at[2]),
        pltpu.make_async_copy(normed, normed_out, local.at[3]),
        pltpu.make_async_copy(packed, packed_out, local.at[4]),
    ]

    @pl.when(step == 0)
    def _():
        own = pltpu.make_async_copy(tokens.at[me], inputs.at[me], local.at[0])
        own.start()
        greet([{"ctx": me ^ offset} for offset in offsets])
        for offset in offsets[::-1]:
            token_copy(offset).start()

        def project(source):
            hat, _ = normalise(inputs[source].astype(F32))
            low = (hat * row_of(gain) + row_of(shift)).astype(BF16)
            rows = pl.ds(pl.multiple_of(source * block, block), block)
            normed[rows, :] = low
            packed[rows, :] = dot(low, weight[...], 1, 0).astype(BF16)

        own.wait()
        project(me)
        for offset in offsets:
            token_copy(offset).wait_recv()
            if offset == offsets[-1]:
                for earlier in offsets:
                    token_copy(earlier).wait_send()
                for later in offsets[::-1]:
                    cotangent_copy(later).start()
            project(me ^ offset)
        for keep in keeps:
            keep.start()

    @pl.when(step > 0)
    def _():
        attend(step - 1, length_ref[me], packed, mixed_ref, log_ref, v_t, mixed_t)

    @pl.when(step == pl.num_programs(0) - 1)
    def _():
        for keep in keeps:
            keep.wait()
        for offset in offsets:
            cotangent_copy(offset).wait()


def front(ctx, length, tokens, cotangent, weight, gain, shift):
    blocks, block, width = tokens.shape
    rows, groups = blocks * block, width // LANES
    group_of = lambda step: jnp.maximum(step - 1, 0)
    return pl.pallas_call(
        functools.partial(front_kernel, ctx),
        grid=(1 + groups,),
        in_specs=[SMEM, ANY, ANY, whole(weight.shape), VECTOR, VECTOR],
        out_specs=[
            ANY, ANY, ANY, ANY,
            pl.BlockSpec((rows, LANES), lambda step: (0, group_of(step))),
            pl.BlockSpec((1, HEADS, rows), lambda step: (group_of(step), 0, 0)),
        ],
        out_shape=[
            struct(tokens.shape),
            struct((rows, width)),
            struct((rows, 3 * width)),
            struct((blocks, block - COT_TAIL, width)),
            struct((rows, width)),
            struct((groups, HEADS, rows), F32),
        ],
        scratch_shapes=[
            pltpu.VMEM(tokens.shape, BF16),
            pltpu.VMEM((rows, width), BF16),
            pltpu.VMEM((rows, 3 * width), BF16),
            pltpu.VMEM((LANES, rows), BF16),
            pltpu.VMEM((LANES, BLOCK), F32),
            pltpu.SemaphoreType.DMA((ctx,)),
            pltpu.SemaphoreType.DMA((ctx,)),
            pltpu.SemaphoreType.DMA((ctx,)),
            pltpu.SemaphoreType.DMA((ctx,)),
            pltpu.SemaphoreType.DMA((5,)),
        ],
        compiler_params=pltpu.CompilerParams(
            vmem_limit_bytes=56 * MIB, collective_id=0, has_side_effects=True
        ),
        name="front",
    )(length, tokens, cotangent, weight, gain, shift)


PARTS = 3
KINDS = 8


class Chunk:
    def __init__(self, source, own, stages, send, recv, local, places, second=False):
        self.source, self.own, self.second = source, own, second
        self.r1, self.r2a, self.r2b, self.r3, self.z1, self.z2, self.out = stages
        self.send, self.recv, self.local, self.places = send, recv, local, places
        self.cut = self.r2a.shape[-1]

    def copy(self, kind):
        seq, ctx, core, x, y, low = self.places
        cut = self.cut
        ways = (
            lambda: (self.source.at[:, :, 1 - core], self.r1, {"seq": seq ^ 1}),
            lambda: (self.r1.at[:, 1 - x, :, :, 0:cut], self.r2a, {"seq": seq ^ 2}),
            lambda: (self.r1.at[1 - y, :, :, :, cut:], self.r2b, {"seq": seq ^ 4}),
            lambda: (self.r2a.at[1 - y], self.r3.at[:, :, 0:cut], {"seq": seq ^ 4}),
            lambda: (self.r2b.at[1 - x], self.r3.at[:, :, cut:], {"seq": seq ^ 2}),
            lambda: (self.r3.at[1 - low], self.z1, {"ctx": ctx ^ 1}),
            lambda: (self.z1, self.z2, {"ctx": ctx ^ 2}),
            lambda: (self.out.at[low], self.out.at[low], {"ctx": ctx ^ 1}),
        )
        source, target, partner = ways[kind]()
        return to_partner(source, target, self.send.at[kind], self.recv.at[kind], partner)

    def own_copy(self):
        core = self.places[2]
        return pltpu.make_async_copy(self.source.at[:, :, core], self.own, self.local)

    def add_second(self):
        _, _, _, x, y, _ = self.places
        cut = self.cut
        self.copy(1).wait_recv()
        self.copy(2).wait_recv()
        for other in range(2):
            self.r2a[other] += self.r1[other, x, :, :, 0:cut]
            self.r2b[other] += self.r1[y, other, :, :, cut:]

    def finish_second(self):
        self.add_second()
        for kind in range(3):
            self.copy(kind).wait_send()

    def event(self, number):
        seq, ctx, core, x, y, low = self.places
        cut = self.cut
        if number == 0:
            self.copy(0).start()
            if self.own is not None:
                self.own_copy().start()
        if number == 1:
            self.copy(0).wait_recv()
            if self.own is not None:
                self.own_copy().wait()
            for along_y in range(2):
                for along_x in range(2):
                    if self.own is not None:
                        kept = self.own[along_y, along_x]
                    else:
                        kept = self.source[along_y, along_x, core]
                    self.r1[along_y, along_x] += kept
            self.copy(1).start()
            self.copy(2).start()
        if number == 2:
            if not self.second:
                self.add_second()
            self.copy(3).start()
            self.copy(4).start()
        if number == 3:
            self.copy(3).wait_recv()
            self.copy(4).wait_recv()
            self.r3[:, :, 0:cut] += self.r2a[y]
            self.r3[:, :, cut:] += self.r2b[x]
            self.copy(5).start()
        if number == 4:
            self.copy(5).wait_recv()
            self.z1[...] += self.r3[low]
            self.copy(6).start()
        if number == 5:
            self.copy(6).wait_recv()
            self.out[low] = self.z1[...] + self.z2[...]
            self.copy(7).start()
        if number == 6:
            to_partner(
                self.out.at[1 - low], self.out.at[1 - low], self.send.at[7], self.recv.at[7],
                {"ctx": ctx ^ 1},
            ).wait_recv()
            for kind in range(3 if self.second else 0, KINDS):
                self.copy(kind).wait_send()


CUT = 512
PIECES = 8


def feed_forward_kernel(
    fast, blocks, length_ref, inputs, mixed, out_weight, gain, shift, up_in, down_in, cot_head,
    cot_in,
    output, grad_down_out, grad_middle_ref, grad_mixed_ref, grad_up_ref, grad_out_ref,
    grad_norm_ref, *rest,
):
    rest = list(rest)
    take = lambda count: [rest.pop(0) for _ in range(count)]
    carried = take(2) if fast else []
    (up_weight, down_weight, normed, upstream, branch, active, hidden, scaled, inverse_of) = take(9)
    (staged, cotangent, grad_down) = take(3)
    (output_send, output_recv, cot_send, cot_recv, local) = take(5)
    step = pl.program_id(0)
    seq, me = lax.axis_index("seq"), lax.axis_index("ctx")
    block, width = staged.shape[1:]
    wide = active.shape[1]
    cuts = wide // CUT
    backward = blocks + 1
    late = backward + blocks
    chunk = None
    if fast:
        send, recv, r1, r2a, r2b = take(5)
        places = (seq, me, seq % 2, (seq // 2) % 2, seq // 4, me % 2)
        chunk = Chunk(
            grad_down, None, (r1, r2a, r2b, None, None, None, None), send, recv, None, places
        )

    def output_copy(row):
        return to_partner(
            staged.at[row], output.at[me], output_send.at[row], output_recv.at[me], {"ctx": row}
        )

    own_output = pltpu.make_async_copy(staged.at[me], output.at[me], local.at[0])
    head = cot_head.shape[1]
    own_cotangent = pltpu.make_async_copy(cot_in.at[me], cotangent.at[me], local.at[4])

    def head_copy(offset):
        other = me ^ offset
        return pltpu.make_async_copy(
            cot_head.at[other], cotangent.at[other, 0:head], local.at[4 + offset]
        )

    def tail_copy(offset):
        return to_partner(
            cot_in.at[me ^ offset, head:block], cotangent.at[me, head:block],
            cot_send.at[offset], cot_recv.at[offset], {"ctx": me ^ offset},
        )

    up_load = pltpu.make_async_copy(up_in, up_weight, local.at[1])
    down_load = pltpu.make_async_copy(down_in, down_weight, local.at[2])

    @pl.when(step == 0)
    def _():
        up_load.start()
        down_load.start()
        partners = [{"ctx": me ^ offset} for offset in range(1, blocks)]
        if fast:
            partners += [{"seq": seq ^ 1}, {"seq": seq ^ 2}, {"seq": seq ^ 4}]
        greet(partners)
        own_cotangent.start()
        for offset in range(blocks - 1, 0, -1):
            tail_copy(offset).start()
            head_copy(offset).start()
        grad_norm_ref[...] = jnp.zeros_like(grad_norm_ref)

    def rows_of(number):
        return pl.ds(pl.multiple_of(number * block, block), block)

    def valid_rows(number):
        places = number * block + lax.broadcasted_iota(jnp.int32, (block, 1), 0)
        return places < length_ref[me]

    @pl.when(step < blocks)
    def _():
        row = me ^ ((step + blocks // 2) % blocks)

        @pl.when(step == blocks - 1)
        def _():
            for offset in range(1, blocks):
                tail_copy(offset).wait()
            output_copy(me ^ 2).start()
            output_copy(me ^ 3).start()
            own_output.start()

        rows = rows_of(row)
        middle = inputs[row].astype(F32) + dot(mixed[rows, :], out_weight[...], 1, 0)
        hat, inverse = normalise(middle)
        scaled[rows, :] = hat
        inverse_of[rows, :] = inverse
        low = (hat * row_of(gain) + row_of(shift)).astype(BF16)
        normed[rows, :] = low

        @pl.when(step == 0)
        def _():
            up_load.wait()
            down_load.wait()

        product_of = lambda cut: dot(low, up_weight[:, cut * CUT : (cut + 1) * CUT], 1, 0)
        current = product_of(0)
        total = middle
        for cut in range(cuts):
            part = slice(cut * CUT, (cut + 1) * CUT)
            following = product_of(cut + 1) if cut + 1 < cuts else None
            value, slope = gelu_and_slope(current)
            value = value.astype(BF16)
            active[rows, part] = value
            hidden[rows, part] = slope.astype(BF16)
            total = total + dot(value, down_weight[part, :], 1, 0)
            current = following
        staged[row] = jnp.where(valid_rows(row), total, 0.0).astype(BF16)

        @pl.when(step == blocks - 1)
        def _():
            output_copy(row).start()

    @pl.when(step == blocks)
    def _():
        own_cotangent.wait()
        for offset in range(1, blocks):
            head_copy(offset).wait()
        for row in range(blocks):
            kept = jnp.where(valid_rows(row), cotangent[row], 0)
            upstream[row * block : (row + 1) * block, :] = kept
        size = wide // PIECES

        @pl.loop(0, PIECES)
        def _(piece):
            columns = pl.ds(pl.multiple_of(piece * size, LANES), size)
            product = dot(active[:, columns], upstream[...], 0, 0)
            product = product.astype(BF16).reshape(2, size // 2, width)
            grad_down[piece // 4, (piece // 2) % 2, piece % 2] = product

        if fast:
            chunk.event(0)
        else:
            pltpu.make_async_copy(grad_down, grad_down_out, local.at[3]).start()

    @pl.when((step >= backward) & (step < late))
    def _():
        number = step - backward
        rows = rows_of(number)
        upstream_low = upstream[rows, :]

        @pl.when(number == 2)
        def _():
            if fast:
                chunk.event(1)

        product_of = lambda cut: dot(
            upstream_low, down_weight[cut * CUT : (cut + 1) * CUT, :], 1, 1
        )
        current = product_of(0)
        grad_normed = 0.0
        for cut in range(cuts):
            part = slice(cut * CUT, (cut + 1) * CUT)
            following = product_of(cut + 1) if cut + 1 < cuts else None
            grad_hidden = (hidden[rows, part].astype(F32) * current).astype(BF16)
            hidden[rows, part] = grad_hidden
            grad_normed = grad_normed + dot(grad_hidden, up_weight[:, part], 1, 1)
            current = following
        hat = scaled[rows, :]
        grad_norm_ref[0:1, :] += jnp.sum(grad_normed * hat, axis=0, keepdims=True)
        grad_norm_ref[1:2, :] += jnp.sum(grad_normed, axis=0, keepdims=True)
        through = normalise_backward(grad_normed, hat, inverse_of[rows, :], row_of(gain))
        grad_middle = upstream_low.astype(F32) + through
        grad_middle_ref[...] = grad_middle
        grad_branch = grad_middle.astype(BF16)
        branch[rows, :] = grad_branch
        grad_mixed_ref[...] = dot(grad_branch, out_weight[...], 1, 1).astype(BF16)

    @pl.when(step == late)
    def _():
        grad_out_ref[...] = dot(mixed[...], branch[...], 0, 0).astype(BF16)

    @pl.when(step >= late)
    def _():
        size = grad_up_ref.shape[1]
        part = pl.ds(pl.multiple_of((step - late) * size, size), size)
        grad_up_ref[...] = dot(normed[...], hidden[:, part], 0, 0).astype(BF16)

    @pl.when(step == pl.num_programs(0) - 1)
    def _():
        own_output.wait()
        for row in range(blocks):

            @pl.when(row != me)
            def _():
                output_copy(row).wait_send()
                to_partner(
                    staged.at[row], output.at[row], output_send.at[row], output_recv.at[row],
                    {"ctx": row},
                ).wait_recv()

        if fast:
            chunk.finish_second()
            for there, here in zip(carried, (r2a, r2b)):
                there[...] = here[...]
        else:
            pltpu.make_async_copy(grad_down, grad_down_out, local.at[3]).wait()


def feed_forward(
    fast, length, inputs, mixed, cot_head, cotangent, out_weight, up_weight, down_weight, gain,
    shift,
):
    blocks, block, width = inputs.shape
    rows, wide = blocks * block, up_weight.shape[1]
    size = 512
    late = 2 * blocks + 1
    steps = late + wide // size
    back_row = lambda step: jnp.clip(step - blocks - 1, 0, blocks - 1)
    up_part = lambda step: jnp.maximum(step - late, 0)
    operands = (inputs, mixed, out_weight)
    piece = wide // PIECES // 2
    lead = (2, 2, 2, 2)
    half = (2, 2, piece, width // 2)
    grad_down_shape = lead + (piece, width) if not fast else (8, LANES)
    carried = [whole(half)] * 2 if fast else []
    extra = []
    if fast:
        extra = [
            pltpu.SemaphoreType.DMA((KINDS,)),
            pltpu.SemaphoreType.DMA((KINDS,)),
            pltpu.VMEM((2, 2, 2, piece, width), BF16),
            pltpu.VMEM(half, BF16),
            pltpu.VMEM(half, BF16),
        ]
    return pl.pallas_call(
        functools.partial(feed_forward_kernel, fast, blocks),
        grid=(steps,),
        in_specs=[SMEM]
        + [whole(operand.shape) for operand in operands]
        + [VECTOR, VECTOR, ANY, ANY, ANY, ANY],
        out_specs=[
            ANY,
            ANY,
            pl.BlockSpec((block, width), lambda step: (back_row(step), 0)),
            pl.BlockSpec((block, width), lambda step: (back_row(step), 0)),
            pl.BlockSpec((width, size), lambda step: (0, up_part(step))),
            whole((width, width)),
            whole((8, width)),
        ]
        + carried,
        out_shape=[
            struct(inputs.shape),
            struct(grad_down_shape),
            struct((rows, width), F32),
            struct((rows, width)),
            struct((width, wide)),
            struct((width, width)),
            struct((8, width), F32),
        ]
        + [struct(half)] * len(carried),
        scratch_shapes=[
            pltpu.VMEM(up_weight.shape, BF16),
            pltpu.VMEM(down_weight.shape, BF16),
            pltpu.VMEM((rows, width), BF16),
            pltpu.VMEM((rows, width), BF16),
            pltpu.VMEM((rows, width), BF16),
            pltpu.VMEM((rows, wide), BF16),
            pltpu.VMEM((rows, wide), BF16),
            pltpu.VMEM((rows, width), F32),
            pltpu.VMEM((rows, 1), F32),
            pltpu.VMEM(inputs.shape, BF16),
            pltpu.VMEM(inputs.shape, BF16),
            pltpu.VMEM(lead + (piece, width), BF16),
            pltpu.SemaphoreType.DMA((blocks,)),
            pltpu.SemaphoreType.DMA((blocks,)),
            pltpu.SemaphoreType.DMA((blocks,)),
            pltpu.SemaphoreType.DMA((blocks,)),
            pltpu.SemaphoreType.DMA((4 + blocks,)),
        ]
        + extra,
        compiler_params=pltpu.CompilerParams(
            vmem_limit_bytes=VMEM_LIMIT, collective_id=1, has_side_effects=True
        ),
        name="feed_forward",
    )(length, *operands, gain, shift, up_weight, down_weight, cot_head, cotangent)


def chunk_scratch(rows, columns, number):
    shapes = [
        (2, 2, 2, rows, columns),
        (2, 2, rows, columns // 2),
        (2, 2, rows, columns // 2),
        (2, rows, columns),
        (rows, columns),
        (rows, columns),
        (2, rows, columns),
    ]
    if number == 0:
        shapes = shapes[3:]
    elif number < 3:
        shapes.insert(0, (2, 2, 2, rows, columns))
    return [pltpu.VMEM(shape, BF16) for shape in shapes]


PLAN = {
    (0, "start"): [(2, 0), (1, 0), (0, 2)],
    (1, "start"): [(2, 1), (1, 1), (0, 3)],
    (1, "end"): [(2, 2)],
    (2, "start"): [(0, 4), (3, 0)],
    (3, "start"): [(1, 2), (2, 3)],
    (3, "end"): [(2, 4), (3, 1), (1, 3)],
    (4, "start"): [(0, 5)],
    (5, "start"): [(3, 2), (4, 0), (1, 4)],
}
PLAN_BEFORE_NORM = [(3, 3)]
PLAN_AFTER_NORM = ["t0", "v0", "v1", "t1"]
PLAN_LAST = [
    (5, 0), (4, 1), (5, 1), "v2", (3, 4), (5, 2), (5, 3), (1, 5), (2, 5), "v3", (4, 2), "t2",
    (2, 6), (4, 3), (3, 5), (0, 6), (5, 4), "v4", (4, 4), "t3", (1, 6), (5, 5), "v5", (3, 6),
    (4, 5), (5, 6), (4, 6),
]
TOKEN_PIECES = 4


def back_kernel(
    fast, ctx, length_ref, q_ref, k_ref, v_ref, mixed_ref, grad_ref, log_ref, inputs_in, normed_in,
    middle_in, weight_in, gain, norm_two, *rest,
):
    rest = list(rest)
    take = lambda count: [rest.pop(0) for _ in range(count)]
    sources = take(4) if fast else []
    (grad_tokens,) = take(1)
    results = take(4) if fast else take(1)
    (vector_out,) = take(1)
    (inputs, normed, middle, weight, grad_normed, pair, partial, staged) = take(8)
    (k_t, grad_q_t, probs_low, grads_low, sum_k, sum_v) = take(6)
    (vectors, vectors_got, local, token_send, token_recv, v_send, v_recv) = take(7)
    step = pl.program_id(0)
    seq, me = lax.axis_index("seq"), lax.axis_index("ctx")
    rows, width = normed.shape
    blocks, block = staged.shape[0], staged.shape[1]
    groups = width // LANES
    chunks = []
    if fast:
        send, recv = take(2)
        places = (seq, me, seq % 2, (seq // 2) % 2, seq // 4, me % 2)
        for number in range(3 + PARTS):
            own, stages = None, [None] * 7
            if number == 0:
                stages[1:] = sources[:2] + take(4)
            elif number < 3:
                own, *stages = take(8)
            else:
                stages = take(7)
            source = sources[number + 1] if number < 3 else partial.at[number - 3]
            chunks.append(
                Chunk(
                    source, own, stages, send.at[number], recv.at[number], local.at[5 + number],
                    places, second=number == 0,
                )
            )

    def token_copy(row, piece, slot):
        size = block // TOKEN_PIECES
        rows_there = slice(piece * size, (piece + 1) * size)
        return to_partner(
            staged.at[row, rows_there], grad_tokens.at[slot, rows_there],
            token_send.at[row, piece], token_recv.at[slot, piece], {"ctx": row},
        )

    def run(name):
        if name[0] == "t":
            for offset in range(ctx - 1, 0, -1):
                token_copy(me ^ offset, int(name[1:]), me).start()
            return
        if not fast:
            return
        if isinstance(name, tuple):
            chunks[name[0]].event(name[1])
            return
        number = int(name[1:])
        partners = [{"seq": seq ^ 1}, {"seq": seq ^ 2}, {"seq": seq ^ 4}]
        partners += [{"ctx": me ^ 1}, {"ctx": me ^ 2}]
        exchange = lambda n: to_partner(
            vectors.at[n], vectors_got.at[n], v_send.at[n], v_recv.at[n], partners[n]
        )
        if number:
            exchange(number - 1).wait()
            vectors[number] = vectors[number - 1] + vectors_got[number - 1]
        if number < len(partners):
            exchange(number).start()

    loads = [
        pltpu.make_async_copy(inputs_in, inputs, local.at[0]),
        pltpu.make_async_copy(normed_in, normed, local.at[1]),
        pltpu.make_async_copy(middle_in, middle, local.at[2]),
        pltpu.make_async_copy(weight_in, weight, local.at[3]),
    ]

    @pl.when(step == 0)
    def _():
        partners = [{"ctx": me ^ offset} for offset in range(1, ctx)]
        if fast:
            partners += [{"seq": seq ^ 1}, {"seq": seq ^ 2}, {"seq": seq ^ 4}]
        greet(partners)
        for load in loads:
            load.start()

    def hook(place):
        for group in range(groups):
            if (group, place) in PLAN:

                @pl.when(step == group)
                def _():
                    for name in PLAN[group, place]:
                        run(name)

    hook("start")

    @pl.when(step < groups)
    def _():
        side = pl.ds(pl.multiple_of((step % 2) * LANES, LANES), LANES)
        attend_backward(
            side, length_ref[me], q_ref, k_ref, v_ref, mixed_ref, grad_ref, log_ref, pair,
            k_t, grad_q_t, probs_low, grads_low, sum_k, sum_v,
        )

    hook("end")

    @pl.when(step == 1)
    def _():
        for load in loads:
            load.wait()
        grad_normed[...] = jnp.zeros_like(grad_normed)

    def weight_gradient(part):
        @pl.loop(0, PARTS)
        def _(name):
            columns = pl.ds(pl.multiple_of(name * 2 * LANES, 2 * LANES), 2 * LANES)
            product = dot(normed[...], pair[name], 0, 0).astype(BF16)
            if fast:
                product = product.reshape(2, 2, 2, 2, width // 16, 2 * LANES)
                partial[part, :, :, :, :, :, columns] = product
            else:
                partial[part, :, columns] = product

    @pl.when((step < groups) & (step % 2 == 1))
    def _():
        part = step // 2

        @pl.loop(0, PARTS)
        def _(name):
            there = pl.multiple_of(name * width + part * 2 * LANES, 2 * LANES)
            grad_normed[...] += dot(pair[name], weight[:, pl.ds(there, 2 * LANES)], 1, 1)

        @pl.when(step < groups - 1)
        def _():
            weight_gradient(part)

    own_tokens = pltpu.make_async_copy(staged.at[me], grad_tokens.at[me], local.at[4])

    @pl.when(step == groups)
    def _():
        for name in PLAN_BEFORE_NORM:
            run(name)
        vectors[0] = jnp.concatenate([jnp.zeros((2, width), F32), norm_two[0:6, :]], axis=0)

        @pl.loop(0, blocks)
        def _(row):
            there = pl.ds(pl.multiple_of(row * block, block), block)
            hat, inverse = normalise(inputs[row].astype(F32))
            grad = grad_normed[there, :]
            vectors[0, 0:1, :] += jnp.sum(grad * hat, axis=0, keepdims=True)
            vectors[0, 1:2, :] += jnp.sum(grad, axis=0, keepdims=True)
            total = middle[there, :] + normalise_backward(grad, hat, inverse, row_of(gain))
            staged[row] = total.astype(BF16)

        own_tokens.start()
        for name in PLAN_AFTER_NORM:
            run(name)
        weight_gradient(PARTS - 1)
        for name in PLAN_LAST:
            run(name)
        if fast:
            for number in range(3):
                results[number][...] = chunks[number].out[...]
            for number in range(PARTS):
                results[3][number] = chunks[3 + number].out[...]
            vector_out[...] = vectors[5]
        else:
            results[0][...] = partial[...]
            vector_out[...] = vectors[0]
        own_tokens.wait()
        for row in range(blocks):

            @pl.when(row != me)
            def _():
                for piece in range(TOKEN_PIECES):
                    token_copy(row, piece, me).wait_send()
                    token_copy(row, piece, row).wait_recv()


def attend_backward(
    side, length, q_ref, k_ref, v_ref, mixed_ref, grad_ref, log_ref, pair,
    k_t, grad_q_t, probs_low, grads_low, sum_k, sum_v,
):
    count = q_ref.shape[0] // BLOCK
    k_t[...] = k_ref[...].T

    def rows_of(i):
        rows = slice(i * BLOCK, (i + 1) * BLOCK)
        product = (grad_ref[rows, :].astype(F32) * mixed_ref[rows, :].astype(F32)).T
        queries = [only_head(q_ref[rows, :], head) for head in range(HEADS)]
        grads = [only_head(grad_ref[rows, :], head) for head in range(HEADS)]
        inner = [
            jnp.sum(product[head * HD : (head + 1) * HD], axis=0, keepdims=True)
            for head in range(HEADS)
        ]
        return (queries, grads, inner)

    prepared = [rows_of(i) for i in range(count)]

    def products_of(i, head):
        span = (i + 1) * BLOCK
        scores = dot(k_ref[0:span, :], prepared[i][0][head], 1, 1)
        return (scores, dot(v_ref[0:span, :], prepared[i][1][head], 1, 1))

    steps = [(i, head) for i in range(count) for head in range(HEADS)]
    current = products_of(*steps[0])
    for number, (i, head) in enumerate(steps):
        below = i * BLOCK
        span = below + BLOCK
        following = products_of(*steps[number + 1]) if number + 1 < len(steps) else None
        scores, grad_probs = current
        scores = mask_diagonal(scores, BLOCK, below, length)
        probs = jnp.exp2(scores * SCALE_LOG2 - log_ref[0, head : head + 1, below:span])
        grad_scores = (probs * (grad_probs - prepared[i][2][head])).astype(BF16)
        columns = slice(head * BLOCK, (head + 1) * BLOCK)
        probs_low[0:span, columns] = probs.astype(BF16)
        grads_low[0:span, columns] = grad_scores
        grad_q_t[head * HD : (head + 1) * HD, :] = dot(
            k_t[head * HD : (head + 1) * HD, 0:span], grad_scores, 1, 0
        )
        if head == HEADS - 1:
            pair[0, below:span, side] = (grad_q_t[...].T * SCALE).astype(BF16)
            grad_v = dot(probs_low[0:span, :], jnp.concatenate(prepared[i][1], 0), 1, 0)
            grad_k = dot(grads_low[0:span, :], jnp.concatenate(prepared[i][0], 0), 1, 0)
            if below:
                sum_v[0:below, :] += grad_v[:below]
                sum_k[0:below, :] += grad_k[:below]
            sum_v[below:span, :] = grad_v[below:]
            sum_k[below:span, :] = grad_k[below:]
        current = following
    pair[1, :, side] = (sum_k[...] * SCALE).astype(BF16)
    pair[2, :, side] = sum_v[...].astype(BF16)


def back(
    fast, ctx, length, packed, mixed, grad_mixed, logs, inputs, normed, middle, weight, gain,
    norm_two, partials,
):
    rows, width = mixed.shape
    blocks, block, _ = inputs.shape
    groups = width // LANES
    group_of = lambda step: jnp.minimum(step, groups - 1)
    columns = lambda part: pl.BlockSpec(
        (rows, LANES), lambda step: (0, part * groups + group_of(step))
    )
    if fast:
        lead = (2, 2, 2, 2)
        carried, partials = partials[:2], partials[2:]
        partials = [
            grad.reshape(lead + (grad.shape[0] // 16, grad.shape[1])) for grad in partials
        ]
        sizes = [(carried[0].shape[2], width)] + [grad.shape[-2:] for grad in partials]
        sizes += [(width // 16, width)] * PARTS
        partials = carried + partials
        reduced = [(2,) + size for size in sizes[:3]] + [(PARTS, 2, width // 16, width)]
        held = [PARTS] + list(lead) + [width // 16, width]
        extra = [
            pltpu.SemaphoreType.DMA((len(sizes), KINDS)),
            pltpu.SemaphoreType.DMA((len(sizes), KINDS)),
        ]
        for number, size in enumerate(sizes):
            extra += chunk_scratch(*size, number)
    else:
        partials = []
        reduced = [(PARTS, width, width)]
        held = [PARTS, width, width]
        extra = []
    scratch = [
        pltpu.VMEM(inputs.shape, BF16),
        pltpu.VMEM((rows, width), BF16),
        pltpu.VMEM((rows, width), F32),
        pltpu.VMEM(weight.shape, BF16),
        pltpu.VMEM((rows, width), F32),
        pltpu.VMEM((PARTS, rows, 2 * LANES), BF16),
        pltpu.VMEM(tuple(held), BF16),
        pltpu.VMEM(inputs.shape, BF16),
        pltpu.VMEM((LANES, rows), BF16),
        pltpu.VMEM((LANES, BLOCK), F32),
        pltpu.VMEM((rows, HEADS * BLOCK), BF16),
        pltpu.VMEM((rows, HEADS * BLOCK), BF16),
        pltpu.VMEM((rows, LANES), F32),
        pltpu.VMEM((rows, LANES), F32),
        pltpu.VMEM((6, 8, width), F32),
        pltpu.VMEM((5, 8, width), F32),
        pltpu.SemaphoreType.DMA((5 + 3 + PARTS,)),
        pltpu.SemaphoreType.DMA((blocks, TOKEN_PIECES)),
        pltpu.SemaphoreType.DMA((blocks, TOKEN_PIECES)),
        pltpu.SemaphoreType.DMA((5,)),
        pltpu.SemaphoreType.DMA((5,)),
    ]
    return pl.pallas_call(
        functools.partial(back_kernel, fast, ctx),
        grid=(groups + 1,),
        in_specs=[
            SMEM, columns(0), columns(1), columns(2), columns(0), columns(0),
            pl.BlockSpec((1, HEADS, rows), lambda step: (group_of(step), 0, 0)),
            ANY, ANY, ANY, ANY, VECTOR, whole(norm_two.shape),
        ] + [whole(partial.shape) if number < 2 else ANY for number, partial in enumerate(partials)],
        out_specs=[ANY] + [whole(shape) for shape in reduced] + [whole((8, width))],
        out_shape=[struct(inputs.shape)]
        + [struct(shape) for shape in reduced]
        + [struct((8, width), F32)],
        scratch_shapes=scratch + extra,
        compiler_params=pltpu.CompilerParams(
            vmem_limit_bytes=VMEM_LIMIT, collective_id=2, has_side_effects=True
        ),
        name="back",
    )(
        length, packed, packed, packed, mixed, grad_mixed, logs, inputs, normed, middle, weight,
        gain, norm_two, *partials,
    )


def exchange(value, axis, size, bit):
    return lax.ppermute(value, axis, [(i, i ^ (1 << bit)) for i in range(size)])


def halve(value, axis, size, bit, dim):
    mine = (lax.axis_index(axis) >> bit) & 1
    kept = lax.dynamic_index_in_dim(value, mine, dim, keepdims=False)
    sent = lax.dynamic_index_in_dim(value, 1 - mine, dim, keepdims=False)
    got = exchange(sent, axis, size, bit)
    return (kept.astype(F32) + got.astype(F32)).astype(BF16)


def scatter_over_seq(value, size, order):
    bits = list(range(size.bit_length() - 1))
    value = value.reshape((2,) * len(bits) + value.shape[1:])
    left = bits[::-1]
    for bit in order:
        value = halve(value, "seq", size, bit, left.index(bit))
        left.remove(bit)
    return value


def sum_over_ctx(value, size):
    bits = list(range(size.bit_length() - 1))
    rows, columns = value.shape
    value = value.reshape((2,) * len(bits) + (rows // size, columns))
    left = bits[::-1]
    for bit in bits:
        value = halve(value, "ctx", size, bit, left.index(bit))
        left.remove(bit)
    for bit in bits[::-1]:
        got = exchange(value, "ctx", size, bit)
        low = ((lax.axis_index("ctx") >> bit) & 1) == 0
        value = jnp.stack([jnp.where(low, value, got), jnp.where(low, got, value)])
    value = value.transpose(tuple(bits[::-1]) + (len(bits), len(bits) + 1))
    return value.reshape(rows, columns)


def sum_weight(grad, seq_size, ctx_size):
    rows, columns = grad.shape
    blocks = grad.reshape(seq_size, rows // seq_size, columns)
    order = list(range(seq_size.bit_length() - 1))
    other = order[:1] + order[1:][::-1]
    half = columns // 2
    first = scatter_over_seq(blocks[:, :, :half], seq_size, order)
    second = scatter_over_seq(blocks[:, :, half:], seq_size, other)
    return sum_over_ctx(jnp.concatenate([first, second], axis=-1), ctx_size)


def unpair(parts, rows, width):
    parts = parts.reshape(PARTS, rows, 3, width // PARTS)
    return parts.transpose(1, 2, 0, 3).reshape(rows, 3 * width)


def finish_kernel(output, tokens, qkv, out, up, down, *results):
    targets, held, wide, copies = results[:6], results[6:12], results[12:16], results[16]
    sources = (output, tokens, qkv, out, up, down)
    loads = [
        pltpu.make_async_copy(source, target, copies.at[number])
        for number, (source, target) in enumerate(zip(sources, held))
    ]
    stores = [
        pltpu.make_async_copy(source, target, copies.at[6 + number])
        for number, (source, target) in enumerate(zip(list(held[:2]) + list(wide), targets))
    ]
    for load in loads:
        load.start()
    for number in range(6):
        loads[number].wait()
        source = held[number]
        if number == 2:
            rows, width = source.shape[2:]
            step = width // 3
            for part in range(PARTS):
                for half in range(2):
                    for name in range(3):
                        first = name * width + part * step
                        value = source[part, half, :, name * step : (name + 1) * step]
                        wide[0][half * rows : (half + 1) * rows, first : first + step] = (
                            value.astype(F32)
                        )
        if number > 2:
            rows = source.shape[1]
            for half in range(2):
                there = slice(half * rows, (half + 1) * rows)
                wide[number - 2][there, :] = source[half].astype(F32)
        stores[number].start()
    for store in stores:
        store.wait()


def finish(output, tokens, qkv, out, up, down):
    flat = lambda part: struct((2 * part.shape[1], part.shape[2]), F32)
    wide = [struct((2 * qkv.shape[2], 3 * qkv.shape[3]), F32), flat(out), flat(up), flat(down)]
    return pl.pallas_call(
        finish_kernel,
        in_specs=[ANY] * 6,
        out_specs=[ANY] * 6,
        out_shape=[struct(output.shape), struct(tokens.shape)] + wide,
        scratch_shapes=[pltpu.VMEM(part.shape, BF16) for part in (output, tokens, qkv, out, up, down)]
        + [pltpu.VMEM(part.shape, F32) for part in wide]
        + [pltpu.SemaphoreType.DMA((12,))],
        compiler_params=pltpu.CompilerParams(vmem_limit_bytes=VMEM_LIMIT),
        name="finish",
    )(output, tokens, qkv, out, up, down)


def make_per_device(seq_size, ctx_size):
    fast = seq_size == 8 and ctx_size == 4

    def per_device(
        tokens,
        lengths,
        query_key_value_weight,
        attention_out_weight,
        up_weight,
        down_weight,
        ln1_gain,
        ln1_shift,
        ln2_gain,
        ln2_shift,
        cotangent,
    ):
        width = tokens.shape[-1]
        inputs, normed_low, packed, cot_head, mixed_low, logs = front(
            ctx_size, lengths, tokens, cotangent, query_key_value_weight, ln1_gain, ln1_shift
        )
        (
            output, grad_down, grad_middle, grad_mixed, grad_up, grad_out, grad_norm_two, *carried
        ) = feed_forward(
            fast, lengths, inputs, mixed_low, cot_head, cotangent, attention_out_weight, up_weight,
            down_weight, ln2_gain, ln2_shift,
        )
        partials = carried + [grad_up, grad_out]
        grad_tokens, *sums, vectors = back(
            fast, ctx_size, lengths, packed, mixed_low, grad_mixed, logs, inputs, normed_low,
            grad_middle, query_key_value_weight, ln1_gain, grad_norm_two, partials,
        )
        share = width // seq_size
        if fast:
            down, up, out, qkv = sums
            output, grad_tokens, qkv, out, up, down = finish(
                output, grad_tokens, qkv, out, up, down
            )
        else:
            grad_qkv = unpair(sums[0], width, width)
            grad_down = grad_down.reshape(-1, width)
            down, up, out, qkv = [
                sum_weight(part, seq_size, ctx_size)
                for part in (grad_down, grad_up, grad_out, grad_qkv)
            ]
            vectors = lax.psum(vectors, ("seq", "ctx"))
        vectors = lax.dynamic_slice_in_dim(vectors, lax.axis_index("seq") * share, share, 1)
        return (
            output,
            grad_tokens,
            qkv.astype(F32),
            out.astype(F32),
            up.astype(F32),
            down.astype(F32),
            vectors[0],
            vectors[1],
            vectors[2],
            vectors[3],
        )

    return per_device


def solution(mesh):
    placed = (P("seq", "ctx", None), P("seq")) + (P(),) * 8 + (P("seq", "ctx", None),)
    weights = (P("seq", None),) * 4 + (P("seq"),) * 4
    return jax.shard_map(
        make_per_device(mesh.shape["seq"], mesh.shape["ctx"]),
        mesh=mesh,
        in_specs=placed,
        out_specs=(P("seq", "ctx", None),) * 2 + weights,
        check_vma=False,
    )
```

```python
import functools
import math

import jax
import jax.numpy as jnp
from jax import lax
from jax.experimental import pallas as pl
from jax.experimental.pallas import tpu as pltpu
from jax.sharding import PartitionSpec as P

HD = 32
LANES = 128
HEADS = LANES // HD
BLOCK = 256
SCALE = HD ** (-0.5)
SCALE_LOG2 = SCALE * math.log2(math.e)
BF16 = jnp.bfloat16
F32 = jnp.float32
MESH = pl.DeviceIdType.MESH
epsilon = 1e-05
MIB = 2**20
VMEM_LIMIT = 62 * MIB
COT_TAIL = 64
ANY = pl.BlockSpec(memory_space=pl.ANY)
SMEM = pl.BlockSpec(memory_space=pltpu.SMEM)
ONE = pl.Buffered(1)
VECTOR = pl.BlockSpec(memory_space=pltpu.VMEM)


def dot(a, b, dim_a, dim_b):
    return lax.dot_general(
        a, b, (((dim_a,), (dim_b,)), ((), ())), preferred_element_type=F32
    )


def whole(shape):
    return pl.BlockSpec(shape, lambda step: (0,) * len(shape), pipeline_mode=ONE)


def row_of(vector):
    return vector[...].reshape(1, -1)


def struct(shape, kind=BF16):
    return jax.ShapeDtypeStruct(shape, kind)


def greet(partners):
    barrier = pltpu.get_barrier_semaphore()
    for partner in partners:
        pl.semaphore_signal(barrier, inc=1, device_id=partner, device_id_type=MESH)
    pl.semaphore_wait(barrier, len(partners))


def to_partner(source, target, send_sem, recv_sem, partner):
    return pltpu.make_async_remote_copy(
        src_ref=source,
        dst_ref=target,
        send_sem=send_sem,
        recv_sem=recv_sem,
        device_id=partner,
        device_id_type=MESH,
    )


def normalise(rows):
    centred = rows - jnp.mean(rows, axis=-1, keepdims=True)
    inverse = lax.rsqrt(jnp.mean(centred * centred, axis=-1, keepdims=True) + epsilon)
    return (centred * inverse, inverse)


def normalise_backward(grad, hat, inverse, gain):
    grad_hat = grad * gain
    along = jnp.mean(grad_hat * hat, axis=-1, keepdims=True)
    return inverse * (grad_hat - jnp.mean(grad_hat, axis=-1, keepdims=True) - hat * along)


def gelu_and_slope(value):
    cdf = 0.5 * lax.erf(value * math.sqrt(0.5)) + 0.5
    bell = jnp.exp2(value * value * (-0.5 * math.log2(math.e)))
    return (value * cdf, cdf + value * (bell * (1.0 / math.sqrt(2.0 * math.pi))))


def only_head(rows, head):
    lanes = lax.broadcasted_iota(jnp.int32, rows.shape, 1)
    return jnp.where(lanes // HD == head, rows, 0)


def mask_diagonal(scores, block, first, length):
    keys = first + lax.broadcasted_iota(jnp.int32, (block, block), 0)
    queries = first + lax.broadcasted_iota(jnp.int32, (block, block), 1)
    allowed = (keys <= queries) & (keys < length)
    below = scores.shape[0] - block
    diagonal = jnp.where(allowed, scores[below:], -1e30)
    return jnp.concatenate([scores[:below], diagonal], 0) if below else diagonal


def attend(group, length, packed, mixed_ref, log_ref, v_t, mixed_t):
    rows, width = packed.shape[0], packed.shape[1] // 3
    count = rows // BLOCK
    columns = [
        pl.ds(pl.multiple_of(part * width + group * LANES, LANES), LANES) for part in range(3)
    ]
    values = packed[:, columns[2]].T
    for head in range(HEADS):
        v_t[head, 0:HD, :] = values[head * HD : (head + 1) * HD, :]
        v_t[head, HD:, :] = jnp.ones((v_t.shape[1] - HD, rows), BF16)

    def scores_of(i, head):
        span = (i + 1) * BLOCK
        query = only_head(packed[i * BLOCK : span, columns[0]], head)
        scores = dot(packed[0:span, columns[1]], query, 1, 1)
        return mask_diagonal(scores, BLOCK, i * BLOCK, length)

    steps = [(i, head) for i in range(count) for head in range(HEADS)]
    scores = scores_of(*steps[0])
    for number, (i, head) in enumerate(steps):
        span = (i + 1) * BLOCK
        following = scores_of(*steps[number + 1]) if number + 1 < len(steps) else None
        summit = jnp.max(scores, axis=0, keepdims=True)
        expo = jnp.exp2(scores * SCALE_LOG2 - summit * SCALE_LOG2)
        part = dot(v_t[head, :, 0:span], expo.astype(BF16), 1, 0)
        denom = part[HD : HD + 1]
        mixed_t[head * HD : (head + 1) * HD, :] = part[:HD] / denom
        log_ref[0, head : head + 1, i * BLOCK : span] = summit * SCALE_LOG2 + jnp.log2(denom)
        if head == HEADS - 1:
            mixed_ref[i * BLOCK : span, :] = mixed_t[...].T.astype(BF16)
        scores = following


def front_kernel(
    ctx, length_ref, tokens, cotangent, weight, gain, shift,
    inputs_out, normed_out, packed_out, cotangent_out, mixed_ref, log_ref,
    inputs, normed, packed, v_t, mixed_t, send, recv, cot_send, cot_recv, local,
):
    step = pl.program_id(0)
    me = lax.axis_index("ctx")
    block = tokens.shape[1]
    offsets = [1] + list(range(2, ctx))

    def token_copy(offset):
        return to_partner(
            tokens.at[me ^ offset], inputs.at[me], send.at[offset], recv.at[offset],
            {"ctx": me ^ offset},
        )

    def cotangent_copy(offset):
        return to_partner(
            cotangent.at[me ^ offset, 0:head], cotangent_out.at[me], cot_send.at[offset],
            cot_recv.at[offset], {"ctx": me ^ offset},
        )

    head = cotangent_out.shape[1]
    keeps = [
        pltpu.make_async_copy(inputs, inputs_out, local.at[2]),
        pltpu.make_async_copy(normed, normed_out, local.at[3]),
        pltpu.make_async_copy(packed, packed_out, local.at[4]),
    ]

    @pl.when(step == 0)
    def _():
        own = pltpu.make_async_copy(tokens.at[me], inputs.at[me], local.at[0])
        own.start()
        greet([{"ctx": me ^ offset} for offset in offsets])
        for offset in offsets[::-1]:
            token_copy(offset).start()

        def project(source):
            hat, _ = normalise(inputs[source].astype(F32))
            low = (hat * row_of(gain) + row_of(shift)).astype(BF16)
            rows = pl.ds(pl.multiple_of(source * block, block), block)
            normed[rows, :] = low
            packed[rows, :] = dot(low, weight[...], 1, 0).astype(BF16)

        own.wait()
        project(me)
        for offset in offsets:
            token_copy(offset).wait_recv()
            if offset == offsets[-1]:
                for earlier in offsets:
                    token_copy(earlier).wait_send()
                for later in offsets[::-1]:
                    cotangent_copy(later).start()
            project(me ^ offset)
        for keep in keeps:
            keep.start()

    @pl.when(step > 0)
    def _():
        attend(step - 1, length_ref[me], packed, mixed_ref, log_ref, v_t, mixed_t)

    @pl.when(step == pl.num_programs(0) - 1)
    def _():
        for keep in keeps:
            keep.wait()
        for offset in offsets:
            cotangent_copy(offset).wait()


def front(ctx, length, tokens, cotangent, weight, gain, shift):
    blocks, block, width = tokens.shape
    rows, groups = blocks * block, width // LANES
    group_of = lambda step: jnp.maximum(step - 1, 0)
    return pl.pallas_call(
        functools.partial(front_kernel, ctx),
        grid=(1 + groups,),
        in_specs=[SMEM, ANY, ANY, whole(weight.shape), VECTOR, VECTOR],
        out_specs=[
            ANY, ANY, ANY, ANY,
            pl.BlockSpec((rows, LANES), lambda step: (0, group_of(step))),
            pl.BlockSpec((1, HEADS, rows), lambda step: (group_of(step), 0, 0)),
        ],
        out_shape=[
            struct(tokens.shape),
            struct((rows, width)),
            struct((rows, 3 * width)),
            struct((blocks, block - COT_TAIL, width)),
            struct((rows, width)),
            struct((groups, HEADS, rows), F32),
        ],
        scratch_shapes=[
            pltpu.VMEM(tokens.shape, BF16),
            pltpu.VMEM((rows, width), BF16),
            pltpu.VMEM((rows, 3 * width), BF16),
            pltpu.VMEM((HEADS, HD + 16, rows), BF16),
            pltpu.VMEM((LANES, BLOCK), F32),
            pltpu.SemaphoreType.DMA((ctx,)),
            pltpu.SemaphoreType.DMA((ctx,)),
            pltpu.SemaphoreType.DMA((ctx,)),
            pltpu.SemaphoreType.DMA((ctx,)),
            pltpu.SemaphoreType.DMA((5,)),
        ],
        compiler_params=pltpu.CompilerParams(
            vmem_limit_bytes=56 * MIB, collective_id=0, has_side_effects=True
        ),
        name="front",
    )(length, tokens, cotangent, weight, gain, shift)


PARTS = 3
KINDS = 8


class Chunk:
    def __init__(self, source, own, stages, send, recv, local, places, second=False):
        self.source, self.own, self.second = source, own, second
        self.r1, self.r2a, self.r2b, self.r3, self.z1, self.z2, self.out = stages
        self.send, self.recv, self.local, self.places = send, recv, local, places
        self.cut = self.r2a.shape[-1]

    def copy(self, kind):
        seq, ctx, core, x, y, low = self.places
        cut = self.cut
        ways = (
            lambda: (self.source.at[:, :, 1 - core], self.r1, {"seq": seq ^ 1}),
            lambda: (self.r1.at[:, 1 - x, :, :, 0:cut], self.r2a, {"seq": seq ^ 2}),
            lambda: (self.r1.at[1 - y, :, :, :, cut:], self.r2b, {"seq": seq ^ 4}),
            lambda: (self.r2a.at[1 - y], self.r3.at[:, :, 0:cut], {"seq": seq ^ 4}),
            lambda: (self.r2b.at[1 - x], self.r3.at[:, :, cut:], {"seq": seq ^ 2}),
            lambda: (self.r3.at[1 - low], self.z1, {"ctx": ctx ^ 1}),
            lambda: (self.z1, self.z2, {"ctx": ctx ^ 2}),
            lambda: (self.out.at[low], self.out.at[low], {"ctx": ctx ^ 1}),
        )
        source, target, partner = ways[kind]()
        return to_partner(source, target, self.send.at[kind], self.recv.at[kind], partner)

    def own_copy(self):
        core = self.places[2]
        return pltpu.make_async_copy(self.source.at[:, :, core], self.own, self.local)

    def add_second(self):
        _, _, _, x, y, _ = self.places
        cut = self.cut
        self.copy(1).wait_recv()
        self.copy(2).wait_recv()
        for other in range(2):
            self.r2a[other] += self.r1[other, x, :, :, 0:cut]
            self.r2b[other] += self.r1[y, other, :, :, cut:]

    def finish_second(self):
        self.add_second()
        for kind in range(3):
            self.copy(kind).wait_send()

    def event(self, number):
        seq, ctx, core, x, y, low = self.places
        cut = self.cut
        if number == 0:
            self.copy(0).start()
            if self.own is not None:
                self.own_copy().start()
        if number == 1:
            self.copy(0).wait_recv()
            if self.own is not None:
                self.own_copy().wait()
            for along_y in range(2):
                for along_x in range(2):
                    if self.own is not None:
                        kept = self.own[along_y, along_x]
                    else:
                        kept = self.source[along_y, along_x, core]
                    self.r1[along_y, along_x] += kept
            self.copy(1).start()
            self.copy(2).start()
        if number == 2:
            if not self.second:
                self.add_second()
            self.copy(3).start()
            self.copy(4).start()
        if number == 3:
            self.copy(3).wait_recv()
            self.copy(4).wait_recv()
            self.r3[:, :, 0:cut] += self.r2a[y]
            self.r3[:, :, cut:] += self.r2b[x]
            self.copy(5).start()
        if number == 4:
            self.copy(5).wait_recv()
            self.z1[...] += self.r3[low]
            self.copy(6).start()
        if number == 5:
            self.copy(6).wait_recv()
            self.out[low] = self.z1[...] + self.z2[...]
            self.copy(7).start()
        if number == 6:
            to_partner(
                self.out.at[1 - low], self.out.at[1 - low], self.send.at[7], self.recv.at[7],
                {"ctx": ctx ^ 1},
            ).wait_recv()
            for kind in range(3 if self.second else 0, KINDS):
                self.copy(kind).wait_send()


CUT = 512
PIECES = 8


def feed_forward_kernel(
    fast, blocks, length_ref, gain, shift, inputs_in, mixed_in, out_in, up_in, down_in, cot_head,
    cot_in,
    output, grad_down_out, grad_middle_ref, grad_mixed_ref, grad_up_ref, grad_out_ref,
    grad_norm_ref, *rest,
):
    rest = list(rest)
    take = lambda count: [rest.pop(0) for _ in range(count)]
    carried = take(2) if fast else []
    (up_weight, down_weight, normed, upstream, branch, active, hidden, scaled, inverse_of) = take(9)
    (staged, cotangent, grad_down, inputs, mixed, out_weight) = take(6)
    (output_send, output_recv, cot_send, cot_recv, local) = take(5)
    step = pl.program_id(0)
    seq, me = lax.axis_index("seq"), lax.axis_index("ctx")
    block, width = staged.shape[1:]
    wide = active.shape[1]
    cuts = wide // CUT
    backward = blocks + 1
    late = backward + blocks
    chunk = None
    if fast:
        send, recv, r1, r2a, r2b = take(5)
        places = (seq, me, seq % 2, (seq // 2) % 2, seq // 4, me % 2)
        chunk = Chunk(
            grad_down, None, (r1, r2a, r2b, None, None, None, None), send, recv, None, places
        )

    def output_copy(row):
        return to_partner(
            staged.at[row], output.at[me], output_send.at[row], output_recv.at[me], {"ctx": row}
        )

    own_output = pltpu.make_async_copy(staged.at[me], output.at[me], local.at[0])
    head = cot_head.shape[1]
    own_cotangent = pltpu.make_async_copy(cot_in.at[me], cotangent.at[me], local.at[4])

    def head_copy(offset):
        other = me ^ offset
        return pltpu.make_async_copy(
            cot_head.at[other], cotangent.at[other, 0:head], local.at[4 + offset]
        )

    def tail_copy(offset):
        return to_partner(
            cot_in.at[me ^ offset, head:block], cotangent.at[me, head:block],
            cot_send.at[offset], cot_recv.at[offset], {"ctx": me ^ offset},
        )

    up_load = pltpu.make_async_copy(up_in, up_weight, local.at[1])
    down_load = pltpu.make_async_copy(down_in, down_weight, local.at[2])

    first_loads = [
        pltpu.make_async_copy(out_in, out_weight, local.at[4 + blocks]),
        pltpu.make_async_copy(mixed_in, mixed, local.at[5 + blocks]),
        pltpu.make_async_copy(inputs_in, inputs, local.at[6 + blocks]),
    ]

    @pl.when(step == 0)
    def _():
        for load in first_loads:
            load.start()
        up_load.start()
        down_load.start()
        partners = [{"ctx": me ^ offset} for offset in range(1, blocks)]
        if fast:
            partners += [{"seq": seq ^ 1}, {"seq": seq ^ 2}, {"seq": seq ^ 4}]
        greet(partners)
        own_cotangent.start()
        for offset in range(blocks - 1, 0, -1):
            tail_copy(offset).start()
            head_copy(offset).start()
        grad_norm_ref[...] = jnp.zeros_like(grad_norm_ref)
        for load in first_loads:
            load.wait()

    def rows_of(number):
        return pl.ds(pl.multiple_of(number * block, block), block)

    def valid_rows(number):
        places = number * block + lax.broadcasted_iota(jnp.int32, (block, 1), 0)
        return places < length_ref[me]

    @pl.when(step < blocks)
    def _():
        row = me ^ ((step + blocks // 2) % blocks)

        @pl.when(step == blocks - 1)
        def _():
            for offset in range(1, blocks):
                tail_copy(offset).wait()
            output_copy(me ^ 2).start()
            output_copy(me ^ 3).start()
            own_output.start()

        rows = rows_of(row)
        middle = inputs[row].astype(F32) + dot(mixed[rows, :], out_weight[...], 1, 0)
        hat, inverse = normalise(middle)
        scaled[rows, :] = hat
        inverse_of[rows, :] = inverse
        low = (hat * row_of(gain) + row_of(shift)).astype(BF16)
        normed[rows, :] = low

        @pl.when(step == 0)
        def _():
            up_load.wait()
            down_load.wait()

        product_of = lambda cut: dot(low, up_weight[:, cut * CUT : (cut + 1) * CUT], 1, 0)
        current = product_of(0)
        total = middle
        for cut in range(cuts):
            part = slice(cut * CUT, (cut + 1) * CUT)
            following = product_of(cut + 1) if cut + 1 < cuts else None
            value, slope = gelu_and_slope(current)
            value = value.astype(BF16)
            active[rows, part] = value
            hidden[rows, part] = slope.astype(BF16)
            total = total + dot(value, down_weight[part, :], 1, 0)
            current = following
        staged[row] = jnp.where(valid_rows(row), total, 0.0).astype(BF16)

        @pl.when(step == blocks - 1)
        def _():
            output_copy(row).start()

    @pl.when(step == blocks)
    def _():
        own_cotangent.wait()
        for offset in range(1, blocks):
            head_copy(offset).wait()
        for row in range(blocks):
            kept = jnp.where(valid_rows(row), cotangent[row], 0)
            upstream[row * block : (row + 1) * block, :] = kept
        size = wide // PIECES

        @pl.loop(0, PIECES)
        def _(piece):
            columns = pl.ds(pl.multiple_of(piece * size, LANES), size)
            product = dot(active[:, columns], upstream[...], 0, 0)
            product = product.astype(BF16).reshape(2, size // 2, width)
            grad_down[piece // 4, (piece // 2) % 2, piece % 2] = product

        if fast:
            chunk.event(0)
        else:
            pltpu.make_async_copy(grad_down, grad_down_out, local.at[3]).start()

    @pl.when((step >= backward) & (step < late))
    def _():
        number = step - backward
        rows = rows_of(number)
        upstream_low = upstream[rows, :]

        @pl.when(number == 2)
        def _():
            if fast:
                chunk.event(1)

        product_of = lambda cut: dot(
            upstream_low, down_weight[cut * CUT : (cut + 1) * CUT, :], 1, 1
        )
        current = product_of(0)
        grad_normed = 0.0
        for cut in range(cuts):
            part = slice(cut * CUT, (cut + 1) * CUT)
            following = product_of(cut + 1) if cut + 1 < cuts else None
            grad_hidden = (hidden[rows, part].astype(F32) * current).astype(BF16)
            hidden[rows, part] = grad_hidden
            grad_normed = grad_normed + dot(grad_hidden, up_weight[:, part], 1, 1)
            current = following
        hat = scaled[rows, :]
        grad_norm_ref[0:1, :] += jnp.sum(grad_normed * hat, axis=0, keepdims=True)
        grad_norm_ref[1:2, :] += jnp.sum(grad_normed, axis=0, keepdims=True)
        through = normalise_backward(grad_normed, hat, inverse_of[rows, :], row_of(gain))
        grad_middle = upstream_low.astype(F32) + through
        grad_middle_ref[...] = grad_middle
        grad_branch = grad_middle.astype(BF16)
        branch[rows, :] = grad_branch
        grad_mixed_ref[...] = dot(grad_branch, out_weight[...], 1, 1).astype(BF16)

    @pl.when(step == late)
    def _():
        grad_out_ref[...] = dot(mixed[...], branch[...], 0, 0).astype(BF16)

    @pl.when(step >= late)
    def _():
        size = grad_up_ref.shape[1]
        part = pl.ds(pl.multiple_of((step - late) * size, size), size)
        grad_up_ref[...] = dot(normed[...], hidden[:, part], 0, 0).astype(BF16)

    @pl.when(step == pl.num_programs(0) - 1)
    def _():
        own_output.wait()
        for row in range(blocks):

            @pl.when(row != me)
            def _():
                output_copy(row).wait_send()
                to_partner(
                    staged.at[row], output.at[row], output_send.at[row], output_recv.at[row],
                    {"ctx": row},
                ).wait_recv()

        if fast:
            chunk.finish_second()
            for there, here in zip(carried, (r2a, r2b)):
                there[...] = here[...]
        else:
            pltpu.make_async_copy(grad_down, grad_down_out, local.at[3]).wait()


def feed_forward(
    fast, length, inputs, mixed, cot_head, cotangent, out_weight, up_weight, down_weight, gain,
    shift,
):
    blocks, block, width = inputs.shape
    rows, wide = blocks * block, up_weight.shape[1]
    size = 1024
    late = 2 * blocks + 1
    steps = late + wide // size
    back_row = lambda step: jnp.clip(step - blocks - 1, 0, blocks - 1)
    up_part = lambda step: jnp.maximum(step - late, 0)
    operands = (inputs, mixed, out_weight, up_weight, down_weight, cot_head, cotangent)
    piece = wide // PIECES // 2
    lead = (2, 2, 2, 2)
    half = (2, 2, piece, width // 2)
    grad_down_shape = lead + (piece, width) if not fast else (8, LANES)
    carried = [whole(half)] * 2 if fast else []
    extra = []
    if fast:
        extra = [
            pltpu.SemaphoreType.DMA((KINDS,)),
            pltpu.SemaphoreType.DMA((KINDS,)),
            pltpu.VMEM((2, 2, 2, piece, width), BF16),
            pltpu.VMEM(half, BF16),
            pltpu.VMEM(half, BF16),
        ]
    return pl.pallas_call(
        functools.partial(feed_forward_kernel, fast, blocks),
        grid=(steps,),
        in_specs=[SMEM, VECTOR, VECTOR] + [ANY] * len(operands),
        out_specs=[
            ANY,
            ANY,
            pl.BlockSpec((block, width), lambda step: (back_row(step), 0)),
            pl.BlockSpec((block, width), lambda step: (back_row(step), 0)),
            pl.BlockSpec((width, size), lambda step: (0, up_part(step))),
            whole((width, width)),
            whole((8, width)),
        ]
        + carried,
        out_shape=[
            struct(inputs.shape),
            struct(grad_down_shape),
            struct((rows, width), F32),
            struct((rows, width)),
            struct((width, wide)),
            struct((width, width)),
            struct((8, width), F32),
        ]
        + [struct(half)] * len(carried),
        scratch_shapes=[
            pltpu.VMEM(up_weight.shape, BF16),
            pltpu.VMEM(down_weight.shape, BF16),
            pltpu.VMEM((rows, width), BF16),
            pltpu.VMEM((rows, width), BF16),
            pltpu.VMEM((rows, width), BF16),
            pltpu.VMEM((rows, wide), BF16),
            pltpu.VMEM((rows, wide), BF16),
            pltpu.VMEM((rows, width), F32),
            pltpu.VMEM((rows, 1), F32),
            pltpu.VMEM(inputs.shape, BF16),
            pltpu.VMEM(inputs.shape, BF16),
            pltpu.VMEM(lead + (piece, width), BF16),
            pltpu.VMEM(inputs.shape, BF16),
            pltpu.VMEM(mixed.shape, BF16),
            pltpu.VMEM(out_weight.shape, BF16),
            pltpu.SemaphoreType.DMA((blocks,)),
            pltpu.SemaphoreType.DMA((blocks,)),
            pltpu.SemaphoreType.DMA((blocks,)),
            pltpu.SemaphoreType.DMA((blocks,)),
            pltpu.SemaphoreType.DMA((7 + blocks,)),
        ]
        + extra,
        compiler_params=pltpu.CompilerParams(
            vmem_limit_bytes=VMEM_LIMIT, collective_id=1, has_side_effects=True
        ),
        name="feed_forward",
    )(length, gain, shift, *operands)


def chunk_scratch(rows, columns, number):
    shapes = [
        (2, 2, 2, rows, columns),
        (2, 2, rows, columns // 2),
        (2, 2, rows, columns // 2),
        (2, rows, columns),
        (rows, columns),
        (rows, columns),
        (2, rows, columns),
    ]
    if number == 0:
        shapes = shapes[3:]
    elif number < 3:
        shapes.insert(0, (2, 2, 2, rows, columns))
    return [pltpu.VMEM(shape, BF16) for shape in shapes]


PLAN = {
    (0, "start"): [(2, 0), (1, 0), (0, 2)],
    (1, "start"): [(2, 1), (1, 1), (0, 3)],
    (1, "end"): [(2, 2)],
    (2, "start"): [(0, 4), (3, 0)],
    (3, "start"): [(1, 2), (2, 3)],
    (3, "end"): [(2, 4), (3, 1), (1, 3)],
    (4, "start"): [(0, 5)],
    (5, "start"): [(3, 2), (4, 0), (1, 4)],
}
PLAN_BEFORE_NORM = [(3, 3)]
PLAN_AFTER_NORM = ['t0', 't1', 'v0', 'v1']
PLAN_LAST = [(5, 0), (4, 1), (5, 1), 'v2', 't2', (3, 4), (5, 2), (1, 5), (2, 5), (5, 3), 'v3', 't3', (4, 2), (2, 6), (4, 3), (3, 5), (0, 6), (5, 4), 'v4', (4, 4), (1, 6), (5, 5), 'v5', (3, 6), (4, 5), (5, 6), (4, 6)]
TOKEN_PIECES = 4


def back_kernel(
    fast, ctx, length_ref, q_ref, k_ref, v_ref, mixed_ref, grad_ref, log_ref, inputs_in, normed_in,
    middle_in, weight_in, gain, norm_two, *rest,
):
    rest = list(rest)
    take = lambda count: [rest.pop(0) for _ in range(count)]
    sources = take(4) if fast else []
    (grad_tokens,) = take(1)
    results = take(4) if fast else take(1)
    (vector_out,) = take(1)
    (inputs, normed, middle, weight, grad_normed, pair, partial, staged) = take(8)
    (k_t, grad_q_t, probs_low, grads_low, sum_k, sum_v) = take(6)
    (vectors, vectors_got, local, token_send, token_recv, v_send, v_recv) = take(7)
    step = pl.program_id(0)
    seq, me = lax.axis_index("seq"), lax.axis_index("ctx")
    rows, width = normed.shape
    blocks, block = staged.shape[0], staged.shape[1]
    groups = width // LANES
    chunks = []
    if fast:
        send, recv = take(2)
        places = (seq, me, seq % 2, (seq // 2) % 2, seq // 4, me % 2)
        for number in range(3 + PARTS):
            own, stages = None, [None] * 7
            if number == 0:
                stages[1:] = sources[:2] + take(4)
            elif number < 3:
                own, *stages = take(8)
            else:
                stages = take(7)
            source = sources[number + 1] if number < 3 else partial.at[number - 3]
            chunks.append(
                Chunk(
                    source, own, stages, send.at[number], recv.at[number], local.at[5 + number],
                    places, second=number == 0,
                )
            )

    def token_copy(row, piece, slot):
        size = block // TOKEN_PIECES
        rows_there = slice(piece * size, (piece + 1) * size)
        return to_partner(
            staged.at[row, rows_there], grad_tokens.at[slot, rows_there],
            token_send.at[row, piece], token_recv.at[slot, piece], {"ctx": row},
        )

    def run(name):
        if name[0] == "t":
            for offset in range(ctx - 1, 0, -1):
                token_copy(me ^ offset, int(name[1:]), me).start()
            return
        if not fast:
            return
        if isinstance(name, tuple):
            chunks[name[0]].event(name[1])
            return
        number = int(name[1:])
        partners = [{"seq": seq ^ 1}, {"seq": seq ^ 2}, {"seq": seq ^ 4}]
        partners += [{"ctx": me ^ 1}, {"ctx": me ^ 2}]
        exchange = lambda n: to_partner(
            vectors.at[n], vectors_got.at[n], v_send.at[n], v_recv.at[n], partners[n]
        )
        if number:
            exchange(number - 1).wait()
            vectors[number] = vectors[number - 1] + vectors_got[number - 1]
        if number < len(partners):
            exchange(number).start()

    loads = [
        pltpu.make_async_copy(inputs_in, inputs, local.at[0]),
        pltpu.make_async_copy(normed_in, normed, local.at[1]),
        pltpu.make_async_copy(middle_in, middle, local.at[2]),
        pltpu.make_async_copy(weight_in, weight, local.at[3]),
    ]

    @pl.when(step == 0)
    def _():
        partners = [{"ctx": me ^ offset} for offset in range(1, ctx)]
        if fast:
            partners += [{"seq": seq ^ 1}, {"seq": seq ^ 2}, {"seq": seq ^ 4}]
        greet(partners)
        for load in loads:
            load.start()

    def hook(place):
        for group in range(groups):
            if (group, place) in PLAN:

                @pl.when(step == group)
                def _():
                    for name in PLAN[group, place]:
                        run(name)

    hook("start")

    @pl.when(step < groups)
    def _():
        side = pl.ds(pl.multiple_of((step % 2) * LANES, LANES), LANES)
        attend_backward(
            side, length_ref[me], q_ref, k_ref, v_ref, mixed_ref, grad_ref, log_ref, pair,
            k_t, grad_q_t, probs_low, grads_low, sum_k, sum_v,
        )

    hook("end")

    @pl.when(step == 1)
    def _():
        for load in loads:
            load.wait()
        grad_normed[...] = jnp.zeros_like(grad_normed)

    def weight_gradient(part):
        @pl.loop(0, PARTS)
        def _(name):
            columns = pl.ds(pl.multiple_of(name * 2 * LANES, 2 * LANES), 2 * LANES)
            product = dot(normed[...], pair[name], 0, 0).astype(BF16)
            if fast:
                product = product.reshape(2, 2, 2, 2, width // 16, 2 * LANES)
                partial[part, :, :, :, :, :, columns] = product
            else:
                partial[part, :, columns] = product

    @pl.when((step < groups) & (step % 2 == 1))
    def _():
        part = step // 2

        @pl.loop(0, PARTS)
        def _(name):
            there = pl.multiple_of(name * width + part * 2 * LANES, 2 * LANES)
            grad_normed[...] += dot(pair[name], weight[:, pl.ds(there, 2 * LANES)], 1, 1)

        @pl.when(step < groups - 1)
        def _():
            weight_gradient(part)

    own_tokens = pltpu.make_async_copy(staged.at[me], grad_tokens.at[me], local.at[4])

    @pl.when(step == groups)
    def _():
        for name in PLAN_BEFORE_NORM:
            run(name)
        vectors[0] = jnp.concatenate([jnp.zeros((2, width), F32), norm_two[0:6, :]], axis=0)

        @pl.loop(0, blocks)
        def _(row):
            there = pl.ds(pl.multiple_of(row * block, block), block)
            hat, inverse = normalise(inputs[row].astype(F32))
            grad = grad_normed[there, :]
            vectors[0, 0:1, :] += jnp.sum(grad * hat, axis=0, keepdims=True)
            vectors[0, 1:2, :] += jnp.sum(grad, axis=0, keepdims=True)
            total = middle[there, :] + normalise_backward(grad, hat, inverse, row_of(gain))
            staged[row] = total.astype(BF16)

        own_tokens.start()
        for name in PLAN_AFTER_NORM:
            run(name)
        weight_gradient(PARTS - 1)
        for name in PLAN_LAST:
            run(name)
        if fast:
            for number in range(3):
                results[number][...] = chunks[number].out[...]
            for number in range(PARTS):
                results[3][number] = chunks[3 + number].out[...]
            vector_out[...] = vectors[5]
        else:
            results[0][...] = partial[...]
            vector_out[...] = vectors[0]
        own_tokens.wait()
        for row in range(blocks):

            @pl.when(row != me)
            def _():
                for piece in range(TOKEN_PIECES):
                    token_copy(row, piece, me).wait_send()
                    token_copy(row, piece, row).wait_recv()


def attend_backward(
    side, length, q_ref, k_ref, v_ref, mixed_ref, grad_ref, log_ref, pair,
    k_t, grad_q_t, probs_low, grads_low, sum_k, sum_v,
):
    count = q_ref.shape[0] // BLOCK
    k_t[...] = k_ref[...].T

    def rows_of(i):
        rows = slice(i * BLOCK, (i + 1) * BLOCK)
        product = (grad_ref[rows, :].astype(F32) * mixed_ref[rows, :].astype(F32)).T
        queries = [only_head(q_ref[rows, :], head) for head in range(HEADS)]
        grads = [only_head(grad_ref[rows, :], head) for head in range(HEADS)]
        inner = [
            jnp.sum(product[head * HD : (head + 1) * HD], axis=0, keepdims=True)
            for head in range(HEADS)
        ]
        return (queries, grads, inner)

    prepared = [rows_of(i) for i in range(count)]

    def products_of(i, head):
        span = (i + 1) * BLOCK
        scores = dot(k_ref[0:span, :], prepared[i][0][head], 1, 1)
        return (scores, dot(v_ref[0:span, :], prepared[i][1][head], 1, 1))

    steps = [(i, head) for i in range(count) for head in range(HEADS)]
    current = products_of(*steps[0])
    for number, (i, head) in enumerate(steps):
        below = i * BLOCK
        span = below + BLOCK
        following = products_of(*steps[number + 1]) if number + 1 < len(steps) else None
        scores, grad_probs = current
        scores = mask_diagonal(scores, BLOCK, below, length)
        probs = jnp.exp2(scores * SCALE_LOG2 - log_ref[0, head : head + 1, below:span])
        grad_scores = (probs * (grad_probs - prepared[i][2][head])).astype(BF16)
        columns = slice(head * BLOCK, (head + 1) * BLOCK)
        probs_low[0:span, columns] = probs.astype(BF16)
        grads_low[0:span, columns] = grad_scores
        grad_q_t[head * HD : (head + 1) * HD, :] = dot(
            k_t[head * HD : (head + 1) * HD, 0:span], grad_scores, 1, 0
        )
        if head == HEADS - 1:
            pair[0, below:span, side] = (grad_q_t[...].T * SCALE).astype(BF16)
            grad_v = dot(probs_low[0:span, :], jnp.concatenate(prepared[i][1], 0), 1, 0)
            grad_k = dot(grads_low[0:span, :], jnp.concatenate(prepared[i][0], 0), 1, 0)
            if below:
                sum_v[0:below, :] += grad_v[:below]
                sum_k[0:below, :] += grad_k[:below]
            sum_v[below:span, :] = grad_v[below:]
            sum_k[below:span, :] = grad_k[below:]
        current = following
    pair[1, :, side] = (sum_k[...] * SCALE).astype(BF16)
    pair[2, :, side] = sum_v[...].astype(BF16)


def back(
    fast, ctx, length, packed, mixed, grad_mixed, logs, inputs, normed, middle, weight, gain,
    norm_two, partials,
):
    rows, width = mixed.shape
    blocks, block, _ = inputs.shape
    groups = width // LANES
    group_of = lambda step: jnp.minimum(step, groups - 1)
    columns = lambda part: pl.BlockSpec(
        (rows, LANES), lambda step: (0, part * groups + group_of(step))
    )
    if fast:
        lead = (2, 2, 2, 2)
        carried, partials = partials[:2], partials[2:]
        partials = [
            grad.reshape(lead + (grad.shape[0] // 16, grad.shape[1])) for grad in partials
        ]
        sizes = [(carried[0].shape[2], width)] + [grad.shape[-2:] for grad in partials]
        sizes += [(width // 16, width)] * PARTS
        partials = carried + partials
        reduced = [(2,) + size for size in sizes[:3]] + [(PARTS, 2, width // 16, width)]
        held = [PARTS] + list(lead) + [width // 16, width]
        extra = [
            pltpu.SemaphoreType.DMA((len(sizes), KINDS)),
            pltpu.SemaphoreType.DMA((len(sizes), KINDS)),
        ]
        for number, size in enumerate(sizes):
            extra += chunk_scratch(*size, number)
    else:
        partials = []
        reduced = [(PARTS, width, width)]
        held = [PARTS, width, width]
        extra = []
    scratch = [
        pltpu.VMEM(inputs.shape, BF16),
        pltpu.VMEM((rows, width), BF16),
        pltpu.VMEM((rows, width), F32),
        pltpu.VMEM(weight.shape, BF16),
        pltpu.VMEM((rows, width), F32),
        pltpu.VMEM((PARTS, rows, 2 * LANES), BF16),
        pltpu.VMEM(tuple(held), BF16),
        pltpu.VMEM(inputs.shape, BF16),
        pltpu.VMEM((LANES, rows), BF16),
        pltpu.VMEM((LANES, BLOCK), F32),
        pltpu.VMEM((rows, HEADS * BLOCK), BF16),
        pltpu.VMEM((rows, HEADS * BLOCK), BF16),
        pltpu.VMEM((rows, LANES), F32),
        pltpu.VMEM((rows, LANES), F32),
        pltpu.VMEM((6, 8, width), F32),
        pltpu.VMEM((5, 8, width), F32),
        pltpu.SemaphoreType.DMA((5 + 3 + PARTS,)),
        pltpu.SemaphoreType.DMA((blocks, TOKEN_PIECES)),
        pltpu.SemaphoreType.DMA((blocks, TOKEN_PIECES)),
        pltpu.SemaphoreType.DMA((5,)),
        pltpu.SemaphoreType.DMA((5,)),
    ]
    return pl.pallas_call(
        functools.partial(back_kernel, fast, ctx),
        grid=(groups + 1,),
        in_specs=[
            SMEM, columns(0), columns(1), columns(2), columns(0), columns(0),
            pl.BlockSpec((1, HEADS, rows), lambda step: (group_of(step), 0, 0)),
            ANY, ANY, ANY, ANY, VECTOR, whole(norm_two.shape),
        ] + [whole(partial.shape) if number < 2 else ANY for number, partial in enumerate(partials)],
        out_specs=[ANY] + [whole(shape) for shape in reduced] + [whole((8, width))],
        out_shape=[struct(inputs.shape)]
        + [struct(shape) for shape in reduced]
        + [struct((8, width), F32)],
        scratch_shapes=scratch + extra,
        compiler_params=pltpu.CompilerParams(
            vmem_limit_bytes=VMEM_LIMIT, collective_id=2, has_side_effects=True
        ),
        name="back",
    )(
        length, packed, packed, packed, mixed, grad_mixed, logs, inputs, normed, middle, weight,
        gain, norm_two, *partials,
    )


def exchange(value, axis, size, bit):
    return lax.ppermute(value, axis, [(i, i ^ (1 << bit)) for i in range(size)])


def halve(value, axis, size, bit, dim):
    mine = (lax.axis_index(axis) >> bit) & 1
    kept = lax.dynamic_index_in_dim(value, mine, dim, keepdims=False)
    sent = lax.dynamic_index_in_dim(value, 1 - mine, dim, keepdims=False)
    got = exchange(sent, axis, size, bit)
    return (kept.astype(F32) + got.astype(F32)).astype(BF16)


def scatter_over_seq(value, size, order):
    bits = list(range(size.bit_length() - 1))
    value = value.reshape((2,) * len(bits) + value.shape[1:])
    left = bits[::-1]
    for bit in order:
        value = halve(value, "seq", size, bit, left.index(bit))
        left.remove(bit)
    return value


def sum_over_ctx(value, size):
    bits = list(range(size.bit_length() - 1))
    rows, columns = value.shape
    value = value.reshape((2,) * len(bits) + (rows // size, columns))
    left = bits[::-1]
    for bit in bits:
        value = halve(value, "ctx", size, bit, left.index(bit))
        left.remove(bit)
    for bit in bits[::-1]:
        got = exchange(value, "ctx", size, bit)
        low = ((lax.axis_index("ctx") >> bit) & 1) == 0
        value = jnp.stack([jnp.where(low, value, got), jnp.where(low, got, value)])
    value = value.transpose(tuple(bits[::-1]) + (len(bits), len(bits) + 1))
    return value.reshape(rows, columns)


def sum_weight(grad, seq_size, ctx_size):
    rows, columns = grad.shape
    blocks = grad.reshape(seq_size, rows // seq_size, columns)
    order = list(range(seq_size.bit_length() - 1))
    other = order[:1] + order[1:][::-1]
    half = columns // 2
    first = scatter_over_seq(blocks[:, :, :half], seq_size, order)
    second = scatter_over_seq(blocks[:, :, half:], seq_size, other)
    return sum_over_ctx(jnp.concatenate([first, second], axis=-1), ctx_size)


def unpair(parts, rows, width):
    parts = parts.reshape(PARTS, rows, 3, width // PARTS)
    return parts.transpose(1, 2, 0, 3).reshape(rows, 3 * width)


def finish_kernel(output, tokens, qkv, out, up, down, *results):
    targets, held, wide, copies = results[:6], results[6:12], results[12:16], results[16]
    sources = (output, tokens, qkv, out, up, down)
    loads = [
        pltpu.make_async_copy(source, target, copies.at[number])
        for number, (source, target) in enumerate(zip(sources, held))
    ]
    stores = [
        pltpu.make_async_copy(source, target, copies.at[6 + number])
        for number, (source, target) in enumerate(zip(list(held[:2]) + list(wide), targets))
    ]
    for load in loads:
        load.start()
    for number in range(6):
        loads[number].wait()
        source = held[number]
        if number == 2:
            rows, width = source.shape[2:]
            step = width // 3
            for part in range(PARTS):
                for half in range(2):
                    for name in range(3):
                        first = name * width + part * step
                        value = source[part, half, :, name * step : (name + 1) * step]
                        wide[0][half * rows : (half + 1) * rows, first : first + step] = (
                            value.astype(F32)
                        )
        if number > 2:
            rows = source.shape[1]
            for half in range(2):
                there = slice(half * rows, (half + 1) * rows)
                wide[number - 2][there, :] = source[half].astype(F32)
        stores[number].start()
    for store in stores:
        store.wait()


def finish(output, tokens, qkv, out, up, down):
    flat = lambda part: struct((2 * part.shape[1], part.shape[2]), F32)
    wide = [struct((2 * qkv.shape[2], 3 * qkv.shape[3]), F32), flat(out), flat(up), flat(down)]
    return pl.pallas_call(
        finish_kernel,
        in_specs=[ANY] * 6,
        out_specs=[ANY] * 6,
        out_shape=[struct(output.shape), struct(tokens.shape)] + wide,
        scratch_shapes=[pltpu.VMEM(part.shape, BF16) for part in (output, tokens, qkv, out, up, down)]
        + [pltpu.VMEM(part.shape, F32) for part in wide]
        + [pltpu.SemaphoreType.DMA((12,))],
        compiler_params=pltpu.CompilerParams(vmem_limit_bytes=VMEM_LIMIT),
        name="finish",
    )(output, tokens, qkv, out, up, down)


def make_per_device(seq_size, ctx_size):
    fast = seq_size == 8 and ctx_size == 4

    def per_device(
        tokens,
        lengths,
        query_key_value_weight,
        attention_out_weight,
        up_weight,
        down_weight,
        ln1_gain,
        ln1_shift,
        ln2_gain,
        ln2_shift,
        cotangent,
    ):
        width = tokens.shape[-1]
        inputs, normed_low, packed, cot_head, mixed_low, logs = front(
            ctx_size, lengths, tokens, cotangent, query_key_value_weight, ln1_gain, ln1_shift
        )
        (
            output, grad_down, grad_middle, grad_mixed, grad_up, grad_out, grad_norm_two, *carried
        ) = feed_forward(
            fast, lengths, inputs, mixed_low, cot_head, cotangent, attention_out_weight, up_weight,
            down_weight, ln2_gain, ln2_shift,
        )
        partials = carried + [grad_up, grad_out]
        grad_tokens, *sums, vectors = back(
            fast, ctx_size, lengths, packed, mixed_low, grad_mixed, logs, inputs, normed_low,
            grad_middle, query_key_value_weight, ln1_gain, grad_norm_two, partials,
        )
        share = width // seq_size
        if fast:
            down, up, out, qkv = sums
            output, grad_tokens, qkv, out, up, down = finish(
                output, grad_tokens, qkv, out, up, down
            )
        else:
            grad_qkv = unpair(sums[0], width, width)
            grad_down = grad_down.reshape(-1, width)
            down, up, out, qkv = [
                sum_weight(part, seq_size, ctx_size)
                for part in (grad_down, grad_up, grad_out, grad_qkv)
            ]
            vectors = lax.psum(vectors, ("seq", "ctx"))
        vectors = lax.dynamic_slice_in_dim(vectors, lax.axis_index("seq") * share, share, 1)
        return (
            output,
            grad_tokens,
            qkv.astype(F32),
            out.astype(F32),
            up.astype(F32),
            down.astype(F32),
            vectors[0],
            vectors[1],
            vectors[2],
            vectors[3],
        )

    return per_device


def solution(mesh):
    placed = (P("seq", "ctx", None), P("seq")) + (P(),) * 8 + (P("seq", "ctx", None),)
    weights = (P("seq", None),) * 4 + (P("seq"),) * 4
    return jax.shard_map(
        make_per_device(mesh.shape["seq"], mesh.shape["ctx"]),
        mesh=mesh,
        in_specs=placed,
        out_specs=(P("seq", "ctx", None),) * 2 + weights,
        check_vma=False,
    )
```

```python
import functools
import math

import jax
import jax.numpy as jnp
from jax import lax
from jax.experimental import pallas as pl
from jax.experimental.pallas import tpu as pltpu
from jax.sharding import PartitionSpec as P

HD = 32
LANES = 128
HEADS = LANES // HD
BLOCK = 256
SCALE = HD ** (-0.5)
SCALE_LOG2 = SCALE * math.log2(math.e)
BF16 = jnp.bfloat16
F32 = jnp.float32
MESH = pl.DeviceIdType.MESH
epsilon = 1e-05
MIB = 2**20
VMEM_LIMIT = 62 * MIB
X_PIECES = 4
COT_TAIL = 64
ANY = pl.BlockSpec(memory_space=pl.ANY)
SMEM = pl.BlockSpec(memory_space=pltpu.SMEM)
ONE = pl.Buffered(1)
VECTOR = pl.BlockSpec(memory_space=pltpu.VMEM)


def dot(a, b, dim_a, dim_b):
    return lax.dot_general(
        a, b, (((dim_a,), (dim_b,)), ((), ())), preferred_element_type=F32
    )


def whole(shape):
    return pl.BlockSpec(shape, lambda step: (0,) * len(shape), pipeline_mode=ONE)


def row_of(vector):
    return vector[...].reshape(1, -1)


def struct(shape, kind=BF16):
    return jax.ShapeDtypeStruct(shape, kind)


def greet(partners):
    barrier = pltpu.get_barrier_semaphore()
    for partner in partners:
        pl.semaphore_signal(barrier, inc=1, device_id=partner, device_id_type=MESH)
    pl.semaphore_wait(barrier, len(partners))


def to_partner(source, target, send_sem, recv_sem, partner):
    return pltpu.make_async_remote_copy(
        src_ref=source,
        dst_ref=target,
        send_sem=send_sem,
        recv_sem=recv_sem,
        device_id=partner,
        device_id_type=MESH,
    )


def normalise(rows):
    centred = rows - jnp.mean(rows, axis=-1, keepdims=True)
    inverse = lax.rsqrt(jnp.mean(centred * centred, axis=-1, keepdims=True) + epsilon)
    return (centred * inverse, inverse)


def normalise_backward(grad, hat, inverse, gain):
    grad_hat = grad * gain
    along = jnp.mean(grad_hat * hat, axis=-1, keepdims=True)
    return inverse * (grad_hat - jnp.mean(grad_hat, axis=-1, keepdims=True) - hat * along)


def gelu_and_slope(value):
    cdf = 0.5 * lax.erf(value * math.sqrt(0.5)) + 0.5
    bell = jnp.exp2(value * value * (-0.5 * math.log2(math.e)))
    return (value * cdf, cdf + value * (bell * (1.0 / math.sqrt(2.0 * math.pi))))


def only_head(rows, head):
    lanes = lax.broadcasted_iota(jnp.int32, rows.shape, 1)
    return jnp.where(lanes // HD == head, rows, 0)


def mask_diagonal(scores, block, first, length):
    keys = first + lax.broadcasted_iota(jnp.int32, (block, block), 0)
    queries = first + lax.broadcasted_iota(jnp.int32, (block, block), 1)
    allowed = (keys <= queries) & (keys < length)
    below = scores.shape[0] - block
    diagonal = jnp.where(allowed, scores[below:], -1e30)
    return jnp.concatenate([scores[:below], diagonal], 0) if below else diagonal


def attend(group, length, packed, mixed_ref, log_ref, v_t, mixed_t):
    rows, width = packed.shape[0], packed.shape[1] // 3
    count = rows // BLOCK
    columns = [
        pl.ds(pl.multiple_of(part * width + group * LANES, LANES), LANES) for part in range(3)
    ]
    values = packed[:, columns[2]].T
    for head in range(HEADS):
        v_t[head, 0:HD, :] = values[head * HD : (head + 1) * HD, :]
        v_t[head, HD:, :] = jnp.ones((v_t.shape[1] - HD, rows), BF16)

    def scores_of(i, head):
        span = (i + 1) * BLOCK
        query = only_head(packed[i * BLOCK : span, columns[0]], head)
        scores = dot(packed[0:span, columns[1]], query, 1, 1)
        return mask_diagonal(scores, BLOCK, i * BLOCK, length)

    steps = [(i, head) for i in range(count) for head in range(HEADS)]
    scores = scores_of(*steps[0])
    for number, (i, head) in enumerate(steps):
        span = (i + 1) * BLOCK
        following = scores_of(*steps[number + 1]) if number + 1 < len(steps) else None
        summit = jnp.max(scores, axis=0, keepdims=True)
        expo = jnp.exp2(scores * SCALE_LOG2 - summit * SCALE_LOG2)
        part = dot(v_t[head, :, 0:span], expo.astype(BF16), 1, 0)
        denom = part[HD : HD + 1]
        mixed_t[head * HD : (head + 1) * HD, :] = part[:HD] / denom
        log_ref[0, head : head + 1, i * BLOCK : span] = summit * SCALE_LOG2 + jnp.log2(denom)
        if head == HEADS - 1:
            mixed_ref[i * BLOCK : span, :] = mixed_t[...].T.astype(BF16)
        scores = following


def front_kernel(
    ctx, length_ref, tokens, cotangent, weight, gain, shift,
    inputs_out, normed_out, packed_out, cotangent_out, mixed_ref, log_ref,
    inputs, normed, packed, v_t, mixed_t, send, recv, cot_send, cot_recv, local,
):
    step = pl.program_id(0)
    me = lax.axis_index("ctx")
    block = tokens.shape[1]
    offsets = [1] + list(range(2, ctx))

    def token_copy(offset, piece):
        size = block // X_PIECES
        there = slice(piece * size, (piece + 1) * size)
        return to_partner(
            tokens.at[me ^ offset, there], inputs.at[me, there], send.at[offset, piece],
            recv.at[offset, piece], {"ctx": me ^ offset},
        )

    def cotangent_copy(offset):
        return to_partner(
            cotangent.at[me ^ offset, 0:head], cotangent_out.at[me], cot_send.at[offset],
            cot_recv.at[offset], {"ctx": me ^ offset},
        )

    head = cotangent_out.shape[1]
    keeps = [
        pltpu.make_async_copy(inputs, inputs_out, local.at[2]),
        pltpu.make_async_copy(normed, normed_out, local.at[3]),
        pltpu.make_async_copy(packed, packed_out, local.at[4]),
    ]

    @pl.when(step == 0)
    def _():
        own = pltpu.make_async_copy(tokens.at[me], inputs.at[me], local.at[0])
        own.start()
        greet([{"ctx": me ^ offset} for offset in offsets])
        for piece in range(X_PIECES):
            for offset in offsets[::-1]:
                token_copy(offset, piece).start()

        def project(source):
            hat, _ = normalise(inputs[source].astype(F32))
            low = (hat * row_of(gain) + row_of(shift)).astype(BF16)
            rows = pl.ds(pl.multiple_of(source * block, block), block)
            normed[rows, :] = low
            packed[rows, :] = dot(low, weight[...], 1, 0).astype(BF16)

        own.wait()
        project(me)
        for offset in offsets:
            for piece in range(X_PIECES):
                token_copy(offset, piece).wait_recv()
            if offset == offsets[-1]:
                for earlier in offsets:
                    for piece in range(X_PIECES):
                        token_copy(earlier, piece).wait_send()
                for later in offsets[::-1]:
                    cotangent_copy(later).start()
            project(me ^ offset)
        for keep in keeps:
            keep.start()

    @pl.when(step > 0)
    def _():
        attend(step - 1, length_ref[me], packed, mixed_ref, log_ref, v_t, mixed_t)

    @pl.when(step == pl.num_programs(0) - 1)
    def _():
        for keep in keeps:
            keep.wait()
        for offset in offsets:
            cotangent_copy(offset).wait()


def front(ctx, length, tokens, cotangent, weight, gain, shift):
    blocks, block, width = tokens.shape
    rows, groups = blocks * block, width // LANES
    group_of = lambda step: jnp.maximum(step - 1, 0)
    return pl.pallas_call(
        functools.partial(front_kernel, ctx),
        grid=(1 + groups,),
        in_specs=[SMEM, ANY, ANY, whole(weight.shape), VECTOR, VECTOR],
        out_specs=[
            ANY, ANY, ANY, ANY,
            pl.BlockSpec((rows, LANES), lambda step: (0, group_of(step))),
            pl.BlockSpec((1, HEADS, rows), lambda step: (group_of(step), 0, 0)),
        ],
        out_shape=[
            struct(tokens.shape),
            struct((rows, width)),
            struct((rows, 3 * width)),
            struct((blocks, block - COT_TAIL, width)),
            struct((rows, width)),
            struct((groups, HEADS, rows), F32),
        ],
        scratch_shapes=[
            pltpu.VMEM(tokens.shape, BF16),
            pltpu.VMEM((rows, width), BF16),
            pltpu.VMEM((rows, 3 * width), BF16),
            pltpu.VMEM((HEADS, HD + 16, rows), BF16),
            pltpu.VMEM((LANES, BLOCK), F32),
            pltpu.SemaphoreType.DMA((ctx, X_PIECES)),
            pltpu.SemaphoreType.DMA((ctx, X_PIECES)),
            pltpu.SemaphoreType.DMA((ctx,)),
            pltpu.SemaphoreType.DMA((ctx,)),
            pltpu.SemaphoreType.DMA((5,)),
        ],
        compiler_params=pltpu.CompilerParams(
            vmem_limit_bytes=56 * MIB, collective_id=0, has_side_effects=True
        ),
        name="front",
    )(length, tokens, cotangent, weight, gain, shift)


PARTS = 3
KINDS = 8


class Chunk:
    def __init__(self, source, own, stages, send, recv, local, places, second=False):
        self.source, self.own, self.second = source, own, second
        self.r1, self.r2a, self.r2b, self.r3, self.z1, self.z2, self.out = stages
        self.send, self.recv, self.local, self.places = send, recv, local, places
        self.cut = self.r2a.shape[-1]

    def copy(self, kind):
        seq, ctx, core, x, y, low = self.places
        cut = self.cut
        ways = (
            lambda: (self.source.at[:, :, 1 - core], self.r1, {"seq": seq ^ 1}),
            lambda: (self.r1.at[:, 1 - x, :, :, 0:cut], self.r2a, {"seq": seq ^ 2}),
            lambda: (self.r1.at[1 - y, :, :, :, cut:], self.r2b, {"seq": seq ^ 4}),
            lambda: (self.r2a.at[1 - y], self.r3.at[:, :, 0:cut], {"seq": seq ^ 4}),
            lambda: (self.r2b.at[1 - x], self.r3.at[:, :, cut:], {"seq": seq ^ 2}),
            lambda: (self.r3.at[1 - low], self.z1, {"ctx": ctx ^ 1}),
            lambda: (self.z1, self.z2, {"ctx": ctx ^ 2}),
            lambda: (self.out.at[low], self.out.at[low], {"ctx": ctx ^ 1}),
        )
        source, target, partner = ways[kind]()
        return to_partner(source, target, self.send.at[kind], self.recv.at[kind], partner)

    def own_copy(self):
        core = self.places[2]
        return pltpu.make_async_copy(self.source.at[:, :, core], self.own, self.local)

    def add_second(self):
        _, _, _, x, y, _ = self.places
        cut = self.cut
        self.copy(1).wait_recv()
        self.copy(2).wait_recv()
        for other in range(2):
            self.r2a[other] += self.r1[other, x, :, :, 0:cut]
            self.r2b[other] += self.r1[y, other, :, :, cut:]

    def finish_second(self):
        self.add_second()
        for kind in range(3):
            self.copy(kind).wait_send()

    def event(self, number):
        seq, ctx, core, x, y, low = self.places
        cut = self.cut
        if number == 0:
            self.copy(0).start()
            if self.own is not None:
                self.own_copy().start()
        if number == 1:
            self.copy(0).wait_recv()
            if self.own is not None:
                self.own_copy().wait()
            for along_y in range(2):
                for along_x in range(2):
                    if self.own is not None:
                        kept = self.own[along_y, along_x]
                    else:
                        kept = self.source[along_y, along_x, core]
                    self.r1[along_y, along_x] += kept
            self.copy(1).start()
            self.copy(2).start()
        if number == 2:
            if not self.second:
                self.add_second()
            self.copy(3).start()
            self.copy(4).start()
        if number == 3:
            self.copy(3).wait_recv()
            self.copy(4).wait_recv()
            self.r3[:, :, 0:cut] += self.r2a[y]
            self.r3[:, :, cut:] += self.r2b[x]
            self.copy(5).start()
        if number == 4:
            self.copy(5).wait_recv()
            self.z1[...] += self.r3[low]
            self.copy(6).start()
        if number == 5:
            self.copy(6).wait_recv()
            self.out[low] = self.z1[...] + self.z2[...]
            self.copy(7).start()
        if number == 6:
            to_partner(
                self.out.at[1 - low], self.out.at[1 - low], self.send.at[7], self.recv.at[7],
                {"ctx": ctx ^ 1},
            ).wait_recv()
            for kind in range(3 if self.second else 0, KINDS):
                self.copy(kind).wait_send()


CUT = 512
PIECES = 8


def feed_forward_kernel(
    fast, blocks, length_ref, gain, shift, inputs_in, mixed_in, out_in, up_in, down_in, cot_head,
    cot_in,
    output, grad_down_out, grad_middle_ref, grad_mixed_ref, grad_up_ref, grad_out_ref,
    grad_norm_ref, *rest,
):
    rest = list(rest)
    take = lambda count: [rest.pop(0) for _ in range(count)]
    carried = take(2) if fast else []
    (up_weight, down_weight, normed, upstream, branch, active, hidden, scaled, inverse_of) = take(9)
    (staged, cotangent, grad_down, inputs, mixed, out_weight) = take(6)
    (output_send, output_recv, cot_send, cot_recv, local) = take(5)
    step = pl.program_id(0)
    seq, me = lax.axis_index("seq"), lax.axis_index("ctx")
    block, width = staged.shape[1:]
    wide = active.shape[1]
    cuts = wide // CUT
    backward = blocks + 1
    late = backward + blocks
    chunk = None
    if fast:
        send, recv, r1, r2a, r2b = take(5)
        places = (seq, me, seq % 2, (seq // 2) % 2, seq // 4, me % 2)
        chunk = Chunk(
            grad_down, None, (r1, r2a, r2b, None, None, None, None), send, recv, None, places
        )

    def output_copy(row):
        return to_partner(
            staged.at[row], output.at[me], output_send.at[row], output_recv.at[me], {"ctx": row}
        )

    own_output = pltpu.make_async_copy(staged.at[me], output.at[me], local.at[0])
    head = cot_head.shape[1]
    own_cotangent = pltpu.make_async_copy(cot_in.at[me], cotangent.at[me], local.at[4])

    def head_copy(offset):
        other = me ^ offset
        return pltpu.make_async_copy(
            cot_head.at[other], cotangent.at[other, 0:head], local.at[4 + offset]
        )

    def tail_copy(offset):
        return to_partner(
            cot_in.at[me ^ offset, head:block], cotangent.at[me, head:block],
            cot_send.at[offset], cot_recv.at[offset], {"ctx": me ^ offset},
        )

    up_load = pltpu.make_async_copy(up_in, up_weight, local.at[1])
    down_load = pltpu.make_async_copy(down_in, down_weight, local.at[2])

    first_loads = [
        pltpu.make_async_copy(out_in, out_weight, local.at[4 + blocks]),
        pltpu.make_async_copy(mixed_in, mixed, local.at[5 + blocks]),
        pltpu.make_async_copy(inputs_in, inputs, local.at[6 + blocks]),
    ]

    @pl.when(step == 0)
    def _():
        for load in first_loads:
            load.start()
        up_load.start()
        down_load.start()
        partners = [{"ctx": me ^ offset} for offset in range(1, blocks)]
        if fast:
            partners += [{"seq": seq ^ 1}, {"seq": seq ^ 2}, {"seq": seq ^ 4}]
        greet(partners)
        own_cotangent.start()
        for offset in range(blocks - 1, 0, -1):
            tail_copy(offset).start()
            head_copy(offset).start()
        grad_norm_ref[...] = jnp.zeros_like(grad_norm_ref)
        for load in first_loads:
            load.wait()

    def rows_of(number):
        return pl.ds(pl.multiple_of(number * block, block), block)

    def valid_rows(number):
        places = number * block + lax.broadcasted_iota(jnp.int32, (block, 1), 0)
        return places < length_ref[me]

    @pl.when(step < blocks)
    def _():
        row = me ^ ((step + blocks // 2) % blocks)

        @pl.when(step == blocks - 1)
        def _():
            for offset in range(1, blocks):
                tail_copy(offset).wait()
            output_copy(me ^ 2).start()
            output_copy(me ^ 3).start()
            own_output.start()

        rows = rows_of(row)
        middle = inputs[row].astype(F32) + dot(mixed[rows, :], out_weight[...], 1, 0)
        hat, inverse = normalise(middle)
        scaled[rows, :] = hat
        inverse_of[rows, :] = inverse
        low = (hat * row_of(gain) + row_of(shift)).astype(BF16)
        normed[rows, :] = low

        @pl.when(step == 0)
        def _():
            up_load.wait()

        product_of = lambda cut: dot(low, up_weight[:, cut * CUT : (cut + 1) * CUT], 1, 0)
        current = product_of(0)

        @pl.when(step == 0)
        def _():
            down_load.wait()

        total = middle
        for cut in range(cuts):
            part = slice(cut * CUT, (cut + 1) * CUT)
            following = product_of(cut + 1) if cut + 1 < cuts else None
            value, slope = gelu_and_slope(current)
            value = value.astype(BF16)
            active[rows, part] = value
            hidden[rows, part] = slope.astype(BF16)
            total = total + dot(value, down_weight[part, :], 1, 0)
            current = following
        staged[row] = jnp.where(valid_rows(row), total, 0.0).astype(BF16)

        @pl.when(step == blocks - 1)
        def _():
            output_copy(row).start()

    @pl.when(step == blocks)
    def _():
        own_cotangent.wait()
        for offset in range(1, blocks):
            head_copy(offset).wait()
        for row in range(blocks):
            kept = jnp.where(valid_rows(row), cotangent[row], 0)
            upstream[row * block : (row + 1) * block, :] = kept
        size = wide // PIECES

        @pl.loop(0, PIECES)
        def _(piece):
            columns = pl.ds(pl.multiple_of(piece * size, LANES), size)
            product = dot(active[:, columns], upstream[...], 0, 0)
            product = product.astype(BF16).reshape(2, size // 2, width)
            grad_down[piece // 4, (piece // 2) % 2, piece % 2] = product

        if fast:
            chunk.event(0)
        else:
            pltpu.make_async_copy(grad_down, grad_down_out, local.at[3]).start()

    @pl.when((step >= backward) & (step < late))
    def _():
        number = step - backward
        rows = rows_of(number)
        upstream_low = upstream[rows, :]

        @pl.when(number == 2)
        def _():
            if fast:
                chunk.event(1)

        product_of = lambda cut: dot(
            upstream_low, down_weight[cut * CUT : (cut + 1) * CUT, :], 1, 1
        )
        current = product_of(0)
        grad_normed = 0.0
        for cut in range(cuts):
            part = slice(cut * CUT, (cut + 1) * CUT)
            following = product_of(cut + 1) if cut + 1 < cuts else None
            grad_hidden = (hidden[rows, part].astype(F32) * current).astype(BF16)
            hidden[rows, part] = grad_hidden
            grad_normed = grad_normed + dot(grad_hidden, up_weight[:, part], 1, 1)
            current = following
        hat = scaled[rows, :]
        grad_norm_ref[0:1, :] += jnp.sum(grad_normed * hat, axis=0, keepdims=True)
        grad_norm_ref[1:2, :] += jnp.sum(grad_normed, axis=0, keepdims=True)
        through = normalise_backward(grad_normed, hat, inverse_of[rows, :], row_of(gain))
        grad_middle = upstream_low.astype(F32) + through
        grad_middle_ref[...] = grad_middle
        grad_branch = grad_middle.astype(BF16)
        branch[rows, :] = grad_branch
        grad_mixed_ref[...] = dot(grad_branch, out_weight[...], 1, 1).astype(BF16)

    @pl.when(step == late)
    def _():
        grad_out_ref[...] = dot(mixed[...], branch[...], 0, 0).astype(BF16)

    @pl.when(step >= late)
    def _():
        size = grad_up_ref.shape[1]
        part = pl.ds(pl.multiple_of((step - late) * size, size), size)
        grad_up_ref[...] = dot(normed[...], hidden[:, part], 0, 0).astype(BF16)

    @pl.when(step == pl.num_programs(0) - 1)
    def _():
        own_output.wait()
        for row in range(blocks):

            @pl.when(row != me)
            def _():
                output_copy(row).wait_send()
                to_partner(
                    staged.at[row], output.at[row], output_send.at[row], output_recv.at[row],
                    {"ctx": row},
                ).wait_recv()

        if fast:
            chunk.finish_second()
            for there, here in zip(carried, (r2a, r2b)):
                there[...] = here[...]
        else:
            pltpu.make_async_copy(grad_down, grad_down_out, local.at[3]).wait()


def feed_forward(
    fast, length, inputs, mixed, cot_head, cotangent, out_weight, up_weight, down_weight, gain,
    shift,
):
    blocks, block, width = inputs.shape
    rows, wide = blocks * block, up_weight.shape[1]
    size = 1024
    late = 2 * blocks + 1
    steps = late + wide // size
    back_row = lambda step: jnp.clip(step - blocks - 1, 0, blocks - 1)
    up_part = lambda step: jnp.maximum(step - late, 0)
    operands = (inputs, mixed, out_weight, up_weight, down_weight, cot_head, cotangent)
    piece = wide // PIECES // 2
    lead = (2, 2, 2, 2)
    half = (2, 2, piece, width // 2)
    grad_down_shape = lead + (piece, width) if not fast else (8, LANES)
    carried = [whole(half)] * 2 if fast else []
    extra = []
    if fast:
        extra = [
            pltpu.SemaphoreType.DMA((KINDS,)),
            pltpu.SemaphoreType.DMA((KINDS,)),
            pltpu.VMEM((2, 2, 2, piece, width), BF16),
            pltpu.VMEM(half, BF16),
            pltpu.VMEM(half, BF16),
        ]
    return pl.pallas_call(
        functools.partial(feed_forward_kernel, fast, blocks),
        grid=(steps,),
        in_specs=[SMEM, VECTOR, VECTOR] + [ANY] * len(operands),
        out_specs=[
            ANY,
            ANY,
            pl.BlockSpec((block, width), lambda step: (back_row(step), 0)),
            pl.BlockSpec((block, width), lambda step: (back_row(step), 0)),
            pl.BlockSpec((width, size), lambda step: (0, up_part(step))),
            whole((width, width)),
            whole((8, width)),
        ]
        + carried,
        out_shape=[
            struct(inputs.shape),
            struct(grad_down_shape),
            struct((rows, width), F32),
            struct((rows, width)),
            struct((width, wide)),
            struct((width, width)),
            struct((8, width), F32),
        ]
        + [struct(half)] * len(carried),
        scratch_shapes=[
            pltpu.VMEM(up_weight.shape, BF16),
            pltpu.VMEM(down_weight.shape, BF16),
            pltpu.VMEM((rows, width), BF16),
            pltpu.VMEM((rows, width), BF16),
            pltpu.VMEM((rows, width), BF16),
            pltpu.VMEM((rows, wide), BF16),
            pltpu.VMEM((rows, wide), BF16),
            pltpu.VMEM((rows, width), F32),
            pltpu.VMEM((rows, 1), F32),
            pltpu.VMEM(inputs.shape, BF16),
            pltpu.VMEM(inputs.shape, BF16),
            pltpu.VMEM(lead + (piece, width), BF16),
            pltpu.VMEM(inputs.shape, BF16),
            pltpu.VMEM(mixed.shape, BF16),
            pltpu.VMEM(out_weight.shape, BF16),
            pltpu.SemaphoreType.DMA((blocks,)),
            pltpu.SemaphoreType.DMA((blocks,)),
            pltpu.SemaphoreType.DMA((blocks,)),
            pltpu.SemaphoreType.DMA((blocks,)),
            pltpu.SemaphoreType.DMA((7 + blocks,)),
        ]
        + extra,
        compiler_params=pltpu.CompilerParams(
            vmem_limit_bytes=VMEM_LIMIT, collective_id=1, has_side_effects=True
        ),
        name="feed_forward",
    )(length, gain, shift, *operands)


def chunk_scratch(rows, columns, number):
    shapes = [
        (2, 2, 2, rows, columns),
        (2, 2, rows, columns // 2),
        (2, 2, rows, columns // 2),
        (2, rows, columns),
        (rows, columns),
        (rows, columns),
        (2, rows, columns),
    ]
    if number == 0:
        shapes = shapes[3:]
    elif number < 3:
        shapes.insert(0, (2, 2, 2, rows, columns))
    return [pltpu.VMEM(shape, BF16) for shape in shapes]


PLAN = {
    (0, "start"): [(2, 0), (1, 0), (0, 2)],
    (1, "start"): [(2, 1), (1, 1), (0, 3)],
    (1, "end"): [(2, 2)],
    (2, "start"): [(0, 4), (3, 0)],
    (3, "start"): [(1, 2), (2, 3)],
    (3, "end"): [(2, 4), (3, 1), (1, 3)],
    (4, "start"): [(0, 5)],
    (5, "start"): [(3, 2), (4, 0), (1, 4)],
}
PLAN_BEFORE_NORM = [(3, 3)]
PLAN_AFTER_NORM = ['t0', 't1', 'v0', 'v1']
PLAN_LAST = [(5, 0), (4, 1), (5, 1), 'v2', 't2', (3, 4), (5, 2), (1, 5), (2, 5), (5, 3), 'v3', 't3', (4, 2), (2, 6), (4, 3), (3, 5), (0, 6), (5, 4), 'v4', (4, 4), (1, 6), (5, 5), 'v5', (3, 6), (4, 5), (5, 6), (4, 6)]
TOKEN_PIECES = 4


def back_kernel(
    fast, ctx, length_ref, q_ref, k_ref, v_ref, mixed_ref, grad_ref, log_ref, inputs_in, normed_in,
    middle_in, weight_in, gain, norm_two, *rest,
):
    rest = list(rest)
    take = lambda count: [rest.pop(0) for _ in range(count)]
    sources = take(4) if fast else []
    (grad_tokens,) = take(1)
    results = take(4) if fast else take(1)
    (vector_out,) = take(1)
    (inputs, normed, middle, weight, grad_normed, pair, partial, staged) = take(8)
    (k_t, grad_q_t, probs_low, grads_low, sum_k, sum_v) = take(6)
    (vectors, vectors_got, local, token_send, token_recv, v_send, v_recv) = take(7)
    step = pl.program_id(0)
    seq, me = lax.axis_index("seq"), lax.axis_index("ctx")
    rows, width = normed.shape
    blocks, block = staged.shape[0], staged.shape[1]
    groups = width // LANES
    chunks = []
    if fast:
        send, recv = take(2)
        places = (seq, me, seq % 2, (seq // 2) % 2, seq // 4, me % 2)
        for number in range(3 + PARTS):
            own, stages = None, [None] * 7
            if number == 0:
                stages[1:] = sources[:2] + take(4)
            elif number < 3:
                own, *stages = take(8)
            else:
                stages = take(7)
            source = sources[number + 1] if number < 3 else partial.at[number - 3]
            chunks.append(
                Chunk(
                    source, own, stages, send.at[number], recv.at[number], local.at[5 + number],
                    places, second=number == 0,
                )
            )

    def token_copy(row, piece, slot):
        size = block // TOKEN_PIECES
        rows_there = slice(piece * size, (piece + 1) * size)
        return to_partner(
            staged.at[row, rows_there], grad_tokens.at[slot, rows_there],
            token_send.at[row, piece], token_recv.at[slot, piece], {"ctx": row},
        )

    def run(name):
        if name[0] == "t":
            for offset in range(ctx - 1, 0, -1):
                token_copy(me ^ offset, int(name[1:]), me).start()
            return
        if not fast:
            return
        if isinstance(name, tuple):
            chunks[name[0]].event(name[1])
            return
        number = int(name[1:])
        partners = [{"seq": seq ^ 1}, {"seq": seq ^ 2}, {"seq": seq ^ 4}]
        partners += [{"ctx": me ^ 1}, {"ctx": me ^ 2}]
        exchange = lambda n: to_partner(
            vectors.at[n], vectors_got.at[n], v_send.at[n], v_recv.at[n], partners[n]
        )
        if number:
            exchange(number - 1).wait()
            vectors[number] = vectors[number - 1] + vectors_got[number - 1]
        if number < len(partners):
            exchange(number).start()

    loads = [
        pltpu.make_async_copy(inputs_in, inputs, local.at[0]),
        pltpu.make_async_copy(normed_in, normed, local.at[1]),
        pltpu.make_async_copy(middle_in, middle, local.at[2]),
        pltpu.make_async_copy(weight_in, weight, local.at[3]),
    ]

    @pl.when(step == 0)
    def _():
        partners = [{"ctx": me ^ offset} for offset in range(1, ctx)]
        if fast:
            partners += [{"seq": seq ^ 1}, {"seq": seq ^ 2}, {"seq": seq ^ 4}]
        greet(partners)
        for load in loads:
            load.start()

    def hook(place):
        for group in range(groups):
            if (group, place) in PLAN:

                @pl.when(step == group)
                def _():
                    for name in PLAN[group, place]:
                        run(name)

    hook("start")

    @pl.when(step < groups)
    def _():
        side = pl.ds(pl.multiple_of((step % 2) * LANES, LANES), LANES)
        attend_backward(
            side, length_ref[me], q_ref, k_ref, v_ref, mixed_ref, grad_ref, log_ref, pair,
            k_t, grad_q_t, probs_low, grads_low, sum_k, sum_v,
        )

    hook("end")

    @pl.when(step == 1)
    def _():
        for load in loads:
            load.wait()
        grad_normed[...] = jnp.zeros_like(grad_normed)

    def weight_gradient(part):
        @pl.loop(0, PARTS)
        def _(name):
            columns = pl.ds(pl.multiple_of(name * 2 * LANES, 2 * LANES), 2 * LANES)
            product = dot(normed[...], pair[name], 0, 0).astype(BF16)
            if fast:
                product = product.reshape(2, 2, 2, 2, width // 16, 2 * LANES)
                partial[part, :, :, :, :, :, columns] = product
            else:
                partial[part, :, columns] = product

    @pl.when((step < groups) & (step % 2 == 1))
    def _():
        part = step // 2

        @pl.loop(0, PARTS)
        def _(name):
            there = pl.multiple_of(name * width + part * 2 * LANES, 2 * LANES)
            grad_normed[...] += dot(pair[name], weight[:, pl.ds(there, 2 * LANES)], 1, 1)

        @pl.when(step < groups - 1)
        def _():
            weight_gradient(part)

    own_tokens = pltpu.make_async_copy(staged.at[me], grad_tokens.at[me], local.at[4])

    @pl.when(step == groups)
    def _():
        for name in PLAN_BEFORE_NORM:
            run(name)
        vectors[0] = jnp.concatenate([jnp.zeros((2, width), F32), norm_two[0:6, :]], axis=0)

        @pl.loop(0, blocks)
        def _(row):
            there = pl.ds(pl.multiple_of(row * block, block), block)
            hat, inverse = normalise(inputs[row].astype(F32))
            grad = grad_normed[there, :]
            vectors[0, 0:1, :] += jnp.sum(grad * hat, axis=0, keepdims=True)
            vectors[0, 1:2, :] += jnp.sum(grad, axis=0, keepdims=True)
            total = middle[there, :] + normalise_backward(grad, hat, inverse, row_of(gain))
            staged[row] = total.astype(BF16)

        own_tokens.start()
        for name in PLAN_AFTER_NORM:
            run(name)
        weight_gradient(PARTS - 1)
        for name in PLAN_LAST:
            run(name)
        if fast:
            for number in range(3):
                results[number][...] = chunks[number].out[...]
            for number in range(PARTS):
                results[3][number] = chunks[3 + number].out[...]
            vector_out[...] = vectors[5]
        else:
            results[0][...] = partial[...]
            vector_out[...] = vectors[0]
        own_tokens.wait()
        for row in range(blocks):

            @pl.when(row != me)
            def _():
                for piece in range(TOKEN_PIECES):
                    token_copy(row, piece, me).wait_send()
                    token_copy(row, piece, row).wait_recv()


def attend_backward(
    side, length, q_ref, k_ref, v_ref, mixed_ref, grad_ref, log_ref, pair,
    k_t, grad_q_t, probs_low, grads_low, sum_k, sum_v,
):
    count = q_ref.shape[0] // BLOCK
    k_t[...] = k_ref[...].T

    def rows_of(i):
        rows = slice(i * BLOCK, (i + 1) * BLOCK)
        product = (grad_ref[rows, :].astype(F32) * mixed_ref[rows, :].astype(F32)).T
        queries = [only_head(q_ref[rows, :], head) for head in range(HEADS)]
        grads = [only_head(grad_ref[rows, :], head) for head in range(HEADS)]
        inner = [
            jnp.sum(product[head * HD : (head + 1) * HD], axis=0, keepdims=True)
            for head in range(HEADS)
        ]
        return (queries, grads, inner)

    prepared = [rows_of(i) for i in range(count)]

    def products_of(i, head):
        span = (i + 1) * BLOCK
        scores = dot(k_ref[0:span, :], prepared[i][0][head], 1, 1)
        return (scores, dot(v_ref[0:span, :], prepared[i][1][head], 1, 1))

    steps = [(i, head) for i in range(count) for head in range(HEADS)]
    current = products_of(*steps[0])
    for number, (i, head) in enumerate(steps):
        below = i * BLOCK
        span = below + BLOCK
        following = products_of(*steps[number + 1]) if number + 1 < len(steps) else None
        scores, grad_probs = current
        scores = mask_diagonal(scores, BLOCK, below, length)
        probs = jnp.exp2(scores * SCALE_LOG2 - log_ref[0, head : head + 1, below:span])
        grad_scores = (probs * (grad_probs - prepared[i][2][head])).astype(BF16)
        columns = slice(head * BLOCK, (head + 1) * BLOCK)
        probs_low[0:span, columns] = probs.astype(BF16)
        grads_low[0:span, columns] = grad_scores
        grad_q_t[head * HD : (head + 1) * HD, :] = dot(
            k_t[head * HD : (head + 1) * HD, 0:span], grad_scores, 1, 0
        )
        if head == HEADS - 1:
            pair[0, below:span, side] = (grad_q_t[...].T * SCALE).astype(BF16)
            grad_v = dot(probs_low[0:span, :], jnp.concatenate(prepared[i][1], 0), 1, 0)
            grad_k = dot(grads_low[0:span, :], jnp.concatenate(prepared[i][0], 0), 1, 0)
            if below:
                sum_v[0:below, :] += grad_v[:below]
                sum_k[0:below, :] += grad_k[:below]
            sum_v[below:span, :] = grad_v[below:]
            sum_k[below:span, :] = grad_k[below:]
        current = following
    pair[1, :, side] = (sum_k[...] * SCALE).astype(BF16)
    pair[2, :, side] = sum_v[...].astype(BF16)


def back(
    fast, ctx, length, packed, mixed, grad_mixed, logs, inputs, normed, middle, weight, gain,
    norm_two, partials,
):
    rows, width = mixed.shape
    blocks, block, _ = inputs.shape
    groups = width // LANES
    group_of = lambda step: jnp.minimum(step, groups - 1)
    columns = lambda part: pl.BlockSpec(
        (rows, LANES), lambda step: (0, part * groups + group_of(step))
    )
    if fast:
        lead = (2, 2, 2, 2)
        carried, partials = partials[:2], partials[2:]
        partials = [
            grad.reshape(lead + (grad.shape[0] // 16, grad.shape[1])) for grad in partials
        ]
        sizes = [(carried[0].shape[2], width)] + [grad.shape[-2:] for grad in partials]
        sizes += [(width // 16, width)] * PARTS
        partials = carried + partials
        reduced = [(2,) + size for size in sizes[:3]] + [(PARTS, 2, width // 16, width)]
        held = [PARTS] + list(lead) + [width // 16, width]
        extra = [
            pltpu.SemaphoreType.DMA((len(sizes), KINDS)),
            pltpu.SemaphoreType.DMA((len(sizes), KINDS)),
        ]
        for number, size in enumerate(sizes):
            extra += chunk_scratch(*size, number)
    else:
        partials = []
        reduced = [(PARTS, width, width)]
        held = [PARTS, width, width]
        extra = []
    scratch = [
        pltpu.VMEM(inputs.shape, BF16),
        pltpu.VMEM((rows, width), BF16),
        pltpu.VMEM((rows, width), F32),
        pltpu.VMEM(weight.shape, BF16),
        pltpu.VMEM((rows, width), F32),
        pltpu.VMEM((PARTS, rows, 2 * LANES), BF16),
        pltpu.VMEM(tuple(held), BF16),
        pltpu.VMEM(inputs.shape, BF16),
        pltpu.VMEM((LANES, rows), BF16),
        pltpu.VMEM((LANES, BLOCK), F32),
        pltpu.VMEM((rows, HEADS * BLOCK), BF16),
        pltpu.VMEM((rows, HEADS * BLOCK), BF16),
        pltpu.VMEM((rows, LANES), F32),
        pltpu.VMEM((rows, LANES), F32),
        pltpu.VMEM((6, 8, width), F32),
        pltpu.VMEM((5, 8, width), F32),
        pltpu.SemaphoreType.DMA((5 + 3 + PARTS,)),
        pltpu.SemaphoreType.DMA((blocks, TOKEN_PIECES)),
        pltpu.SemaphoreType.DMA((blocks, TOKEN_PIECES)),
        pltpu.SemaphoreType.DMA((5,)),
        pltpu.SemaphoreType.DMA((5,)),
    ]
    return pl.pallas_call(
        functools.partial(back_kernel, fast, ctx),
        grid=(groups + 1,),
        in_specs=[
            SMEM, columns(0), columns(1), columns(2), columns(0), columns(0),
            pl.BlockSpec((1, HEADS, rows), lambda step: (group_of(step), 0, 0)),
            ANY, ANY, ANY, ANY, VECTOR, whole(norm_two.shape),
        ] + [whole(partial.shape) if number < 2 else ANY for number, partial in enumerate(partials)],
        out_specs=[ANY] + [whole(shape) for shape in reduced] + [whole((8, width))],
        out_shape=[struct(inputs.shape)]
        + [struct(shape) for shape in reduced]
        + [struct((8, width), F32)],
        scratch_shapes=scratch + extra,
        compiler_params=pltpu.CompilerParams(
            vmem_limit_bytes=VMEM_LIMIT, collective_id=2, has_side_effects=True
        ),
        name="back",
    )(
        length, packed, packed, packed, mixed, grad_mixed, logs, inputs, normed, middle, weight,
        gain, norm_two, *partials,
    )


def exchange(value, axis, size, bit):
    return lax.ppermute(value, axis, [(i, i ^ (1 << bit)) for i in range(size)])


def halve(value, axis, size, bit, dim):
    mine = (lax.axis_index(axis) >> bit) & 1
    kept = lax.dynamic_index_in_dim(value, mine, dim, keepdims=False)
    sent = lax.dynamic_index_in_dim(value, 1 - mine, dim, keepdims=False)
    got = exchange(sent, axis, size, bit)
    return (kept.astype(F32) + got.astype(F32)).astype(BF16)


def scatter_over_seq(value, size, order):
    bits = list(range(size.bit_length() - 1))
    value = value.reshape((2,) * len(bits) + value.shape[1:])
    left = bits[::-1]
    for bit in order:
        value = halve(value, "seq", size, bit, left.index(bit))
        left.remove(bit)
    return value


def sum_over_ctx(value, size):
    bits = list(range(size.bit_length() - 1))
    rows, columns = value.shape
    value = value.reshape((2,) * len(bits) + (rows // size, columns))
    left = bits[::-1]
    for bit in bits:
        value = halve(value, "ctx", size, bit, left.index(bit))
        left.remove(bit)
    for bit in bits[::-1]:
        got = exchange(value, "ctx", size, bit)
        low = ((lax.axis_index("ctx") >> bit) & 1) == 0
        value = jnp.stack([jnp.where(low, value, got), jnp.where(low, got, value)])
    value = value.transpose(tuple(bits[::-1]) + (len(bits), len(bits) + 1))
    return value.reshape(rows, columns)


def sum_weight(grad, seq_size, ctx_size):
    rows, columns = grad.shape
    blocks = grad.reshape(seq_size, rows // seq_size, columns)
    order = list(range(seq_size.bit_length() - 1))
    other = order[:1] + order[1:][::-1]
    half = columns // 2
    first = scatter_over_seq(blocks[:, :, :half], seq_size, order)
    second = scatter_over_seq(blocks[:, :, half:], seq_size, other)
    return sum_over_ctx(jnp.concatenate([first, second], axis=-1), ctx_size)


def unpair(parts, rows, width):
    parts = parts.reshape(PARTS, rows, 3, width // PARTS)
    return parts.transpose(1, 2, 0, 3).reshape(rows, 3 * width)


def finish_kernel(output, tokens, qkv, out, up, down, *results):
    targets, held, wide, copies = results[:6], results[6:12], results[12:16], results[16]
    sources = (output, tokens, qkv, out, up, down)
    loads = [
        pltpu.make_async_copy(source, target, copies.at[number])
        for number, (source, target) in enumerate(zip(sources, held))
    ]
    stores = [
        pltpu.make_async_copy(source, target, copies.at[6 + number])
        for number, (source, target) in enumerate(zip(list(held[:2]) + list(wide), targets))
    ]
    for load in loads:
        load.start()
    for number in range(6):
        loads[number].wait()
        source = held[number]
        if number == 2:
            rows, width = source.shape[2:]
            step = width // 3
            for part in range(PARTS):
                for half in range(2):
                    for name in range(3):
                        first = name * width + part * step
                        value = source[part, half, :, name * step : (name + 1) * step]
                        wide[0][half * rows : (half + 1) * rows, first : first + step] = (
                            value.astype(F32)
                        )
        if number > 2:
            rows = source.shape[1]
            for half in range(2):
                there = slice(half * rows, (half + 1) * rows)
                wide[number - 2][there, :] = source[half].astype(F32)
        stores[number].start()
    for store in stores:
        store.wait()


def finish(output, tokens, qkv, out, up, down):
    flat = lambda part: struct((2 * part.shape[1], part.shape[2]), F32)
    wide = [struct((2 * qkv.shape[2], 3 * qkv.shape[3]), F32), flat(out), flat(up), flat(down)]
    return pl.pallas_call(
        finish_kernel,
        in_specs=[ANY] * 6,
        out_specs=[ANY] * 6,
        out_shape=[struct(output.shape), struct(tokens.shape)] + wide,
        scratch_shapes=[pltpu.VMEM(part.shape, BF16) for part in (output, tokens, qkv, out, up, down)]
        + [pltpu.VMEM(part.shape, F32) for part in wide]
        + [pltpu.SemaphoreType.DMA((12,))],
        compiler_params=pltpu.CompilerParams(vmem_limit_bytes=VMEM_LIMIT),
        name="finish",
    )(output, tokens, qkv, out, up, down)


def make_per_device(seq_size, ctx_size):
    fast = seq_size == 8 and ctx_size == 4

    def per_device(
        tokens,
        lengths,
        query_key_value_weight,
        attention_out_weight,
        up_weight,
        down_weight,
        ln1_gain,
        ln1_shift,
        ln2_gain,
        ln2_shift,
        cotangent,
    ):
        width = tokens.shape[-1]
        inputs, normed_low, packed, cot_head, mixed_low, logs = front(
            ctx_size, lengths, tokens, cotangent, query_key_value_weight, ln1_gain, ln1_shift
        )
        (
            output, grad_down, grad_middle, grad_mixed, grad_up, grad_out, grad_norm_two, *carried
        ) = feed_forward(
            fast, lengths, inputs, mixed_low, cot_head, cotangent, attention_out_weight, up_weight,
            down_weight, ln2_gain, ln2_shift,
        )
        partials = carried + [grad_up, grad_out]
        grad_tokens, *sums, vectors = back(
            fast, ctx_size, lengths, packed, mixed_low, grad_mixed, logs, inputs, normed_low,
            grad_middle, query_key_value_weight, ln1_gain, grad_norm_two, partials,
        )
        share = width // seq_size
        if fast:
            down, up, out, qkv = sums
            output, grad_tokens, qkv, out, up, down = finish(
                output, grad_tokens, qkv, out, up, down
            )
        else:
            grad_qkv = unpair(sums[0], width, width)
            grad_down = grad_down.reshape(-1, width)
            down, up, out, qkv = [
                sum_weight(part, seq_size, ctx_size)
                for part in (grad_down, grad_up, grad_out, grad_qkv)
            ]
            vectors = lax.psum(vectors, ("seq", "ctx"))
        vectors = lax.dynamic_slice_in_dim(vectors, lax.axis_index("seq") * share, share, 1)
        return (
            output,
            grad_tokens,
            qkv.astype(F32),
            out.astype(F32),
            up.astype(F32),
            down.astype(F32),
            vectors[0],
            vectors[1],
            vectors[2],
            vectors[3],
        )

    return per_device


def solution(mesh):
    placed = (P("seq", "ctx", None), P("seq")) + (P(),) * 8 + (P("seq", "ctx", None),)
    weights = (P("seq", None),) * 4 + (P("seq"),) * 4
    return jax.shard_map(
        make_per_device(mesh.shape["seq"], mesh.shape["ctx"]),
        mesh=mesh,
        in_specs=placed,
        out_specs=(P("seq", "ctx", None),) * 2 + weights,
        check_vma=False,
    )
```
